32 devices in a mesh: tm: 16 (over z, y, x), space: 2 (over core).
Axes of the slice: x: 2, y: 2, z: 4, core: 2. Of those that a mesh axis runs over, the one named last changes fastest.
Arguments:
- diag_inverse: bfloat16 [32, 2048, 2048], P('tm', 'space'), may hold values from -0.5 to 1.25, as said below
- coupling: bfloat16 [32, 2048, 2048], P('tm', 'space'), may hold values from -0.078125 to 0.078125
- arrow: bfloat16 [32, 256, 2048], P('tm', None, 'space'), may hold values from -0.046875 to 0.046875
- tip_inverse: bfloat16 [256, 256], replicated, may hold values from -0.5 to 1.25, as said below
- noise: bfloat16 [32, 2048, 256], P('tm', 'space'), may hold values from -6 to 6
- noise_fixed: float32 [256, 256], P(None, 'space'), may hold values from -6 to 6
- section_lengths: int32 [16], replicated, may hold values from 1 to 2, 24 in all
Outputs:
- sample: bfloat16 [32, 2048, 256], P('tm', 'space')
- fixed_sample: float32 [256, 256], P(None, 'space')
The draws below stay inside these ranges and needn't reach their ends.
Inputs may be any that keep to these rules, and one draw needn't show every extreme that they name: `diag_inverse`: each of its 32 blocks is lower triangular with a diagonal between 0.5 and 1.25. `tip_inverse`: lower triangular with a diagonal between 0.5 and 1.25. `section_lengths`: the lengths sum to 24.
All inputs are finite; a program needn't handle non-finite values.
Results may differ from the reference program's by a relative error of at most 0.012.
Values may be sent and summed in bfloat16 or wider, within the bound.
No kernel may reach another device: no remote copies, remote signals or barrier semaphores. Data moves between devices by JAX's collectives and lax.ppermute only.
A program may use at most 64 MiB of HBM per device.

```python
import math
import jax
import jax.numpy as jnp
import numpy as np
from jax import lax

NS = 2048
NF = 256
COLS = 256
SLOTS = 2
STEPS = 24
BLOCKS = 32
N_TM = 16
N_SPACE = 2


def lower_block(one_key, width):
    key_diag, key_lower = jax.random.split(one_key)
    diagonal = jax.random.uniform(key_diag, (width,), jnp.float32, 0.5, 1.25)
    lower = jnp.clip(jax.random.normal(key_lower, (width, width), jnp.float32), -4.0, 4.0)
    row_ids = lax.broadcasted_iota(jnp.int32, (width, width), 0)
    col_ids = lax.broadcasted_iota(jnp.int32, (width, width), 1)
    lower = jnp.where(row_ids > col_ids, lower * (0.7 / math.sqrt(width)), 0.0)
    return (lower + jnp.where(row_ids == col_ids, diagonal[None, :], 0.0)).astype(jnp.bfloat16)


def draw_diag_inverse(key, part):
    all_keys = jax.random.split(jax.random.fold_in(key, 11), BLOCKS)

    def one_block(one_key):
        return lower_block(one_key, NS)
    return lax.map(one_block, all_keys)


def draw_tip_inverse(key, part):
    return lower_block(jax.random.fold_in(key, 7), NF)


def block_levels(rng, shape, cuts, smallest, largest):
    def one(axis_at, shards_of):
        draws = jax.random.uniform(jax.random.fold_in(jax.random.fold_in(rng, 6), axis_at), (shards_of,), jnp.float32, smallest / len(cuts), largest / len(cuts))
        return jnp.repeat(jnp.exp(draws), shape[axis_at] // shards_of).reshape((-1,) + (1,) * (len(shape) - axis_at - 1))

    factor_of = one(*cuts[0])
    for cut in cuts[1:]:
        factor_of = factor_of * one(*cut)
    return factor_of


def split_up(count, total, most, lean):
    loads = [(1 << 20) // math.isqrt(grade ** lean) + 1 for grade in range(2, count + 1)]
    rest, given = total - most - (count - 1), [1] * (count - 1)
    while rest > 0:
        movable = [i for i in range(count - 1) if given[i] < most]
        whole, budget = sum([loads[i] for i in movable]), rest
        for i in movable:
            extra = min(most - given[i], max(1, budget * loads[i] // whole), rest)
            given[i] = given[i] + extra
            rest = rest - extra
    return np.array([most] + given)


def uneven_parts(rng, count, total, bound, skew):
    if count == 2:
        one = jax.random.randint(rng, (), max(1, total - bound), min(bound, total - 1) + 1)
        return jnp.stack([one, total - one])
    sizes = jnp.asarray(split_up(count, total, bound, skew), jnp.int32)
    twos = (count - 1) // 2
    donor, taker = sizes[1:1 + 2 * twos:2], sizes[2:2 + 2 * twos:2]
    slack = jnp.minimum(donor - 1, bound - taker)
    moved = jax.random.randint(jax.random.fold_in(rng, 1), (twos,), 0, 1 << 20) % (slack + 1)
    sizes = sizes.at[1:1 + 2 * twos:2].set(donor - moved).at[2:2 + 2 * twos:2].set(taker + moved)
    return sizes[jax.random.permutation(jax.random.fold_in(rng, 2), count)]


def gaussian(key, shape, scale, bound, cuts=(), held_as=jnp.bfloat16):
    entries = scale * jax.random.normal(key, shape, jnp.float32)
    if cuts:
        entries = entries * block_levels(key, shape, cuts, -0.22, 0.18)
    return jnp.clip(entries, -bound, bound).astype(held_as)


def setup_inputs(seed: int = 0) -> dict:
    seeds = jax.random.split(jax.random.key(seed), 8)
    return {
        "diag_inverse": draw_diag_inverse(jax.random.fold_in(seeds[7], 71), 0),
        "coupling": gaussian(seeds[1], (BLOCKS, NS, NS), (3 * NS) ** -0.5, 0.078125, ((0, 16), (1, 2))),
        "arrow": gaussian(seeds[2], (BLOCKS, NF, NS), (8 * NS) ** -0.5, 0.046875, ((0, 16), (2, 2))),
        "tip_inverse": draw_tip_inverse(jax.random.fold_in(seeds[7], 71), 0),
        "noise": gaussian(seeds[4], (BLOCKS, NS, COLS), 1.0, 6.0, ((0, 16), (1, 2))),
        "noise_fixed": gaussian(seeds[5], (NF, COLS), 1.0, 6.0, ((1, 2),), jnp.float32),
        "section_lengths": uneven_parts(seeds[6], N_TM, STEPS, SLOTS, 0).astype(jnp.int32),
    }


def grouped_transpose(matrix, vector):
    group_rows = matrix.shape[0] // N_SPACE
    blocks = matrix.reshape(N_SPACE, group_rows, matrix.shape[1]).astype(jnp.float32)
    pieces = vector.reshape(N_SPACE, group_rows, vector.shape[1]).astype(jnp.float32)
    partial_value = jnp.einsum("grc,grm->gcm", blocks, pieces)
    rounded = lax.optimization_barrier(partial_value.astype(jnp.bfloat16))
    return jnp.sum(rounded.astype(jnp.float32), axis=0)


def reference(diag_inverse, coupling, arrow, tip_inverse, noise, noise_fixed, section_lengths):
    slot_ids = jnp.arange(BLOCKS, dtype=jnp.int32)
    slot_live = (slot_ids % SLOTS) < section_lengths[slot_ids // SLOTS]
    first_slot = (slot_ids % SLOTS) == 0
    last_slot = (slot_ids % SLOTS) == SLOTS - 1
    initial = jnp.zeros((NS, COLS), jnp.bfloat16)

    def forward(earlier, inputs):
        inverse, couple, source, is_live, is_first = inputs
        earlier = jnp.where(is_first, jnp.zeros_like(earlier), earlier)
        pulled = jnp.dot(couple, earlier, preferred_element_type=jnp.float32)
        target = (source.astype(jnp.float32) - pulled).astype(jnp.bfloat16)
        solved = jnp.dot(inverse, target, preferred_element_type=jnp.float32)
        rounded = solved.astype(jnp.bfloat16)
        kept = jnp.where(is_live, rounded, jnp.zeros_like(rounded))
        return jnp.where(is_live, rounded, earlier), (solved, kept)

    _, (forward_value, forward_bar) = lax.scan(forward, initial, (diag_inverse, coupling, noise, slot_live, first_slot))

    def add_arrow(running, inputs):
        arrow_block, values = inputs
        return running + jnp.dot(arrow_block, values, preferred_element_type=jnp.float32), None

    arrow_total, _ = lax.scan(add_arrow, jnp.zeros((NF, COLS), jnp.float32), (arrow, forward_bar))
    mixed_sum = (noise_fixed - arrow_total).astype(jnp.bfloat16)
    tip_forward = jnp.dot(tip_inverse, mixed_sum, preferred_element_type=jnp.float32)
    fixed_sample = lax.dot_general(tip_inverse, tip_forward.astype(jnp.bfloat16), (((0,), (0,)), ((), ())), preferred_element_type=jnp.float32)
    fixed_bar = fixed_sample.astype(jnp.bfloat16)

    def backward(carried, inputs):
        inverse, couple, arrow_block, values, is_live, is_last = inputs
        carried = jnp.where(is_last, jnp.zeros_like(carried), carried)
        spread = lax.dot_general(arrow_block, fixed_bar, (((0,), (0,)), ((), ())), preferred_element_type=jnp.float32)
        target = (values - spread - carried).astype(jnp.bfloat16)
        solved = grouped_transpose(inverse, target)
        rounded = solved.astype(jnp.bfloat16)
        rounded = jnp.where(is_live, rounded, jnp.zeros_like(rounded))
        passed = grouped_transpose(couple, rounded)
        return jnp.where(is_live, passed, carried), rounded

    _, sample = lax.scan(backward, jnp.zeros((NS, COLS), jnp.float32), (diag_inverse, coupling, arrow, forward_value, slot_live, last_slot), reverse=True)
    return sample, fixed_sample
```

```python
import jax
import jax.numpy as jnp
from jax import lax
from jax.sharding import PartitionSpec as P

ROWS = (((0,), (0,)), ((), ()))


def dot(left, right):
    return jnp.dot(left, right, preferred_element_type=jnp.float32)


def dot_rows(left, right):
    return lax.dot_general(left, right, ROWS, preferred_element_type=jnp.float32)


def make_on_device(n_tm, n_space):
    def shift_space(value, step, wrap):
        pairs = [
            (i, (i + step) % n_space)
            for i in range(n_space)
            if wrap or 0 <= i + step < n_space
        ]
        return lax.ppermute(value, "space", pairs)

    def on_device(diag_inverse, coupling, arrow, tip_inverse, noise, noise_fixed, section_lengths):
        slot_count, rows, _ = diag_inverse.shape
        fixed_rows = arrow.shape[1]
        fixed_width = noise_fixed.shape[1]
        position = lax.axis_index("tm")
        core = lax.axis_index("space")
        own_length = lax.dynamic_index_in_dim(section_lengths, position, 0, keepdims=False)
        live = [s < own_length for s in range(slot_count)]

        def gather(piece, lower):
            whole = jnp.zeros((n_space * rows, piece.shape[1]), piece.dtype)
            whole = lax.dynamic_update_slice(whole, piece, (core * rows, 0))
            for step in range(1, n_space):
                other = shift_space(piece, step, not lower)
                source = (core - step) % n_space
                if lower:
                    other = jnp.where(core >= step, other, jnp.zeros_like(other))
                whole = lax.dynamic_update_slice(whole, other, (source * rows, 0))
            return whole

        def scatter_sum(partial, axis, lower):
            def block(index):
                return lax.dynamic_slice_in_dim(partial, index * rows, rows, axis)

            total = lax.reduce_precision(block(core), 8, 7)
            for step in range(1, n_space):
                sent = block((core - step) % n_space).astype(jnp.bfloat16)
                got = shift_space(sent, -step, not lower).astype(jnp.float32)
                total = total + got
            return total

        def solve(slot, right):
            return dot(diag_inverse[slot], gather(right, True))

        response = [None] * slot_count
        pushed = None
        for slot in reversed(range(1, slot_count)):
            right = jnp.where(live[slot], arrow[slot], jnp.zeros_like(arrow[slot]))
            if pushed is not None:
                right = (right.astype(jnp.float32) - pushed).astype(jnp.bfloat16)
            response[slot] = scatter_sum(
                dot(right, diag_inverse[slot]), 1, True
            ).astype(jnp.bfloat16)
            pushed = scatter_sum(dot(response[slot], coupling[slot]), 1, False)

        first = solve(0, noise[0])
        bars = [first.astype(jnp.bfloat16)]
        arrow_part = dot(arrow[0], bars[0])
        values = [first]
        for slot in range(1, slot_count):
            pulled = dot(coupling[slot], gather(bars[slot - 1], False))
            target = (noise[slot].astype(jnp.float32) - pulled).astype(jnp.bfloat16)
            if slot == 1:
                arrow_part = arrow_part + dot(response[1], target)
            else:
                arrow_part = arrow_part + dot(response[slot], noise[slot])
            values.append(solve(slot, target))
            bars.append(values[slot].astype(jnp.bfloat16))

        def own_columns(index):
            return lax.dynamic_slice_in_dim(arrow_part, index * fixed_width, fixed_width, 1)

        total = own_columns(core)
        for step in range(1, n_space):
            sent = own_columns((core - step) % n_space).astype(jnp.bfloat16)
            total = total + shift_space(sent, -step, True).astype(jnp.float32)
        bit = 1
        while bit < n_tm:
            rounded = lax.reduce_precision(total, 8, 7)
            got = lax.ppermute(
                rounded.astype(jnp.bfloat16), "tm", [(i, i ^ bit) for i in range(n_tm)]
            )
            total = rounded + got.astype(jnp.float32)
            bit *= 2
        mixed = (noise_fixed - total).astype(jnp.bfloat16)
        tip_forward = dot(tip_inverse, mixed)
        fixed_out = dot_rows(tip_inverse, tip_forward.astype(jnp.bfloat16))
        fixed_own = fixed_out.astype(jnp.bfloat16)
        fixed_bar = jnp.zeros((fixed_rows, n_space * fixed_width), jnp.bfloat16)
        fixed_bar = lax.dynamic_update_slice(fixed_bar, fixed_own, (0, core * fixed_width))
        for step in range(1, n_space):
            fixed_bar = lax.dynamic_update_slice(
                fixed_bar,
                shift_space(fixed_own, step, True),
                (0, ((core - step) % n_space) * fixed_width),
            )

        base = [None] * slot_count
        carried = None
        for slot in reversed(range(slot_count)):
            target = values[slot]
            if carried is not None:
                target = target - carried
            solved = scatter_sum(
                dot_rows(diag_inverse[slot], target.astype(jnp.bfloat16)), 0, True
            )
            base[slot] = jnp.where(live[slot], solved, 0.0)
            if slot > 0:
                carried = scatter_sum(
                    dot_rows(coupling[slot], base[slot].astype(jnp.bfloat16)), 0, False
                )
        right = arrow[0]
        if pushed is not None:
            right = (right.astype(jnp.float32) - pushed).astype(jnp.bfloat16)
        response[0] = scatter_sum(dot(right, diag_inverse[0]), 1, True).astype(jnp.bfloat16)
        outputs = [
            (base[s] - dot_rows(response[s], fixed_bar)).astype(jnp.bfloat16)
            for s in range(slot_count)
        ]
        return (jnp.stack(outputs), fixed_out)

    return on_device


def solution(mesh):
    shape = dict(mesh.shape)
    return jax.shard_map(
        make_on_device(shape["tm"], shape["space"]),
        mesh=mesh,
        in_specs=(
            P("tm", "space", None),
            P("tm", "space", None),
            P("tm", None, "space"),
            P(),
            P("tm", "space", None),
            P(None, "space"),
            P(),
        ),
        out_specs=(P("tm", "space", None), P(None, "space")),
        check_vma=False,
    )
```

```python
import jax
import jax.numpy as jnp
from jax import lax
from jax.experimental import pallas as pl
from jax.experimental.pallas import tpu as pltpu
from jax.sharding import PartitionSpec as P

BF = jnp.bfloat16
F32 = jnp.float32
MIB = 1 << 20


def dot(left, right):
    return jnp.dot(left, right, preferred_element_type=F32)


def dot_last(left, right):
    return lax.dot_general(left, right, (((1,), (1,)), ((), ())), preferred_element_type=F32)


def rounded(value):
    return value.astype(BF).astype(F32)


def total_of(own_ref, got_refs):
    total = rounded(own_ref[...])
    for got in got_refs:
        total = total + got[...].astype(F32)
    return total


def shape_of(shape, dtype):
    return jax.ShapeDtypeStruct(shape, dtype)


def build(n_tm, n_space, rows, columns, fixed_rows):
    nodes = n_space * rows
    tile = 256 if rows % 256 == 0 else rows
    tiles = rows // tile
    width = columns // n_space
    peers = range(1, n_space)

    def at_core():
        return lax.axis_index("space")

    def block(step, offset=0, size=rows):
        owner = lax.rem(at_core() - step + n_space, n_space)
        return pl.ds(pl.multiple_of(owner * rows + offset, tile), size)

    def call(body, outs, args, flops, moved, places=None, scratch=()):
        places = places or {}
        specs = [pl.BlockSpec(memory_space=places.get(i, pltpu.VMEM)) for i in range(len(args))]
        args = [
            pltpu.with_memory_space_constraint(a, pltpu.HBM)
            if places.get(i) is pltpu.HBM
            else a
            for i, a in enumerate(args)
        ]
        return pl.pallas_call(
            body,
            in_specs=specs,
            out_specs=[pl.BlockSpec(memory_space=pltpu.VMEM)] * len(outs),
            out_shape=outs,
            scratch_shapes=list(scratch),
            cost_estimate=pl.CostEstimate(flops=flops, bytes_accessed=moved, transcendentals=0),
            compiler_params=pltpu.CompilerParams(vmem_limit_bytes=16 * MIB),
        )(*args)

    def lower_rows(left, factor, own_ref, other_ref, wait=None):
        for j in range(tiles):
            at = j * tile
            if wait:
                wait(0, j)
            own_ref[:, at : at + tile] = dot(
                left[:, at:], factor[at:, block(0, at, tile)]
            )
        for step in peers:

            @pl.when(at_core() >= step)
            def _():
                for j in range(tiles):
                    at = j * tile
                    if wait:
                        wait(step, j)
                    other_ref[step - 1, :, at : at + tile] = dot(
                        left, factor[:, block(step, at, tile)]
                    ).astype(BF)

            @pl.when(at_core() < step)
            def _():
                other_ref[step - 1] = jnp.zeros_like(other_ref[step - 1])

    def full_rows(left, factor, own_ref, other_ref, wait=None):
        for step in (*peers, 0):
            for j in range(tiles):
                at = j * tile
                if wait:
                    wait(step, j)
                product = dot(left, factor[:, block(step, at, tile)])
                if step:
                    other_ref[step - 1, :, at : at + tile] = product.astype(BF)
                else:
                    own_ref[:, at : at + tile] = product

    def lower_own(factor, right, out_ref, wait=None):
        for i in range(tiles):
            at = i * tile
            if wait:
                wait(0, i)
            out_ref[at : at + tile] = dot(
                factor[at : at + tile, block(0, 0, at + tile)], right[: at + tile]
            )

    def start_kernel(diag, arrow, noise, lengths, d0, d1, own, other, first, e1, n0, sem1, sem0, sems):
        copies1, copies0 = {}, {}
        arrow_copy = pltpu.make_async_copy(arrow.at[1], e1, sems.at[0])
        noise_copy = pltpu.make_async_copy(noise.at[0], n0, sems.at[1])
        arrow_copy.start()
        for j in range(tiles):
            at = j * tile
            part = (pl.ds(at, rows - at), block(0, at, tile))
            copies1[0, j] = pltpu.make_async_copy(diag.at[(1, *part)], d1.at[part], sem1.at[0, j])
            copies1[0, j].start()
            part = (pl.ds(at, tile), block(0, 0, at + tile))
            copies0[0, j] = pltpu.make_async_copy(diag.at[(0, *part)], d0.at[part], sem0.at[0, j])
        for step in peers:
            for j in range(tiles):
                at = j * tile
                part = (pl.ds(0, rows), block(step, at, tile))
                copies1[step, j] = pltpu.make_async_copy(
                    diag.at[(1, *part)], d1.at[part], sem1.at[step, j]
                )
                part = (pl.ds(at, tile), block(step))
                copies0[step, j] = pltpu.make_async_copy(
                    diag.at[(0, *part)], d0.at[part], sem0.at[step, j]
                )

            @pl.when(at_core() >= step)
            def _():
                for j in range(tiles):
                    copies1[step, j].start()

        noise_copy.start()
        for j in range(tiles):
            copies0[0, j].start()
        for step in peers:

            @pl.when(at_core() >= step)
            def _():
                for j in range(tiles):
                    copies0[step, j].start()

        arrow_copy.wait()
        live = lengths[lax.axis_index("tm")] > 1
        left = jnp.where(live, e1[...], jnp.zeros_like(e1[...]))
        lower_rows(left, d1, own, other, lambda step, j: copies1[step, j].wait())
        noise_copy.wait()
        lower_own(d0, n0, first, lambda step, j: copies0[step, j].wait())
        for step in peers:

            @pl.when(at_core() >= step)
            def _():
                for j in range(tiles):
                    copies0[step, j].wait()

    def lower_rest(factor, first, got, at):
        out = first[at : at + tile]
        for step in peers:
            out = out + dot(factor[at : at + tile, block(step)], got[step - 1][...])
        return out

    def first_value_kernel(factor, first, *refs):
        got, (value, bar) = refs[: n_space - 1], refs[n_space - 1 :]
        value[...] = first[...]
        for step in peers:

            @pl.when(at_core() >= step)
            def _():
                for i in range(tiles):
                    at = i * tile
                    value[at : at + tile] = value[at : at + tile] + dot(
                        factor[at : at + tile, block(step)], got[step - 1][...]
                    )

        bar[...] = value[...].astype(BF)

    def response_kernel(coupling, value, own, *refs):
        got = refs[: n_space - 1]
        k1, response, pushed_own, pushed_other, value_rows, sem = refs[n_space - 1 :]
        copies = {}
        for step in (*peers, 0):
            for j in range(tiles):
                part = (pl.ds(0, rows), block(step, j * tile, tile))
                copies[step, j] = pltpu.make_async_copy(
                    coupling.at[(1, *part)], k1.at[part], sem.at[step, j]
                )
                copies[step, j].start()
        response[...] = total_of(own, got).astype(BF)
        full_rows(
            response[...], k1, pushed_own, pushed_other, lambda step, j: copies[step, j].wait()
        )
        value_rows[...] = value[...].T

    def target_kernel(k1, bar, noise, arrow, response, *refs):
        got, (target, part) = refs[: n_space - 1], refs[n_space - 1 :]
        pieces = [bar, *got]
        for i in range(tiles):
            at = i * tile
            pulled = jnp.zeros((tile, columns), F32)
            for step, piece in enumerate(pieces):
                pulled = pulled + dot(k1[at : at + tile, block(step)], piece[...])
            source = noise[1, at : at + tile].astype(F32)
            target[at : at + tile] = (source - pulled).astype(BF)
        total = dot(arrow[0], bar[...]) + dot(response[...], target[...])
        part[...] = total.T

    def first_response_kernel(d0, d1, arrow, target, pushed_own, *refs):
        got, (own, other, first) = refs[: n_space - 1], refs[n_space - 1 :]
        left = (arrow[0].astype(F32) - total_of(pushed_own, got)).astype(BF)
        lower_rows(left, d0, own, other)
        lower_own(d1, target, first)

    def last_solve_kernel(d1, first, *refs):
        got, (own, other, value) = refs[: n_space - 1], refs[n_space - 1 :]
        value[...] = first[...]
        for step in peers:

            @pl.when(at_core() >= step)
            def _():
                for i in range(tiles):
                    at = i * tile
                    value[at : at + tile] = value[at : at + tile] + dot(
                        d1[at : at + tile, block(step)], got[step - 1][...]
                    )

        lower_rows(value[...].T.astype(BF), d1, own, other)

    def pass_kernel(k1, lengths, solved, *refs):
        got, (base, own, other) = refs[: n_space - 1], refs[n_space - 1 :]
        live = lengths[lax.axis_index("tm")] > 1
        value = jnp.where(live, total_of(solved, got), 0.0)
        base[...] = value
        full_rows(value.astype(BF), k1, own, other)

    def first_solve_kernel(d0, value_rows, passed, *refs):
        got, (own, other) = refs[: n_space - 1], refs[n_space - 1 :]
        left = (value_rows[...] - total_of(passed, got)).astype(BF)
        lower_rows(left, d0, own, other)

    def tip_kernel(noise_fixed, tip, total, got, out, fixed):
        whole = total[...] + got[...].astype(F32)
        mixed = (noise_fixed[...].T - whole).astype(BF)
        forward = dot_last(mixed, tip[...])
        sample = dot(forward.astype(BF), tip[...])
        fixed[...] = sample.astype(BF)
        out[...] = sample.T

    def final_kernel(response, base, solved, pushed, fixed, *refs):
        got_solved, refs = refs[: n_space - 1], refs[n_space - 1 :]
        got_pushed, refs = refs[: n_space - 1], refs[n_space - 1 :]
        got_fixed, (out, whole) = refs[: n_space - 1], refs[n_space - 1 :]
        for step, piece in enumerate([fixed, *got_fixed]):
            owner = lax.rem(at_core() - step + n_space, n_space)
            whole[pl.ds(pl.multiple_of(owner * width, width), width)] = piece[...]
        out[1] = (base[...] - dot(whole[...], response[...])).T.astype(BF)
        left = total_of(pushed, got_pushed).astype(BF)
        out[0] = (total_of(solved, got_solved) - dot(whole[...], left)).T.astype(BF)

    def swap(value, step):
        pairs = [(i, (i - step) % n_space) for i in range(n_space)]
        return lax.ppermute(value, "space", pairs)

    def send_up(value):
        return [swap(value, -step) for step in peers]

    def send_down(values):
        return [swap(values[step - 1], step) for step in peers]

    wide = 2 * rows * nodes * columns
    factor_bytes = 2 * rows * nodes
    node_f32, node_bf = shape_of((rows, columns), F32), shape_of((rows, columns), BF)
    flat_f32 = shape_of((columns, rows), F32)
    flat_others = shape_of((n_space - 1, columns, rows), BF)
    fixed_f32 = shape_of((fixed_rows, rows), F32)
    fixed_bf = shape_of((fixed_rows, rows), BF)
    fixed_others = shape_of((n_space - 1, fixed_rows, rows), BF)
    in_vmem = pltpu.VMEM((rows, nodes), BF)
    dma = pltpu.SemaphoreType.DMA

    def on_device(diag_inverse, coupling, arrow, tip_inverse, noise, noise_fixed, section_lengths):
        core = at_core()
        got_noise = send_up(noise[0])
        d0, d1, own, other, first = call(
            start_kernel,
            [in_vmem, in_vmem, fixed_f32, fixed_others, node_f32],
            [diag_inverse, arrow, noise, section_lengths],
            wide,
            2 * factor_bytes,
            {0: pltpu.HBM, 1: pltpu.HBM, 2: pltpu.HBM, 3: pltpu.SMEM},
            [
                pltpu.VMEM((fixed_rows, rows), BF),
                pltpu.VMEM((rows, columns), BF),
                dma((n_space, tiles)),
                dma((n_space, tiles)),
                dma((2,)),
            ],
        )
        got_response = send_down(other)
        value, bar = call(
            first_value_kernel, [node_f32, node_bf], [d0, first, *got_noise], wide // 2, factor_bytes
        )
        got_bar = send_up(bar)
        k1, response, pushed_own, pushed_other, value_rows = call(
            response_kernel,
            [in_vmem, fixed_bf, fixed_f32, fixed_others, flat_f32],
            [coupling, value, own, *got_response],
            wide,
            factor_bytes,
            {0: pltpu.HBM},
            [dma((n_space, tiles))],
        )
        target, part = call(
            target_kernel,
            [node_bf, shape_of((columns, fixed_rows), F32)],
            [k1, bar, noise, arrow, response, *got_bar],
            wide,
            factor_bytes,
        )
        got_target = send_up(target)
        got_pushed = send_down(pushed_other)

        def own_part(step):
            return lax.dynamic_slice_in_dim(part, ((core - step) % n_space) * width, width, 0)

        total = own_part(0)
        for step in peers:
            total = total + swap(own_part(step).astype(BF), step).astype(F32)
        got = jnp.zeros_like(total, BF)
        bit = 1
        while bit < n_tm:
            total = lax.reduce_precision(total + got.astype(F32), 8, 7)
            got = lax.ppermute(total.astype(BF), "tm", [(i, i ^ bit) for i in range(n_tm)])
            bit *= 2

        first_own, first_other, first = call(
            first_response_kernel,
            [fixed_f32, fixed_others, node_f32],
            [d0, d1, arrow, target, pushed_own, *got_pushed],
            wide,
            factor_bytes,
        )
        got_first = send_down(first_other)
        solved, other, _ = call(
            last_solve_kernel,
            [flat_f32, flat_others, node_f32],
            [d1, first, *got_target],
            wide * 3 // 2,
            factor_bytes,
        )
        got_solved = send_down(other)
        base, passed, other = call(
            pass_kernel,
            [flat_f32, flat_f32, flat_others],
            [k1, section_lengths, solved, *got_solved],
            wide,
            factor_bytes,
            {1: pltpu.SMEM},
        )
        got_passed = send_down(other)
        solved, other = call(
            first_solve_kernel,
            [flat_f32, flat_others],
            [d0, value_rows, passed, *got_passed],
            wide,
            factor_bytes,
        )
        got_solved = send_down(other)
        fixed_out, fixed = call(
            tip_kernel,
            [shape_of((fixed_rows, width), F32), shape_of((width, fixed_rows), BF)],
            [noise_fixed, tip_inverse, total, got],
            4 * fixed_rows * fixed_rows * width,
            8 * fixed_rows * fixed_rows,
        )
        (sample,) = call(
            final_kernel,
            [shape_of((2, rows, columns), BF)],
            [response, base, solved, first_own, fixed, *got_solved, *got_first, *send_up(fixed)],
            4 * rows * fixed_rows * columns,
            factor_bytes,
            scratch=[pltpu.VMEM((columns, fixed_rows), BF)],
        )
        return (sample, fixed_out)

    return on_device


def solution(mesh):
    sizes = dict(mesh.shape)

    def program(diag_inverse, coupling, arrow, tip_inverse, noise, noise_fixed, section_lengths):
        device = build(
            sizes["tm"],
            sizes["space"],
            diag_inverse.shape[1] // sizes["space"],
            noise.shape[2],
            arrow.shape[1],
        )
        return jax.shard_map(
            device,
            mesh=mesh,
            in_specs=(
                P("tm", "space", None),
                P("tm", "space", None),
                P("tm", None, "space"),
                P(),
                P("tm", "space", None),
                P(None, "space"),
                P(),
            ),
            out_specs=(P("tm", "space", None), P(None, "space")),
            check_vma=False,
        )(diag_inverse, coupling, arrow, tip_inverse, noise, noise_fixed, section_lengths)

    return program
```

```python
import jax
import jax.numpy as jnp
from jax import lax
from jax.experimental import pallas as pl
from jax.experimental.pallas import tpu as pltpu
from jax.sharding import PartitionSpec as P

BF = jnp.bfloat16
F32 = jnp.float32
MIB = 1 << 20


def dot(left, right):
    return jnp.dot(left, right, preferred_element_type=F32)


def dot_last(left, right):
    return lax.dot_general(left, right, (((1,), (1,)), ((), ())), preferred_element_type=F32)


def rounded(value):
    return value.astype(BF).astype(F32)


def total_of(own_ref, got_refs):
    total = rounded(own_ref[...])
    for got in got_refs:
        total = total + got[...].astype(F32)
    return total


def shape_of(shape, dtype):
    return jax.ShapeDtypeStruct(shape, dtype)


def build(n_tm, n_space, rows, columns, fixed_rows):
    nodes = n_space * rows
    tile = 256 if rows % 256 == 0 else rows
    tiles = rows // tile
    width = columns // n_space
    peers = range(1, n_space)

    def at_core():
        return lax.axis_index("space")

    def block(step, offset=0, size=rows):
        owner = lax.rem(at_core() - step + n_space, n_space)
        return pl.ds(pl.multiple_of(owner * rows + offset, tile), size)

    def part_rows(step):
        owner = lax.rem(at_core() - step + n_space, n_space)
        return pl.ds(pl.multiple_of(owner * width, width), width)

    def call(body, outs, args, flops, moved, places=None, scratch=()):
        places = places or {}
        specs = [pl.BlockSpec(memory_space=places.get(i, pltpu.VMEM)) for i in range(len(args))]
        args = [
            pltpu.with_memory_space_constraint(a, pltpu.HBM)
            if places.get(i) is pltpu.HBM
            else a
            for i, a in enumerate(args)
        ]
        return pl.pallas_call(
            body,
            in_specs=specs,
            out_specs=[pl.BlockSpec(memory_space=pltpu.VMEM)] * len(outs),
            out_shape=outs,
            scratch_shapes=list(scratch),
            cost_estimate=pl.CostEstimate(flops=flops, bytes_accessed=moved, transcendentals=0),
            compiler_params=pltpu.CompilerParams(vmem_limit_bytes=16 * MIB),
        )(*args)

    def lower_rows(left, factor, own_ref, other_ref):
        for step in peers:

            @pl.when(at_core() >= step)
            def _():
                other_ref[step - 1] = dot(left[...], factor[:, block(step)]).astype(BF)

            @pl.when(at_core() < step)
            def _():
                other_ref[step - 1] = jnp.zeros_like(other_ref[step - 1])

        for j in range(tiles):
            at = j * tile
            own_ref[:, at : at + tile] = dot(left[:, at:], factor[at:, block(0, at, tile)])

    def full_rows(left, factor, own_ref, other_ref):
        for step in peers:
            other_ref[step - 1] = dot(left[...], factor[:, block(step)]).astype(BF)
        own_ref[...] = dot(left[...], factor[:, block(0)])

    def lower_own(factor, right, out_ref, wait=None):
        for i in range(tiles):
            at = i * tile
            if wait:
                wait(i)
            out_ref[at : at + tile] = dot(
                factor[at : at + tile, block(0, 0, at + tile)], right[: at + tile]
            )

    def lower_rest(factor, got, value):
        for step in peers:

            @pl.when(at_core() >= step)
            def _():
                value[...] = value[...] + dot(factor[:, block(step)], got[step - 1][...])

    def start_kernel(
        diag, coupling, arrow, noise, lengths,
        d0, d1, k1, own, other, first, mask,
        e1, n0, live_scratch, sem1, sem0, semk, sems,
    ):
        arrow_copy = pltpu.make_async_copy(arrow.at[1], e1, sems.at[0])
        noise_copy = pltpu.make_async_copy(noise.at[0], n0, sems.at[1])
        live_copy = pltpu.make_async_copy(lengths, live_scratch, sems.at[2])

        def lower_copies(slot, target, sem):
            copies = {}
            for step in range(n_space):
                for i in range(tiles):
                    at = i * tile
                    size = rows if step else at + tile
                    part = (pl.ds(at, tile), block(step, 0, size))
                    copies[step, i] = pltpu.make_async_copy(
                        diag.at[(slot, *part)], target.at[part], sem.at[step, i]
                    )
            return copies

        def each(copies, act):
            for i in range(tiles):
                act(copies[0, i])
            for step in peers:

                @pl.when(at_core() >= step)
                def _():
                    for i in range(tiles):
                        act(copies[step, i])

        copies1 = lower_copies(1, d1, sem1)
        copies0 = lower_copies(0, d0, sem0)
        copiesk = []
        for i in range(tiles):
            part = pl.ds(i * tile, tile)
            copiesk.append(pltpu.make_async_copy(coupling.at[1, part], k1.at[part], semk.at[i]))
        live_copy.start()
        arrow_copy.start()
        each(copies1, lambda copy: copy.start())
        noise_copy.start()
        each(copies0, lambda copy: copy.start())
        for copy in copiesk:
            copy.start()
        live_copy.wait()
        arrow_copy.wait()
        live = live_scratch[lax.axis_index("tm")] > 1
        mask[...] = jnp.where(live, jnp.ones_like(mask[...]), jnp.zeros_like(mask[...]))
        e1[...] = jnp.where(live, e1[...], jnp.zeros_like(e1[...]))
        each(copies1, lambda copy: copy.wait())
        lower_rows(e1, d1, own, other)
        noise_copy.wait()
        lower_own(d0, n0, first, lambda i: copies0[0, i].wait())
        for step in peers:

            @pl.when(at_core() >= step)
            def _():
                for i in range(tiles):
                    copies0[step, i].wait()

        for copy in copiesk:
            copy.wait()

    def first_value_kernel(d0, value, *refs):
        got, (out, bar) = refs[: n_space - 1], refs[n_space - 1 :]
        out[...] = value[...]
        lower_rest(d0, [piece.at[0] for piece in got], out)
        bar[...] = out[...].astype(BF)

    def response_kernel(k1, value, own, *refs):
        got = refs[: n_space - 1]
        response, pushed_own, pushed_other, value_rows = refs[n_space - 1 :]
        response[...] = total_of(own, got).astype(BF)
        full_rows(response, k1, pushed_own, pushed_other)
        value_rows[...] = value[...].T

    def target_kernel(k1, bar, noise, arrow, response, *refs):
        got, (target, part_own, part_other, whole) = refs[: n_space - 1], refs[n_space - 1 :]
        pieces = [bar, *got]
        for i in range(tiles):
            at = i * tile
            pulled = jnp.zeros((tile, columns), F32)
            for step, piece in enumerate(pieces):
                pulled = pulled + dot(k1[at : at + tile, block(step)], piece[...])
            source = noise[1, at : at + tile].astype(F32)
            target[at : at + tile] = (source - pulled).astype(BF)
        whole[...] = (dot(arrow[0], bar[...]) + dot(response[...], target[...])).T
        part_own[...] = whole[part_rows(0)]
        for step in peers:
            part_other[step - 1] = whole[part_rows(step)].astype(BF)

    def first_response_kernel(d0, d1, arrow, target, pushed_own, part, *refs):
        got, refs = refs[: n_space - 1], refs[n_space - 1 :]
        got_parts, (own, other, first, sent) = refs[: n_space - 1], refs[n_space - 1 :]
        total = part[...]
        for piece in got_parts:
            total = total + piece[...].astype(F32)
        sent[...] = total.astype(BF)
        left = (arrow[0].astype(F32) - total_of(pushed_own, got)).astype(BF)
        lower_rows(left, d0, own, other)
        lower_own(d1, target, first)

    def fold_kernel(sent, got, out):
        out[...] = (sent[...].astype(F32) + got[...].astype(F32)).astype(BF)

    def last_solve_kernel(d1, first, *refs):
        got, (own, other, value) = refs[: n_space - 1], refs[n_space - 1 :]
        value[...] = first[...]
        lower_rest(d1, got, value)
        lower_rows(value[...].T.astype(BF), d1, own, other)

    def pass_kernel(k1, mask, solved, *refs):
        got, (base, own, other) = refs[: n_space - 1], refs[n_space - 1 :]
        value = jnp.where(mask[:1, :1] > 0, total_of(solved, got), 0.0)
        base[...] = value
        full_rows(value.astype(BF), k1, own, other)

    def first_solve_kernel(d0, value_rows, passed, *refs):
        got, (own, other) = refs[: n_space - 1], refs[n_space - 1 :]
        left = (value_rows[...] - total_of(passed, got)).astype(BF)
        lower_rows(left, d0, own, other)

    def tip_kernel(noise_fixed, tip, sent, *refs):
        got, (out, fixed) = refs[:-2], refs[-2:]
        whole = sent[...].astype(F32)
        for piece in got:
            whole = whole + piece[...].astype(F32)
        mixed = (noise_fixed[...].T - whole).astype(BF)
        forward = dot_last(mixed, tip[...])
        sample = dot(forward.astype(BF), tip[...])
        fixed[...] = sample.astype(BF)
        out[...] = sample.T

    def final_kernel(response, base, solved, pushed, fixed, *refs):
        got_solved, refs = refs[: n_space - 1], refs[n_space - 1 :]
        got_pushed, refs = refs[: n_space - 1], refs[n_space - 1 :]
        got_fixed, (out, whole) = refs[: n_space - 1], refs[n_space - 1 :]
        for step, piece in enumerate([fixed, *got_fixed]):
            whole[part_rows(step)] = piece[...]
        out[1] = (base[...] - dot(whole[...], response[...])).T.astype(BF)
        left = total_of(pushed, got_pushed).astype(BF)
        out[0] = (total_of(solved, got_solved) - dot(whole[...], left)).T.astype(BF)

    def swap(value, step):
        pairs = [(i, (i - step) % n_space) for i in range(n_space)]
        return lax.ppermute(value, "space", pairs)

    def send_up(value):
        return [swap(value, -step) for step in peers]

    def send_down(values):
        return [swap(values[step - 1], step) for step in peers]

    bits = [1 << i for i in range(n_tm.bit_length() - 1)]
    assert n_tm == 1 << len(bits)

    def swap_bit(value, bit):
        return lax.ppermute(value, "tm", [(i, i ^ bit) for i in range(n_tm)])

    wide = 2 * rows * nodes * columns
    factor_bytes = 2 * rows * nodes
    node_f32, node_bf = shape_of((rows, columns), F32), shape_of((rows, columns), BF)
    flat_f32 = shape_of((columns, rows), F32)
    flat_others = shape_of((n_space - 1, columns, rows), BF)
    fixed_f32 = shape_of((fixed_rows, rows), F32)
    fixed_bf = shape_of((fixed_rows, rows), BF)
    fixed_others = shape_of((n_space - 1, fixed_rows, rows), BF)
    part_bf = shape_of((width, fixed_rows), BF)
    in_vmem = pltpu.VMEM((rows, nodes), BF)
    dma = pltpu.SemaphoreType.DMA

    def fold(sent, got):
        return call(fold_kernel, [part_bf], [sent, got], width * fixed_rows, 6 * width * fixed_rows)[0]

    class Sum:
        def __init__(self, sent):
            self.left = list(bits)
            self.send(sent)

        def send(self, sent):
            self.sent, self.got = sent, None
            if self.left:
                self.got = swap_bit(sent, self.left.pop(0))

        def fold(self):
            if self.left:
                self.send(fold(self.sent, self.got))

        def fold_into(self, body, outs, args, *rest):
            if not self.left:
                return call(body, outs, args, *rest)
            count = len(args)

            def both(*refs):
                ins, (sent, got) = refs[:count], refs[count : count + 2]
                outs_refs, folded = refs[count + 2 : -1], refs[-1]
                fold_kernel(sent, got, folded)
                body(*ins, *outs_refs)

            *results, sent = call(both, [*outs, part_bf], [*args, self.sent, self.got], *rest)
            self.send(sent)
            return results

    def on_device(diag_inverse, coupling, arrow, tip_inverse, noise, noise_fixed, section_lengths):
        got_noise = send_up(noise)
        d0, d1, k1, own, other, value, mask = call(
            start_kernel,
            [in_vmem, in_vmem, in_vmem, fixed_f32, fixed_others, node_f32, shape_of((8, 128), F32)],
            [diag_inverse, coupling, arrow, noise, section_lengths],
            wide,
            3 * factor_bytes,
            {i: pltpu.HBM for i in range(5)},
            [
                pltpu.VMEM((fixed_rows, rows), BF),
                pltpu.VMEM((rows, columns), BF),
                pltpu.SMEM(section_lengths.shape, jnp.int32),
                dma((n_space, tiles)),
                dma((n_space, tiles)),
                dma((tiles,)),
                dma((3,)),
            ],
        )
        got_response = send_down(other)
        value, bar = call(
            first_value_kernel, [node_f32, node_bf], [d0, value, *got_noise], wide // 2, factor_bytes
        )
        got_bar = send_up(bar)
        response, pushed_own, pushed_other, value_rows = call(
            response_kernel,
            [fixed_bf, fixed_f32, fixed_others, flat_f32],
            [k1, value, own, *got_response],
            wide,
            factor_bytes,
        )
        got_pushed = send_down(pushed_other)
        target, part_own, part_other = call(
            target_kernel,
            [node_bf, shape_of((width, fixed_rows), F32), shape_of((n_space - 1, width, fixed_rows), BF)],
            [k1, bar, noise, arrow, response, *got_bar],
            wide,
            factor_bytes,
            scratch=[pltpu.VMEM((columns, fixed_rows), F32)],
        )
        got_target = send_up(target)
        got_parts = send_down(part_other)
        first_own, first_other, value, sent = call(
            first_response_kernel,
            [fixed_f32, fixed_others, node_f32, part_bf],
            [d0, d1, arrow, target, pushed_own, part_own, *got_pushed, *got_parts],
            wide,
            factor_bytes,
        )
        summed = Sum(sent)
        got_first = send_down(first_other)
        solved, other, _ = summed.fold_into(
            last_solve_kernel,
            [flat_f32, flat_others, node_f32],
            [d1, value, *got_target],
            wide * 3 // 2,
            factor_bytes,
        )
        got_solved = send_down(other)
        summed.fold()
        base, passed, other = summed.fold_into(
            pass_kernel,
            [flat_f32, flat_f32, flat_others],
            [k1, mask, solved, *got_solved],
            wide,
            factor_bytes,
        )
        got_passed = send_down(other)
        while summed.left:
            summed.fold()
        last = [summed.sent, summed.got] if bits else [summed.sent]
        fixed_out, fixed = call(
            tip_kernel,
            [shape_of((fixed_rows, width), F32), part_bf],
            [noise_fixed, tip_inverse, *last],
            4 * fixed_rows * fixed_rows * width,
            8 * fixed_rows * fixed_rows,
        )
        solved, other = call(
            first_solve_kernel,
            [flat_f32, flat_others],
            [d0, value_rows, passed, *got_passed],
            wide,
            factor_bytes,
        )
        got_solved = send_down(other)
        (sample,) = call(
            final_kernel,
            [shape_of((2, rows, columns), BF)],
            [response, base, solved, first_own, fixed, *got_solved, *got_first, *send_up(fixed)],
            4 * rows * fixed_rows * columns,
            factor_bytes,
            scratch=[pltpu.VMEM((columns, fixed_rows), BF)],
        )
        return (sample, fixed_out)

    return on_device


def solution(mesh):
    sizes = dict(mesh.shape)

    def program(diag_inverse, coupling, arrow, tip_inverse, noise, noise_fixed, section_lengths):
        device = build(
            sizes["tm"],
            sizes["space"],
            diag_inverse.shape[1] // sizes["space"],
            noise.shape[2],
            arrow.shape[1],
        )
        return jax.shard_map(
            device,
            mesh=mesh,
            in_specs=(
                P("tm", "space", None),
                P("tm", "space", None),
                P("tm", None, "space"),
                P(),
                P("tm", "space", None),
                P(None, "space"),
                P(),
            ),
            out_specs=(P("tm", "space", None), P(None, "space")),
            check_vma=False,
        )(diag_inverse, coupling, arrow, tip_inverse, noise, noise_fixed, section_lengths)

    return program
```

```python
import jax
import jax.numpy as jnp
from jax import lax
from jax.experimental import pallas as pl
from jax.experimental.pallas import tpu as pltpu
from jax.sharding import PartitionSpec as P

BF = jnp.bfloat16
F32 = jnp.float32
MIB = 1 << 20


def dot(left, right):
    return jnp.dot(left, right, preferred_element_type=F32)


def dot_last(left, right):
    return lax.dot_general(left, right, (((1,), (1,)), ((), ())), preferred_element_type=F32)


def rounded(value):
    return value.astype(BF).astype(F32)


def total_of(own_ref, got_refs):
    total = rounded(own_ref[...])
    for got in got_refs:
        total = total + got[...].astype(F32)
    return total


def shape_of(shape, dtype):
    return jax.ShapeDtypeStruct(shape, dtype)


def build(n_tm, n_space, rows, columns, fixed_rows):
    nodes = n_space * rows
    tile = 256 if rows % 256 == 0 else rows
    tiles = rows // tile
    half = rows // 2
    width = columns // n_space
    peers = range(1, n_space)

    def at_core():
        return lax.axis_index("space")

    def block(step, offset=0, size=rows):
        owner = lax.rem(at_core() - step + n_space, n_space)
        return pl.ds(pl.multiple_of(owner * rows + offset, tile), size)

    def part_rows(step):
        owner = lax.rem(at_core() - step + n_space, n_space)
        return pl.ds(pl.multiple_of(owner * width, width), width)

    def call(body, outs, args, flops, moved, places=None, scratch=(), after=None):
        places = dict(places or {})
        args = list(args)
        count = len(args)
        if after is not None:
            args.append(after)
            places[count] = pl.ANY

        def run(*refs):
            body(*refs[:count], *refs[len(args) :])

        specs = [pl.BlockSpec(memory_space=places.get(i, pltpu.VMEM)) for i in range(len(args))]
        args = [
            pltpu.with_memory_space_constraint(a, pltpu.HBM)
            if places.get(i) is pltpu.HBM
            else a
            for i, a in enumerate(args)
        ]
        return pl.pallas_call(
            run,
            in_specs=specs,
            out_specs=[
                pl.BlockSpec(memory_space=places.get(("out", i), pltpu.VMEM))
                for i in range(len(outs))
            ],
            out_shape=outs,
            scratch_shapes=list(scratch),
            cost_estimate=pl.CostEstimate(flops=flops, bytes_accessed=moved, transcendentals=0),
            compiler_params=pltpu.CompilerParams(vmem_limit_bytes=16 * MIB),
        )(*args)

    def lower_rows(left, factor, own_ref, other_ref):
        for step in peers:

            @pl.when(at_core() >= step)
            def _():
                other_ref[step - 1] = dot(left[...], factor[:, block(step)]).astype(BF)

            @pl.when(at_core() < step)
            def _():
                other_ref[step - 1] = jnp.zeros_like(other_ref[step - 1])

        for j in range(tiles):
            at = j * tile
            own_ref[:, at : at + tile] = dot(left[:, at:], factor[at:, block(0, at, tile)])

    def full_rows(left, low, high, own_ref, other_ref):
        for step in (*peers, 0):
            product = dot(left[:, :half], low[:, block(step)])
            product = product + dot(left[:, half:], high[:, block(step)])
            if step:
                other_ref[step - 1] = product.astype(BF)
            else:
                own_ref[...] = product

    def lower_own(factor, right, out_ref, wait=None):
        for i in range(tiles):
            at = i * tile
            if wait:
                wait(i)
            out_ref[at : at + tile] = dot(
                factor[at : at + tile, block(0, 0, at + tile)], right[: at + tile]
            )

    def lower_rest(factor, got, value):
        for step in peers:

            @pl.when(at_core() >= step)
            def _():
                value[...] = value[...] + dot(factor[:, block(step)], got[step - 1][...])

    def start_kernel(
        diag, arrow, noise, lengths,
        d0, d1, own, other, first, mask,
        e1, n0, live_scratch, sem1, sem0, sems,
    ):
        arrow_copy = pltpu.make_async_copy(arrow.at[1], e1, sems.at[0])
        noise_copy = pltpu.make_async_copy(noise.at[0], n0, sems.at[1])
        live_copy = pltpu.make_async_copy(lengths, live_scratch, sems.at[2])

        def lower_copies(slot, target, sem):
            copies = {}
            for step in range(n_space):
                for i in range(tiles):
                    at = i * tile
                    size = rows if step else at + tile
                    part = (pl.ds(at, tile), block(step, 0, size))
                    copies[step, i] = pltpu.make_async_copy(
                        diag.at[(slot, *part)], target.at[part], sem.at[step, i]
                    )
            return copies

        def each(copies, act):
            for i in range(tiles):
                act(copies[0, i])
            for step in peers:

                @pl.when(at_core() >= step)
                def _():
                    for i in range(tiles):
                        act(copies[step, i])

        copies1 = lower_copies(1, d1, sem1)
        copies0 = lower_copies(0, d0, sem0)
        live_copy.start()
        arrow_copy.start()
        each(copies1, lambda copy: copy.start())
        noise_copy.start()
        each(copies0, lambda copy: copy.start())
        live_copy.wait()
        arrow_copy.wait()
        live = live_scratch[lax.axis_index("tm")] > 1
        mask[...] = jnp.where(live, jnp.ones_like(mask[...]), jnp.zeros_like(mask[...]))
        e1[...] = jnp.where(live, e1[...], jnp.zeros_like(e1[...]))
        each(copies1, lambda copy: copy.wait())
        lower_rows(e1, d1, own, other)
        noise_copy.wait()
        lower_own(d0, n0, first, lambda i: copies0[0, i].wait())
        for step in peers:

            @pl.when(at_core() >= step)
            def _():
                for i in range(tiles):
                    copies0[step, i].wait()

    def first_value_kernel(d0, value, *refs):
        got, (out, bar) = refs[: n_space - 1], refs[n_space - 1 :]
        out[...] = value[...]
        lower_rest(d0, [piece.at[0] for piece in got], out)
        bar[...] = out[...].astype(BF)

    def load_kernel(coupling, value, low, value_rows, sems):
        copies = []
        for i in range(2):
            size = half // 2
            copies.append(
                pltpu.make_async_copy(
                    coupling.at[1, pl.ds(i * size, size)], low.at[pl.ds(i * size, size)], sems.at[i]
                )
            )
            copies[i].start()
        value_rows[...] = value[...].T
        for copy in copies:
            copy.wait()

    def target_kernel(low, coupling, bar, noise, arrow, own, *refs):
        got, refs = refs[: n_space - 1], refs[n_space - 1 :]
        got_own, refs = refs[: n_space - 1], refs[n_space - 1 :]
        high, target, part_own, part_other, response, whole, sems = refs
        size = half // 2
        copies = []
        for i in range(2):
            copies.append(
                pltpu.make_async_copy(
                    coupling.at[1, pl.ds(half + i * size, size)],
                    high.at[pl.ds(i * size, size)],
                    sems.at[i],
                )
            )
            copies[i].start()
        response[...] = total_of(own, got_own).astype(BF)
        whole[...] = dot(arrow[0], bar[...])
        pieces = [bar, *got]
        for i in range(4):
            if i >= 2:
                copies[i - 2].wait()
            factor = low if i < 2 else high
            inner = (i % 2) * size
            pulled = dot(factor[inner : inner + size, block(0)], bar[...])
            for step in peers:
                pulled = pulled + dot(
                    factor[inner : inner + size, block(step)], pieces[step][...]
                )
            at = i * size
            source = noise[1, at : at + size].astype(F32)
            target[at : at + size] = (source - pulled).astype(BF)
        whole[...] = (whole[...] + dot(response[...], target[...])).T
        part_own[...] = whole[part_rows(0)]
        for step in peers:
            part_other[step - 1] = whole[part_rows(step)].astype(BF)

    def core_sum_kernel(part, *refs):
        got, out = refs[:-1], refs[-1]
        total = part[...]
        for piece in got:
            total = total + piece[...].astype(F32)
        out[...] = total.astype(BF)

    def fold_kernel(sent, got, out):
        out[...] = (sent[...].astype(F32) + got[...].astype(F32)).astype(BF)

    def last_solve_kernel(d1, target, *refs):
        got, (own, other, value) = refs[: n_space - 1], refs[n_space - 1 :]
        lower_own(d1, target, value)
        lower_rest(d1, got, value)
        lower_rows(value[...].T.astype(BF), d1, own, other)

    def response_kernel(low, high, response, own, other):
        full_rows(response, low, high, own, other)

    def pass_kernel(low, high, mask, solved, *refs):
        got, (base, own, other) = refs[: n_space - 1], refs[n_space - 1 :]
        value = jnp.where(mask[:1, :1] > 0, total_of(solved, got), 0.0)
        base[...] = value
        full_rows(value.astype(BF), low, high, own, other)

    def first_response_kernel(d0, arrow, pushed, *refs):
        got, (own, other) = refs[: n_space - 1], refs[n_space - 1 :]
        left = (arrow[0].astype(F32) - total_of(pushed, got)).astype(BF)
        lower_rows(left, d0, own, other)

    def first_solve_kernel(d0, value_rows, passed, *refs):
        got, (own, other) = refs[: n_space - 1], refs[n_space - 1 :]
        left = (value_rows[...] - total_of(passed, got)).astype(BF)
        lower_rows(left, d0, own, other)

    def turn_kernel(base, response, first, noise_fixed, *refs):
        got, (last_base, last_resp, first_resp, noise_rows) = refs[: n_space - 1], refs[n_space - 1 :]
        noise_rows[...] = noise_fixed[...].T
        last_base[...] = base[...].T
        last_resp[...] = response[...].astype(F32).T.astype(BF)
        first_resp[...] = total_of(first, got).T.astype(BF)

    def turn_first_kernel(solved, *refs):
        got, out = refs[:-1], refs[-1]
        out[...] = total_of(solved, got).T

    def mixed_kernel(noise_rows, *refs):
        terms, out = refs[:-1], refs[-1]
        total = terms[0][...].astype(F32)
        for piece in terms[1:]:
            total = total + piece[...].astype(F32)
        out[...] = (noise_rows[...] - total).astype(BF)

    def final_kernel(tip, bases, responses, mixed, *refs):
        got, (out, fixed_out, whole, fixed, result, sems) = refs[: n_space - 1], refs[n_space - 1 :]
        for step, piece in enumerate([mixed, *got]):
            whole[part_rows(step)] = piece[...]
        forward = dot_last(whole[...], tip[...])
        fixed[...] = dot(forward.astype(BF), tip[...])
        bar = fixed[...].astype(BF)
        copies = []
        for slot in range(2):
            for i in range(tiles):
                at = i * tile
                part = (slot, pl.ds(at, tile))
                update = dot_last(responses[slot][at : at + tile], bar)
                result[part] = (bases[slot][at : at + tile] - update).astype(BF)
                copies.append(
                    pltpu.make_async_copy(result.at[part], out.at[part], sems.at[slot, i])
                )
                copies[-1].start()
        fixed_out[...] = fixed[part_rows(0)].T
        for copy in copies:
            copy.wait()

    def swap(value, step):
        pairs = [(i, (i - step) % n_space) for i in range(n_space)]
        return lax.ppermute(value, "space", pairs)

    def send_up(value):
        return [swap(value, -step) for step in peers]

    def send_down(values):
        return [swap(values[step - 1], step) for step in peers]

    bits = [1 << i for i in range(n_tm.bit_length() - 1)]
    assert n_tm == 1 << len(bits)

    wide = 2 * rows * nodes * columns
    factor_bytes = 2 * rows * nodes
    node_f32, node_bf = shape_of((rows, columns), F32), shape_of((rows, columns), BF)
    flat_f32 = shape_of((columns, rows), F32)
    flat_others = shape_of((n_space - 1, columns, rows), BF)
    fixed_f32 = shape_of((fixed_rows, rows), F32)
    fixed_bf = shape_of((fixed_rows, rows), BF)
    fixed_others = shape_of((n_space - 1, fixed_rows, rows), BF)
    part_bf = shape_of((width, fixed_rows), BF)
    by_node = shape_of((rows, fixed_rows), BF)
    in_vmem, half_vmem = pltpu.VMEM((rows, nodes), BF), pltpu.VMEM((half, nodes), BF)
    dma = pltpu.SemaphoreType.DMA

    def fold(sent, got, after):
        size = width * fixed_rows
        return call(fold_kernel, [part_bf], [sent, got], size, 6 * size, after=after)[0]

    def swap_bit(value, bit):
        return lax.ppermute(value, "tm", [(i, i ^ bit) for i in range(n_tm)])

    def on_device(diag_inverse, coupling, arrow, tip_inverse, noise, noise_fixed, section_lengths):
        got_noise = send_up(noise)
        d0, d1, own, other, value, mask = call(
            start_kernel,
            [in_vmem, in_vmem, fixed_f32, fixed_others, node_f32, shape_of((8, 128), F32)],
            [diag_inverse, arrow, noise, section_lengths],
            wide,
            2 * factor_bytes,
            {i: pltpu.HBM for i in range(4)},
            [
                pltpu.VMEM((fixed_rows, rows), BF),
                pltpu.VMEM((rows, columns), BF),
                pltpu.SMEM(section_lengths.shape, jnp.int32),
                dma((n_space, tiles)),
                dma((n_space, tiles)),
                dma((3,)),
            ],
        )
        got_response = send_down(other)
        value, bar = call(
            first_value_kernel, [node_f32, node_bf], [d0, value, *got_noise], wide // 2, factor_bytes
        )
        got_bar = send_up(bar)
        low, value_rows = call(
            load_kernel,
            [half_vmem, flat_f32],
            [coupling, value],
            wide // 8,
            factor_bytes,
            {0: pltpu.HBM},
            [dma((2,))],
        )
        high, target, part_own, part_other, response = call(
            target_kernel,
            [
                half_vmem,
                node_bf,
                shape_of((width, fixed_rows), F32),
                shape_of((n_space - 1, width, fixed_rows), BF),
                fixed_bf,
            ],
            [low, coupling, bar, noise, arrow, own, *got_bar, *got_response],
            wide,
            factor_bytes,
            {1: pltpu.HBM},
            [pltpu.VMEM((columns, fixed_rows), F32), dma((2,))],
        )
        got_parts = send_down(part_other)
        got_target = send_up(target)
        (sent,) = call(
            core_sum_kernel, [part_bf], [part_own, *got_parts], width * fixed_rows, 8 * width * fixed_rows
        )
        left = list(bits)
        got = [swap_bit(sent, left.pop(0))] if left else []

        def advance(after):
            nonlocal sent, got
            if left:
                sent = fold(sent, *got, after)
                got = [swap_bit(sent, left.pop(0))]

        solved, other = call(
            last_solve_kernel,
            [flat_f32, flat_others],
            [d1, target, *got_target],
            wide * 3 // 2,
            factor_bytes,
            scratch=[pltpu.VMEM((rows, columns), F32)],
            after=sent,
        )
        got_solved = send_down(other)
        advance(solved)
        pushed, other = call(
            response_kernel, [fixed_f32, fixed_others], [low, high, response], wide, factor_bytes, after=sent
        )
        got_pushed = send_down(other)
        base, passed, other = call(
            pass_kernel,
            [flat_f32, flat_f32, flat_others],
            [low, high, mask, solved, *got_solved],
            wide,
            factor_bytes,
            after=pushed,
        )
        got_passed = send_down(other)
        advance(base)
        first, other = call(
            first_response_kernel,
            [fixed_f32, fixed_others],
            [d0, arrow, pushed, *got_pushed],
            wide,
            factor_bytes,
            after=sent,
        )
        got_first = send_down(other)
        solved, other = call(
            first_solve_kernel,
            [flat_f32, flat_others],
            [d0, value_rows, passed, *got_passed],
            wide,
            factor_bytes,
            after=first,
        )
        got_solved = send_down(other)
        advance(solved)
        last_base, last_resp, first_resp, noise_rows = call(
            turn_kernel,
            [node_f32, by_node, by_node, shape_of((width, fixed_rows), F32)],
            [base, response, first, noise_fixed, *got_first],
            wide // 2,
            factor_bytes,
            after=sent,
        )
        (first_base,) = call(
            turn_first_kernel, [node_f32], [solved, *got_solved], wide // 4, factor_bytes // 2, after=noise_rows
        )
        while left:
            advance(None)
        (mixed,) = call(
            mixed_kernel,
            [part_bf],
            [noise_rows, sent, *got],
            width * fixed_rows,
            8 * width * fixed_rows,
            after=first_base,
        )
        sample, fixed_out = call(
            lambda tip, a, b, c, d, *refs: final_kernel(tip, (a, b), (c, d), *refs),
            [shape_of((2, rows, columns), BF), shape_of((fixed_rows, width), F32)],
            [tip_inverse, first_base, last_base, first_resp, last_resp, mixed, *send_up(mixed)],
            4 * rows * fixed_rows * columns,
            factor_bytes,
            {("out", 0): pl.ANY},
            [
                pltpu.VMEM((columns, fixed_rows), BF),
                pltpu.VMEM((columns, fixed_rows), F32),
                pltpu.VMEM((2, rows, columns), BF),
                dma((2, tiles)),
            ],
        )
        return (sample, fixed_out)

    return on_device


def solution(mesh):
    sizes = dict(mesh.shape)

    def program(diag_inverse, coupling, arrow, tip_inverse, noise, noise_fixed, section_lengths):
        device = build(
            sizes["tm"],
            sizes["space"],
            diag_inverse.shape[1] // sizes["space"],
            noise.shape[2],
            arrow.shape[1],
        )
        return jax.shard_map(
            device,
            mesh=mesh,
            in_specs=(
                P("tm", "space", None),
                P("tm", "space", None),
                P("tm", None, "space"),
                P(),
                P("tm", "space", None),
                P(None, "space"),
                P(),
            ),
            out_specs=(P("tm", "space", None), P(None, "space")),
            check_vma=False,
        )(diag_inverse, coupling, arrow, tip_inverse, noise, noise_fixed, section_lengths)

    return program
```

```python
import jax
import jax.numpy as jnp
from jax import lax
from jax.experimental import pallas as pl
from jax.experimental.pallas import tpu as pltpu
from jax.sharding import PartitionSpec as P

BF = jnp.bfloat16
F32 = jnp.float32
MIB = 1 << 20


def dot(left, right):
    return jnp.dot(left, right, preferred_element_type=F32)


def dot_last(left, right):
    return lax.dot_general(left, right, (((1,), (1,)), ((), ())), preferred_element_type=F32)


def rounded(value):
    return value.astype(BF).astype(F32)


def total_of(own_ref, got_refs):
    total = rounded(own_ref[...])
    for got in got_refs:
        total = total + got[...].astype(F32)
    return total


def shape_of(shape, dtype):
    return jax.ShapeDtypeStruct(shape, dtype)


def build(n_tm, n_space, rows, columns, fixed_rows):
    nodes = n_space * rows
    tile = 256 if rows % 256 == 0 else rows
    tiles = rows // tile
    quarter = rows // 4
    width = columns // n_space
    peers = range(1, n_space)

    def at_core():
        return lax.axis_index("space")

    def block(step, offset=0, size=rows):
        owner = lax.rem(at_core() - step + n_space, n_space)
        return pl.ds(pl.multiple_of(owner * rows + offset, tile), size)

    def part_rows(step):
        owner = lax.rem(at_core() - step + n_space, n_space)
        return pl.ds(pl.multiple_of(owner * width, width), width)

    def call(body, outs, args, flops, moved, places=None, scratch=(), after=None, aliases=None):
        places = dict(places or {})
        args = list(args)
        count = len(args)
        if after is not None:
            args.append(after)
            places[count] = pl.ANY

        def run(*refs):
            body(*refs[:count], *refs[len(args) :])

        specs = [pl.BlockSpec(memory_space=places.get(i, pltpu.VMEM)) for i in range(len(args))]
        args = [
            pltpu.with_memory_space_constraint(a, pltpu.HBM)
            if places.get(i) is pltpu.HBM
            else a
            for i, a in enumerate(args)
        ]
        return pl.pallas_call(
            run,
            in_specs=specs,
            out_specs=[
                pl.BlockSpec(memory_space=places.get(("out", i), pltpu.VMEM))
                for i in range(len(outs))
            ],
            out_shape=outs,
            scratch_shapes=list(scratch),
            input_output_aliases=aliases or {},
            cost_estimate=pl.CostEstimate(
                flops=8 * flops, bytes_accessed=8 * moved, transcendentals=0
            ),
            compiler_params=pltpu.CompilerParams(vmem_limit_bytes=16 * MIB),
        )(*args)

    def lower_rows(left, factor, own_ref, other_ref):
        for step in peers:

            @pl.when(at_core() >= step)
            def _():
                other_ref[step - 1] = dot(left[...], factor[:, block(step)]).astype(BF)

            @pl.when(at_core() < step)
            def _():
                other_ref[step - 1] = jnp.zeros_like(other_ref[step - 1])

        for j in range(tiles):
            at = j * tile
            own_ref[:, at : at + tile] = dot(left[:, at:], factor[at:, block(0, at, tile)])

    def full_rows(left, factor, tail, own_ref, other_ref):
        at = rows - quarter
        for step in (*peers, 0):
            product = dot(left[:, :at], factor[:at, block(step)])
            product = product + dot(left[:, at:], tail[:, block(step)])
            if step:
                other_ref[step - 1] = product.astype(BF)
            else:
                own_ref[...] = product

    def lower_own(factor, right, out_ref, wait=None):
        for i in range(tiles):
            at = i * tile
            if wait:
                wait(i)
            out_ref[at : at + tile] = dot(
                factor[at : at + tile, block(0, 0, at + tile)], right[: at + tile]
            )

    def lower_rest(factor, got, value):
        for step in peers:

            @pl.when(at_core() >= step)
            def _():
                value[...] = value[...] + dot(factor[:, block(step)], got[step - 1][...])

    def start_kernel(
        diag, arrow, noise, lengths,
        d0, d1, own, other, first, mask,
        e1, n0, live_scratch, sem1, sem0, sems,
    ):
        arrow_copy = pltpu.make_async_copy(arrow.at[1], e1, sems.at[0])
        noise_copy = pltpu.make_async_copy(noise.at[0], n0, sems.at[1])
        live_copy = pltpu.make_async_copy(lengths, live_scratch, sems.at[2])

        def lower_copies(slot, target, sem):
            copies = {}
            for step in range(n_space):
                for i in range(tiles):
                    at = i * tile
                    size = rows if step else at + tile
                    part = (pl.ds(at, tile), block(step, 0, size))
                    copies[step, i] = pltpu.make_async_copy(
                        diag.at[(slot, *part)], target.at[part], sem.at[step, i]
                    )
            return copies

        def each(copies, i, act):
            act(copies[0, i])
            for step in peers:

                @pl.when(at_core() >= step)
                def _():
                    act(copies[step, i])

        copies1 = lower_copies(1, d1, sem1)
        copies0 = lower_copies(0, d0, sem0)
        live_copy.start()
        arrow_copy.start()
        for i in range(tiles):
            each(copies1, i, lambda copy: copy.start())
        noise_copy.start()
        live_copy.wait()
        arrow_copy.wait()
        live = live_scratch[lax.axis_index("tm")] > 1
        mask[...] = jnp.where(live, jnp.ones_like(mask[...]), jnp.zeros_like(mask[...]))
        e1[...] = jnp.where(live, e1[...], jnp.zeros_like(e1[...]))
        for i in range(tiles):
            each(copies1, i, lambda copy: copy.wait())
            each(copies0, i, lambda copy: copy.start())
        lower_rows(e1, d1, own, other)
        noise_copy.wait()
        lower_own(d0, n0, first, lambda i: copies0[0, i].wait())
        for step in peers:

            @pl.when(at_core() >= step)
            def _():
                for i in range(tiles):
                    copies0[step, i].wait()

    def k1_copies(coupling, k1, quarters, sems):
        copies = {}
        for i, q in enumerate(quarters):
            part = pl.ds(q * quarter, quarter)
            target = k1.at[part] if k1.shape[0] == rows else k1
            copies[q] = pltpu.make_async_copy(coupling.at[1, part], target, sems.at[i])
        return copies

    def first_value_kernel(d0, value, coupling, *refs):
        got, (out, bar, k1, sems) = refs[: n_space - 1], refs[n_space - 1 :]
        copies = k1_copies(coupling, k1, [0], sems)
        copies[0].start()
        out[...] = value[...]
        lower_rest(d0, [piece.at[0] for piece in got], out)
        bar[...] = out[...].astype(BF)
        copies[0].wait()

    def load_kernel(coupling, value, _, value_rows, k1, sems):
        copies = k1_copies(coupling, k1, [1, 2], sems)
        for copy in copies.values():
            copy.start()
        value_rows[...] = value[...].T
        for copy in copies.values():
            copy.wait()

    def target_kernel(k1, coupling, bar, noise, arrow, own, *refs):
        got, refs = refs[: n_space - 1], refs[n_space - 1 :]
        got_own, refs = refs[: n_space - 1], refs[n_space - 1 :]
        tail, target, part_own, part_other, response, e0, n1, whole, sems = refs
        noise_copy = pltpu.make_async_copy(noise.at[1], n1, sems.at[1])
        arrow_copy = pltpu.make_async_copy(arrow.at[0], e0, sems.at[2])
        copies = k1_copies(coupling, tail, [3], sems)
        noise_copy.start()
        copies[3].start()
        arrow_copy.start()
        response[...] = total_of(own, got_own).astype(BF)
        for i in range(4):
            at = i * quarter
            if i in copies:
                copies[i].wait()
            factor = tail if i == 3 else k1.at[at : at + quarter]
            pulled = dot(factor[:, block(0)], bar[...])
            for step in peers:
                pulled = pulled + dot(factor[:, block(step)], got[step - 1][...])
            if i == 0:
                noise_copy.wait()
            source = n1[at : at + quarter].astype(F32)
            target[at : at + quarter] = (source - pulled).astype(BF)
        arrow_copy.wait()
        whole[...] = (dot(e0[...], bar[...]) + dot(response[...], target[...])).T
        part_own[...] = whole[part_rows(0)]
        for step in peers:
            part_other[step - 1] = whole[part_rows(step)].astype(BF)

    def core_sum_kernel(part, *refs):
        got, out = refs[:-1], refs[-1]
        total = part[...]
        for piece in got:
            total = total + piece[...].astype(F32)
        out[...] = total.astype(BF)

    def fold_kernel(sent, got, out):
        out[...] = (sent[...].astype(F32) + got[...].astype(F32)).astype(BF)

    def last_solve_kernel(d1, target, *refs):
        got, (own, other, value) = refs[: n_space - 1], refs[n_space - 1 :]
        lower_own(d1, target, value)
        lower_rest(d1, got, value)
        lower_rows(value[...].T.astype(BF), d1, own, other)

    def response_kernel(k1, tail, response, own, other):
        full_rows(response, k1, tail, own, other)

    def pass_kernel(k1, tail, mask, solved, *refs):
        got, (base, own, other) = refs[: n_space - 1], refs[n_space - 1 :]
        value = jnp.where(mask[:1, :1] > 0, total_of(solved, got), 0.0)
        base[...] = value
        full_rows(value.astype(BF), k1, tail, own, other)

    def first_response_kernel(d0, e0, pushed, *refs):
        got, (own, other) = refs[: n_space - 1], refs[n_space - 1 :]
        left = (e0[...].astype(F32) - total_of(pushed, got)).astype(BF)
        lower_rows(left, d0, own, other)

    def first_solve_kernel(d0, value_rows, passed, *refs):
        got, (own, other) = refs[: n_space - 1], refs[n_space - 1 :]
        left = (value_rows[...] - total_of(passed, got)).astype(BF)
        lower_rows(left, d0, own, other)

    def turn_kernel(base, response, first, noise_fixed, tip, *refs):
        got, (last_base, last_resp, first_resp, noise_rows) = refs[: n_space - 1], refs[n_space - 1 :]
        noise_rows[...] = noise_fixed[...].T
        last_base[...] = base[...].T
        upper = tip[...].astype(F32).T.astype(BF)

        def through_tip(right):
            inner = dot(tip[...], right).astype(BF)
            return dot(upper, inner).T.astype(BF)

        last_resp[...] = through_tip(response[...])
        first_resp[...] = through_tip(total_of(first, got).astype(BF))

    def turn_first_kernel(solved, *refs):
        got, out = refs[:-1], refs[-1]
        out[...] = total_of(solved, got).T

    def mixed_kernel(noise_rows, *refs):
        terms, out = refs[:-1], refs[-1]
        total = terms[0][...].astype(F32)
        for piece in terms[1:]:
            total = total + piece[...].astype(F32)
        out[...] = (noise_rows[...] - total).astype(BF)

    def final_kernel(tip, bases, responses, mixed, *refs):
        got, (out, fixed_out, whole, result, sems) = refs[: n_space - 1], refs[n_space - 1 :]
        for step, piece in enumerate([mixed, *got]):
            whole[part_rows(step)] = piece[...]
        copies = []
        for slot in range(2):
            for i in range(tiles):
                at = i * tile
                part = (slot, pl.ds(at, tile))
                update = dot_last(responses[slot][at : at + tile], whole[...])
                result[part] = (bases[slot][at : at + tile] - update).astype(BF)
                copies.append(
                    pltpu.make_async_copy(result.at[part], out.at[part], sems.at[slot, i])
                )
                copies[-1].start()
        forward = dot_last(mixed[...], tip[...])
        fixed_out[...] = dot(forward.astype(BF), tip[...]).T
        for copy in copies:
            copy.wait()

    def swap(value, step):
        pairs = [(i, (i - step) % n_space) for i in range(n_space)]
        return lax.ppermute(value, "space", pairs)

    def send_up(value):
        return [swap(value, -step) for step in peers]

    def send_down(values):
        return [swap(values[step - 1], step) for step in peers]

    bits = [1 << i for i in range(n_tm.bit_length() - 1)]
    assert n_tm == 1 << len(bits)

    wide = 2 * rows * nodes * columns
    factor_bytes = 2 * rows * nodes
    node_f32, node_bf = shape_of((rows, columns), F32), shape_of((rows, columns), BF)
    flat_f32 = shape_of((columns, rows), F32)
    flat_others = shape_of((n_space - 1, columns, rows), BF)
    fixed_f32 = shape_of((fixed_rows, rows), F32)
    fixed_bf = shape_of((fixed_rows, rows), BF)
    fixed_others = shape_of((n_space - 1, fixed_rows, rows), BF)
    part_bf = shape_of((width, fixed_rows), BF)
    by_node = shape_of((rows, fixed_rows), BF)
    in_vmem = pltpu.VMEM((rows, nodes), BF)
    dma = pltpu.SemaphoreType.DMA

    def fold(sent, got, after):
        size = width * fixed_rows
        return call(fold_kernel, [part_bf], [sent, got], size, 6 * size, after=after)[0]

    def swap_bit(value, bit):
        return lax.ppermute(value, "tm", [(i, i ^ bit) for i in range(n_tm)])

    def on_device(diag_inverse, coupling, arrow, tip_inverse, noise, noise_fixed, section_lengths):
        got_noise = send_up(noise)
        d0, d1, own, other, value, mask = call(
            start_kernel,
            [in_vmem, in_vmem, fixed_f32, fixed_others, node_f32, shape_of((8, 128), F32)],
            [diag_inverse, arrow, noise, section_lengths],
            wide,
            2 * factor_bytes,
            {i: pltpu.HBM for i in range(4)},
            [
                pltpu.VMEM((fixed_rows, rows), BF),
                pltpu.VMEM((rows, columns), BF),
                pltpu.SMEM(section_lengths.shape, jnp.int32),
                dma((n_space, tiles)),
                dma((n_space, tiles)),
                dma((3,)),
            ],
        )
        got_response = send_down(other)
        value, bar, k1 = call(
            first_value_kernel,
            [node_f32, node_bf, in_vmem],
            [d0, value, coupling, *got_noise],
            wide // 2,
            factor_bytes,
            {2: pltpu.HBM},
            [dma((1,))],
        )
        got_bar = send_up(bar)
        value_rows, k1 = call(
            load_kernel,
            [flat_f32, in_vmem],
            [coupling, value, k1],
            wide // 8,
            factor_bytes,
            {0: pltpu.HBM, 2: pl.ANY, ("out", 1): pl.ANY},
            [dma((2,))],
            aliases={2: 1},
        )
        tail, target, part_own, part_other, response, e0 = call(
            target_kernel,
            [
                pltpu.VMEM((quarter, nodes), BF),
                node_bf,
                shape_of((width, fixed_rows), F32),
                shape_of((n_space - 1, width, fixed_rows), BF),
                fixed_bf,
                fixed_bf,
            ],
            [k1, coupling, bar, noise, arrow, own, *got_bar, *got_response],
            wide,
            factor_bytes,
            {1: pltpu.HBM, 3: pltpu.HBM, 4: pltpu.HBM},
            [
                pltpu.VMEM((rows, columns), BF),
                pltpu.VMEM((columns, fixed_rows), F32),
                dma((3,)),
            ],
        )
        got_parts = send_down(part_other)
        got_target = send_up(target)
        (sent,) = call(
            core_sum_kernel, [part_bf], [part_own, *got_parts], width * fixed_rows, 8 * width * fixed_rows
        )
        left = list(bits)
        got = [swap_bit(sent, left.pop(0))] if left else []

        def advance(after):
            nonlocal sent, got
            if left:
                sent = fold(sent, *got, after)
                got = [swap_bit(sent, left.pop(0))]

        solved, other = call(
            last_solve_kernel,
            [flat_f32, flat_others],
            [d1, target, *got_target],
            wide * 3 // 2,
            factor_bytes,
            scratch=[pltpu.VMEM((rows, columns), F32)],
            after=sent,
        )
        got_solved = send_down(other)
        advance(solved)
        pushed, other = call(
            response_kernel, [fixed_f32, fixed_others], [k1, tail, response], wide, factor_bytes, after=sent
        )
        got_pushed = send_down(other)
        base, passed, other = call(
            pass_kernel,
            [flat_f32, flat_f32, flat_others],
            [k1, tail, mask, solved, *got_solved],
            wide,
            factor_bytes,
            after=pushed,
        )
        got_passed = send_down(other)
        advance(base)
        first, other = call(
            first_response_kernel,
            [fixed_f32, fixed_others],
            [d0, e0, pushed, *got_pushed],
            wide,
            factor_bytes,
            after=sent,
        )
        got_first = send_down(other)
        solved, other = call(
            first_solve_kernel,
            [flat_f32, flat_others],
            [d0, value_rows, passed, *got_passed],
            wide,
            factor_bytes,
            after=first,
        )
        got_solved = send_down(other)
        advance(solved)
        last_base, last_resp, first_resp, noise_rows = call(
            turn_kernel,
            [node_f32, by_node, by_node, shape_of((width, fixed_rows), F32)],
            [base, response, first, noise_fixed, tip_inverse, *got_first],
            wide // 2,
            factor_bytes,
            after=sent,
        )
        (first_base,) = call(
            turn_first_kernel, [node_f32], [solved, *got_solved], wide // 4, factor_bytes // 2, after=noise_rows
        )
        while left:
            advance(None)
        (mixed,) = call(
            mixed_kernel,
            [part_bf],
            [noise_rows, sent, *got],
            width * fixed_rows,
            8 * width * fixed_rows,
            after=first_base,
        )
        sample, fixed_out = call(
            lambda tip, a, b, c, d, *refs: final_kernel(tip, (a, b), (c, d), *refs),
            [shape_of((2, rows, columns), BF), shape_of((fixed_rows, width), F32)],
            [tip_inverse, first_base, last_base, first_resp, last_resp, mixed, *send_up(mixed)],
            4 * rows * fixed_rows * columns,
            factor_bytes,
            {("out", 0): pl.ANY},
            [
                pltpu.VMEM((columns, fixed_rows), BF),
                pltpu.VMEM((2, rows, columns), BF),
                dma((2, tiles)),
            ],
        )
        return (sample, fixed_out)

    return on_device


def solution(mesh):
    sizes = dict(mesh.shape)

    def program(diag_inverse, coupling, arrow, tip_inverse, noise, noise_fixed, section_lengths):
        device = build(
            sizes["tm"],
            sizes["space"],
            diag_inverse.shape[1] // sizes["space"],
            noise.shape[2],
            arrow.shape[1],
        )
        return jax.shard_map(
            device,
            mesh=mesh,
            in_specs=(
                P("tm", "space", None),
                P("tm", "space", None),
                P("tm", None, "space"),
                P(),
                P("tm", "space", None),
                P(None, "space"),
                P(),
            ),
            out_specs=(P("tm", "space", None), P(None, "space")),
            check_vma=False,
        )(diag_inverse, coupling, arrow, tip_inverse, noise, noise_fixed, section_lengths)

    return program
```

```python
import jax
import jax.numpy as jnp
from jax import lax
from jax.experimental import pallas as pl
from jax.experimental.pallas import tpu as pltpu
from jax.sharding import PartitionSpec as P

BF = jnp.bfloat16
F32 = jnp.float32
MIB = 1 << 20


def dot(left, right):
    return jnp.dot(left, right, preferred_element_type=F32)


def dot_last(left, right):
    return lax.dot_general(left, right, (((1,), (1,)), ((), ())), preferred_element_type=F32)


def rounded(value):
    return value.astype(BF).astype(F32)


def total_of(own_ref, got_refs):
    total = rounded(own_ref[...])
    for got in got_refs:
        total = total + got[...].astype(F32)
    return total


def shape_of(shape, dtype):
    return jax.ShapeDtypeStruct(shape, dtype)


def build(n_tm, n_space, rows, columns, fixed_rows):
    nodes = n_space * rows
    tile = 256 if rows % 256 == 0 else rows
    tiles = rows // tile
    quarter = rows // 4
    width = columns // n_space
    peers = range(1, n_space)

    def at_core():
        return lax.axis_index("space")

    def block(step, offset=0, size=rows):
        owner = lax.rem(at_core() - step + n_space, n_space)
        return pl.ds(pl.multiple_of(owner * rows + offset, tile), size)

    def part_rows(step):
        owner = lax.rem(at_core() - step + n_space, n_space)
        return pl.ds(pl.multiple_of(owner * width, width), width)

    def call(body, outs, args, flops, moved, places=None, scratch=(), after=None, aliases=None):
        places = dict(places or {})
        args = list(args)
        count = len(args)
        if after is not None:
            args.append(after)
            places[count] = pl.ANY

        def run(*refs):
            body(*refs[:count], *refs[len(args) :])

        specs = [pl.BlockSpec(memory_space=places.get(i, pltpu.VMEM)) for i in range(len(args))]
        args = [
            pltpu.with_memory_space_constraint(a, pltpu.HBM)
            if places.get(i) is pltpu.HBM
            else a
            for i, a in enumerate(args)
        ]
        return pl.pallas_call(
            run,
            in_specs=specs,
            out_specs=[
                pl.BlockSpec(memory_space=places.get(("out", i), pltpu.VMEM))
                for i in range(len(outs))
            ],
            out_shape=outs,
            scratch_shapes=list(scratch),
            input_output_aliases=aliases or {},
            cost_estimate=pl.CostEstimate(
                flops=16 * flops, bytes_accessed=16 * moved, transcendentals=0
            ),
            compiler_params=pltpu.CompilerParams(vmem_limit_bytes=16 * MIB),
        )(*args)

    def lower_rows(left, factor, own_ref, other_ref):
        for step in peers:

            @pl.when(at_core() >= step)
            def _():
                other_ref[step - 1] = dot(left[...], factor[:, block(step)]).astype(BF)

            @pl.when(at_core() < step)
            def _():
                other_ref[step - 1] = jnp.zeros_like(other_ref[step - 1])

        for j in range(tiles):
            at = j * tile
            own_ref[:, at : at + tile] = dot(left[:, at:], factor[at:, block(0, at, tile)])

    def full_rows(left, factor, tail, own_ref, other_ref):
        at = rows - quarter
        for step in (*peers, 0):
            product = dot(left[:, :at], factor[:at, block(step)])
            product = product + dot(left[:, at:], tail[:, block(step)])
            if step:
                other_ref[step - 1] = product.astype(BF)
            else:
                own_ref[...] = product

    def lower_own(factor, right, out_ref, wait=None):
        for i in range(tiles):
            at = i * tile
            if wait:
                wait(i)
            out_ref[at : at + tile] = dot(
                factor[at : at + tile, block(0, 0, at + tile)], right[: at + tile]
            )

    def lower_rest(factor, got, value):
        for step in peers:

            @pl.when(at_core() >= step)
            def _():
                value[...] = value[...] + dot(factor[:, block(step)], got[step - 1][...])

    def start_kernel(
        diag, arrow, noise, lengths,
        d0, d1, own, other, first, mask,
        e1, n0, live_scratch, sem1, sem0, sems,
    ):
        arrow_copy = pltpu.make_async_copy(arrow.at[1], e1, sems.at[0])
        noise_copy = pltpu.make_async_copy(noise.at[0], n0, sems.at[1])
        live_copy = pltpu.make_async_copy(lengths, live_scratch, sems.at[2])

        def lower_copies(slot, target, sem):
            copies = {}
            for step in range(n_space):
                for i in range(tiles):
                    at = i * tile
                    size = rows if step else at + tile
                    part = (pl.ds(at, tile), block(step, 0, size))
                    copies[step, i] = pltpu.make_async_copy(
                        diag.at[(slot, *part)], target.at[part], sem.at[step, i]
                    )
            return copies

        def each(copies, i, act):
            act(copies[0, i])
            for step in peers:

                @pl.when(at_core() >= step)
                def _():
                    act(copies[step, i])

        copies1 = lower_copies(1, d1, sem1)
        copies0 = lower_copies(0, d0, sem0)
        live_copy.start()
        arrow_copy.start()
        for i in range(tiles):
            each(copies1, i, lambda copy: copy.start(priority=i % 2))
        noise_copy.start()
        live_copy.wait()
        arrow_copy.wait()
        live = live_scratch[lax.axis_index("tm")] > 1
        mask[...] = jnp.where(live, jnp.ones_like(mask[...]), jnp.zeros_like(mask[...]))
        e1[...] = jnp.where(live, e1[...], jnp.zeros_like(e1[...]))
        for i in range(tiles):
            each(copies1, i, lambda copy: copy.wait())
            each(copies0, i, lambda copy: copy.start(priority=i % 2))
        lower_rows(e1, d1, own, other)
        noise_copy.wait()
        lower_own(d0, n0, first, lambda i: copies0[0, i].wait())
        for step in peers:

            @pl.when(at_core() >= step)
            def _():
                for i in range(tiles):
                    copies0[step, i].wait()

    def k1_copies(coupling, k1, quarters, sems):
        copies = {}
        for i, q in enumerate(quarters):
            part = pl.ds(q * quarter, quarter)
            target = k1.at[part] if k1.shape[0] == rows else k1
            copies[q] = pltpu.make_async_copy(coupling.at[1, part], target, sems.at[i])
        return copies

    def first_value_kernel(d0, value, coupling, *refs):
        got, (out, bar, k1, sems) = refs[: n_space - 1], refs[n_space - 1 :]
        copies = k1_copies(coupling, k1, [0], sems)
        copies[0].start()
        out[...] = value[...]
        lower_rest(d0, [piece.at[0] for piece in got], out)
        bar[...] = out[...].astype(BF)
        copies[0].wait()

    def load_kernel(coupling, value, _, value_rows, k1, sems):
        copies = k1_copies(coupling, k1, [1, 2], sems)
        for q, copy in copies.items():
            copy.start(priority=q % 2)
        value_rows[...] = value[...].T
        for copy in copies.values():
            copy.wait()

    def target_kernel(k1, coupling, bar, noise, arrow, own, *refs):
        got, refs = refs[: n_space - 1], refs[n_space - 1 :]
        got_own, refs = refs[: n_space - 1], refs[n_space - 1 :]
        tail, target, part_own, part_other, response, e0, n1, whole, sems = refs
        noise_copy = pltpu.make_async_copy(noise.at[1], n1, sems.at[1])
        arrow_copy = pltpu.make_async_copy(arrow.at[0], e0, sems.at[2])
        copies = k1_copies(coupling, tail, [3], sems)
        noise_copy.start()
        copies[3].start(priority=1)
        arrow_copy.start()
        at = rows - quarter

        def pull(factor, part, before):
            pulled = dot(factor[:, block(0)], bar[...])
            for step in peers:
                pulled = pulled + dot(factor[:, block(step)], got[step - 1][...])
            before.wait()
            target[part] = (n1[part].astype(F32) - pulled).astype(BF)

        response[...] = total_of(own, got_own).astype(BF)
        pull(k1.at[:at], pl.ds(0, at), noise_copy)
        copies[3].wait()
        pull(tail, pl.ds(at, quarter), arrow_copy)
        whole[...] = (dot(e0[...], bar[...]) + dot(response[...], target[...])).T
        part_own[...] = whole[part_rows(0)]
        for step in peers:
            part_other[step - 1] = whole[part_rows(step)].astype(BF)

    def last_own_kernel(d1, target, value):
        lower_own(d1, target, value)

    def core_sum_kernel(part, _, *refs):
        got, (out, _) = refs[:-2], refs[-2:]
        total = part[...]
        for piece in got:
            total = total + piece[...].astype(F32)
        out[...] = total.astype(BF)

    def fold_kernel(sent, got, out):
        out[...] = (sent[...].astype(F32) + got[...].astype(F32)).astype(BF)

    def last_solve_kernel(d1, first, *refs):
        got, (own, other, value) = refs[: n_space - 1], refs[n_space - 1 :]
        value[...] = first[...]
        lower_rest(d1, got, value)
        lower_rows(value[...].T.astype(BF), d1, own, other)

    def response_kernel(k1, tail, response, own, other):
        full_rows(response, k1, tail, own, other)

    def pass_kernel(k1, tail, mask, solved, *refs):
        got, (base, own, other) = refs[: n_space - 1], refs[n_space - 1 :]
        value = jnp.where(mask[:1, :1] > 0, total_of(solved, got), 0.0)
        base[...] = value
        full_rows(value.astype(BF), k1, tail, own, other)

    def first_response_kernel(d0, e0, pushed, *refs):
        got, (own, other) = refs[: n_space - 1], refs[n_space - 1 :]
        left = (e0[...].astype(F32) - total_of(pushed, got)).astype(BF)
        lower_rows(left, d0, own, other)

    def first_solve_kernel(d0, value_rows, passed, *refs):
        got, (own, other) = refs[: n_space - 1], refs[n_space - 1 :]
        left = (value_rows[...] - total_of(passed, got)).astype(BF)
        lower_rows(left, d0, own, other)

    def turn_kernel(base, response, first, noise_fixed, tip, *refs):
        got, (last_base, last_resp, first_resp, noise_rows) = refs[: n_space - 1], refs[n_space - 1 :]
        noise_rows[...] = noise_fixed[...].T
        last_base[...] = base[...].T
        upper = tip[...].astype(F32).T.astype(BF)

        def through_tip(right):
            inner = dot(tip[...], right).astype(BF)
            return dot(upper, inner).T.astype(BF)

        last_resp[...] = through_tip(response[...])
        first_resp[...] = through_tip(total_of(first, got).astype(BF))

    def turn_first_kernel(solved, *refs):
        got, out = refs[:-1], refs[-1]
        out[...] = total_of(solved, got).T

    def mixed_kernel(noise_rows, *refs):
        terms, out = refs[:-1], refs[-1]
        total = terms[0][...].astype(F32)
        for piece in terms[1:]:
            total = total + piece[...].astype(F32)
        out[...] = (noise_rows[...] - total).astype(BF)

    def final_kernel(bases, responses, mixed, *refs):
        got, (out, whole, result, sems) = refs[: n_space - 1], refs[n_space - 1 :]
        for step, piece in enumerate([mixed, *got]):
            whole[part_rows(step)] = piece[...]
        copies = []
        for slot in range(2):
            for i in range(tiles):
                at = i * tile
                part = (slot, pl.ds(at, tile))
                update = dot_last(responses[slot][at : at + tile], whole[...])
                result[part] = (bases[slot][at : at + tile] - update).astype(BF)
                copies.append(
                    pltpu.make_async_copy(result.at[part], out.at[part], sems.at[slot, i])
                )
                copies[-1].start()
        for copy in copies:
            copy.wait()

    def fixed_kernel(tip, mixed, out):
        forward = dot_last(mixed[...], tip[...])
        out[...] = dot(forward.astype(BF), tip[...]).T

    def swap(value, step):
        pairs = [(i, (i - step) % n_space) for i in range(n_space)]
        return lax.ppermute(value, "space", pairs)

    def send_up(value):
        return [swap(value, -step) for step in peers]

    def send_down(values):
        return [swap(values[step - 1], step) for step in peers]

    bits = [1 << i for i in range(n_tm.bit_length() - 1)]
    assert n_tm == 1 << len(bits)

    wide = 2 * rows * nodes * columns
    factor_bytes = 2 * rows * nodes
    node_f32, node_bf = shape_of((rows, columns), F32), shape_of((rows, columns), BF)
    flat_f32 = shape_of((columns, rows), F32)
    flat_others = shape_of((n_space - 1, columns, rows), BF)
    fixed_f32 = shape_of((fixed_rows, rows), F32)
    fixed_bf = shape_of((fixed_rows, rows), BF)
    fixed_others = shape_of((n_space - 1, fixed_rows, rows), BF)
    part_bf = shape_of((width, fixed_rows), BF)
    by_node = shape_of((rows, fixed_rows), BF)
    in_vmem = pltpu.VMEM((rows, nodes), BF)
    dma = pltpu.SemaphoreType.DMA

    def fold(sent, got, after):
        size = width * fixed_rows
        return call(fold_kernel, [part_bf], [sent, got], size, 6 * size, after=after)[0]

    def swap_bit(value, bit):
        return lax.ppermute(value, "tm", [(i, i ^ bit) for i in range(n_tm)])

    def on_device(diag_inverse, coupling, arrow, tip_inverse, noise, noise_fixed, section_lengths):
        got_noise = send_up(noise)
        d0, d1, own, other, value, mask = call(
            start_kernel,
            [in_vmem, in_vmem, fixed_f32, fixed_others, node_f32, shape_of((8, 128), F32)],
            [diag_inverse, arrow, noise, section_lengths],
            wide,
            2 * factor_bytes,
            {i: pltpu.HBM for i in range(4)},
            [
                pltpu.VMEM((fixed_rows, rows), BF),
                pltpu.VMEM((rows, columns), BF),
                pltpu.SMEM(section_lengths.shape, jnp.int32),
                dma((n_space, tiles)),
                dma((n_space, tiles)),
                dma((3,)),
            ],
        )
        got_response = send_down(other)
        value, bar, k1 = call(
            first_value_kernel,
            [node_f32, node_bf, in_vmem],
            [d0, value, coupling, *got_noise],
            wide // 2,
            factor_bytes,
            {2: pltpu.HBM},
            [dma((1,))],
        )
        got_bar = send_up(bar)
        value_rows, k1 = call(
            load_kernel,
            [flat_f32, in_vmem],
            [coupling, value, k1],
            wide // 8,
            factor_bytes,
            {0: pltpu.HBM, 2: pl.ANY, ("out", 1): pl.ANY},
            [dma((2,))],
            aliases={2: 1},
        )
        tail, target, part_own, part_other, response, e0 = call(
            target_kernel,
            [
                pltpu.VMEM((quarter, nodes), BF),
                node_bf,
                shape_of((width, fixed_rows), F32),
                shape_of((n_space - 1, width, fixed_rows), BF),
                fixed_bf,
                fixed_bf,
            ],
            [k1, coupling, bar, noise, arrow, own, *got_bar, *got_response],
            wide,
            factor_bytes,
            {1: pltpu.HBM, 3: pltpu.HBM, 4: pltpu.HBM},
            [
                pltpu.VMEM((rows, columns), BF),
                pltpu.VMEM((columns, fixed_rows), F32),
                dma((3,)),
            ],
        )
        got_parts = send_down(part_other)
        (value,) = call(last_own_kernel, [node_f32], [d1, target], wide // 3, factor_bytes // 4)
        sent, target = call(
            core_sum_kernel,
            [part_bf, node_bf],
            [part_own, target, *got_parts],
            width * fixed_rows,
            8 * width * fixed_rows,
            {1: pl.ANY, ("out", 1): pl.ANY},
            aliases={1: 1},
            after=value,
        )
        got_target = send_up(target)
        left = list(bits)
        got = [swap_bit(sent, left.pop(0))] if left else []

        def advance(after):
            nonlocal sent, got
            if left:
                sent = fold(sent, *got, after)
                got = [swap_bit(sent, left.pop(0))]

        solved, other = call(
            last_solve_kernel,
            [flat_f32, flat_others],
            [d1, value, *got_target],
            wide * 3 // 2,
            factor_bytes,
            scratch=[pltpu.VMEM((rows, columns), F32)],
            after=sent,
        )
        got_solved = send_down(other)
        advance(solved)
        pushed, other = call(
            response_kernel, [fixed_f32, fixed_others], [k1, tail, response], wide, factor_bytes, after=sent
        )
        got_pushed = send_down(other)
        base, passed, other = call(
            pass_kernel,
            [flat_f32, flat_f32, flat_others],
            [k1, tail, mask, solved, *got_solved],
            wide,
            factor_bytes,
            after=pushed,
        )
        got_passed = send_down(other)
        advance(base)
        solved, other = call(
            first_solve_kernel,
            [flat_f32, flat_others],
            [d0, value_rows, passed, *got_passed],
            wide,
            factor_bytes,
            after=sent,
        )
        got_solved = send_down(other)
        advance(solved)
        first, other = call(
            first_response_kernel,
            [fixed_f32, fixed_others],
            [d0, e0, pushed, *got_pushed],
            wide,
            factor_bytes,
            after=sent,
        )
        got_first = send_down(other)
        last_base, last_resp, first_resp, noise_rows = call(
            turn_kernel,
            [node_f32, by_node, by_node, shape_of((width, fixed_rows), F32)],
            [base, response, first, noise_fixed, tip_inverse, *got_first],
            wide,
            factor_bytes,
            after=first,
        )
        (first_base,) = call(
            turn_first_kernel, [node_f32], [solved, *got_solved], wide, factor_bytes, after=noise_rows
        )
        while left:
            advance(None)
        (mixed,) = call(
            mixed_kernel,
            [part_bf],
            [noise_rows, sent, *got],
            width * fixed_rows,
            8 * width * fixed_rows,
            after=first_base,
        )
        got_mixed = send_up(mixed)
        (fixed_out,) = call(
            fixed_kernel,
            [shape_of((fixed_rows, width), F32)],
            [tip_inverse, mixed],
            wide,
            factor_bytes,
        )
        (sample,) = call(
            lambda a, b, c, d, *refs: final_kernel((a, b), (c, d), *refs),
            [shape_of((2, rows, columns), BF)],
            [first_base, last_base, first_resp, last_resp, mixed, *got_mixed],
            4 * rows * fixed_rows * columns,
            factor_bytes,
            {("out", 0): pl.ANY},
            [
                pltpu.VMEM((columns, fixed_rows), BF),
                pltpu.VMEM((2, rows, columns), BF),
                dma((2, tiles)),
            ],
            after=fixed_out,
        )
        return (sample, fixed_out)

    return on_device


def solution(mesh):
    sizes = dict(mesh.shape)

    def program(diag_inverse, coupling, arrow, tip_inverse, noise, noise_fixed, section_lengths):
        device = build(
            sizes["tm"],
            sizes["space"],
            diag_inverse.shape[1] // sizes["space"],
            noise.shape[2],
            arrow.shape[1],
        )
        return jax.shard_map(
            device,
            mesh=mesh,
            in_specs=(
                P("tm", "space", None),
                P("tm", "space", None),
                P("tm", None, "space"),
                P(),
                P("tm", "space", None),
                P(None, "space"),
                P(),
            ),
            out_specs=(P("tm", "space", None), P(None, "space")),
            check_vma=False,
        )(diag_inverse, coupling, arrow, tip_inverse, noise, noise_fixed, section_lengths)

    return program
```

```python
import jax
import jax.numpy as jnp
from jax import lax
from jax.experimental import pallas as pl
from jax.experimental.pallas import tpu as pltpu
from jax.sharding import PartitionSpec as P

BF = jnp.bfloat16
F32 = jnp.float32
MIB = 1 << 20


def dot(left, right):
    return jnp.dot(left, right, preferred_element_type=F32)


def dot_last(left, right):
    return lax.dot_general(left, right, (((1,), (1,)), ((), ())), preferred_element_type=F32)


def rounded(value):
    return value.astype(BF).astype(F32)


def total_of(own_ref, got_refs):
    total = rounded(own_ref[...])
    for got in got_refs:
        total = total + got[...].astype(F32)
    return total


def shape_of(shape, dtype):
    return jax.ShapeDtypeStruct(shape, dtype)


def build(n_tm, n_space, rows, columns, fixed_rows):
    nodes = n_space * rows
    tile = 256 if rows % 256 == 0 else rows
    tiles = rows // tile
    eighth = rows // 8
    head = rows - eighth
    width = columns // n_space
    peers = range(1, n_space)

    def at_core():
        return lax.axis_index("space")

    def block(step, offset=0, size=rows):
        owner = lax.rem(at_core() - step + n_space, n_space)
        return pl.ds(pl.multiple_of(owner * rows + offset, tile), size)

    def part_rows(step):
        owner = lax.rem(at_core() - step + n_space, n_space)
        return pl.ds(pl.multiple_of(owner * width, width), width)

    def call(body, outs, args, cover, places=None, scratch=(), after=None, aliases=None, after_place=pl.ANY):
        places = dict(places or {})
        args = list(args)
        count = len(args)
        if after is not None:
            args.append(after)
            places[count] = after_place

        def run(*refs):
            body(*refs[:count], *refs[len(args) :])

        specs = [pl.BlockSpec(memory_space=places.get(i, pltpu.VMEM)) for i in range(len(args))]
        args = [
            pltpu.with_memory_space_constraint(a, pltpu.HBM)
            if places.get(i) is pltpu.HBM
            else a
            for i, a in enumerate(args)
        ]
        return pl.pallas_call(
            run,
            in_specs=specs,
            out_specs=[
                pl.BlockSpec(memory_space=places.get(("out", i), pltpu.VMEM))
                for i in range(len(outs))
            ],
            out_shape=outs,
            scratch_shapes=list(scratch),
            input_output_aliases=aliases or {},
            cost_estimate=pl.CostEstimate(
                flops=int(cover * 1e9), bytes_accessed=0, transcendentals=0
            ),
            compiler_params=pltpu.CompilerParams(vmem_limit_bytes=16 * MIB),
        )(*args)

    def lower_rows(left, factor, own_ref, other_ref):
        for step in peers:

            @pl.when(at_core() >= step)
            def _():
                other_ref[step - 1] = dot(left[...], factor[:, block(step)]).astype(BF)

            @pl.when(at_core() < step)
            def _():
                other_ref[step - 1] = jnp.zeros_like(other_ref[step - 1])

        for j in range(tiles):
            at = j * tile
            own_ref[:, at : at + tile] = dot(left[:, at:], factor[at:, block(0, at, tile)])

    def full_rows(left, factor, tail, own_ref, other_ref):
        for step in (*peers, 0):
            product = dot(left[:, :head], factor[:head, block(step)])
            product = product + dot(left[:, head:], tail[:, block(step)])
            if step:
                other_ref[step - 1] = product.astype(BF)
            else:
                own_ref[...] = product

    def lower_own(factor, right, out_ref, wait=None):
        for i in range(tiles):
            at = i * tile
            if wait:
                wait(i)
            out_ref[at : at + tile] = dot(
                factor[at : at + tile, block(0, 0, at + tile)], right[: at + tile]
            )

    def lower_rest(factor, got, value):
        for step in peers:

            @pl.when(at_core() >= step)
            def _():
                value[...] = value[...] + dot(factor[:, block(step)], got[step - 1][...])

    def start_kernel(
        diag, arrow, noise, lengths,
        d0, d1, own, other, n0, mask,
        e1, live_scratch, sem1, sem0, sems,
    ):
        arrow_copy = pltpu.make_async_copy(arrow.at[1], e1, sems.at[0])
        noise_copy = pltpu.make_async_copy(noise.at[0], n0, sems.at[1])
        live_copy = pltpu.make_async_copy(lengths, live_scratch, sems.at[2])

        def lower_copies(slot, target, sem):
            copies = {}
            for step in range(n_space):
                for i in range(tiles):
                    at = i * tile
                    size = rows if step else at + tile
                    part = (pl.ds(at, tile), block(step, 0, size))
                    copies[step, i] = pltpu.make_async_copy(
                        diag.at[(slot, *part)], target.at[part], sem.at[step, i]
                    )
            return copies

        def each(copies, i, act):
            act(copies[0, i])
            for step in peers:

                @pl.when(at_core() >= step)
                def _():
                    act(copies[step, i])

        copies1 = lower_copies(1, d1, sem1)
        copies0 = lower_copies(0, d0, sem0)
        live_copy.start()
        arrow_copy.start()
        for i in range(tiles):
            each(copies1, i, lambda copy: copy.start(priority=i % 2))
        live_copy.wait()
        arrow_copy.wait()
        live = live_scratch[lax.axis_index("tm")] > 1
        mask[...] = jnp.where(live, jnp.ones_like(mask[...]), jnp.zeros_like(mask[...]))
        e1[...] = jnp.where(live, e1[...], jnp.zeros_like(e1[...]))
        for i in range(tiles):
            each(copies1, i, lambda copy: copy.wait())
            each(copies0, i, lambda copy: copy.start(priority=i % 2))
        noise_copy.start()
        lower_rows(e1, d1, own, other)
        for i in range(tiles):
            each(copies0, i, lambda copy: copy.wait())
        noise_copy.wait()

    def k1_copies(coupling, k1, first, count, sems):
        copies = []
        for i in range(count):
            part = pl.ds((first + i) * eighth, eighth)
            target = k1.at[part] if k1.shape[0] == rows else k1
            copies.append(pltpu.make_async_copy(coupling.at[1, part], target, sems.at[i]))
            copies[-1].start(priority=i % 2)
        return copies

    def first_value_kernel(d0, n0, coupling, *refs):
        got, (out, bar, k1, sems) = refs[: n_space - 1], refs[n_space - 1 :]
        copies = k1_copies(coupling, k1, 0, 3, sems)
        lower_own(d0, n0, out)
        lower_rest(d0, [piece.at[0] for piece in got], out)
        bar[...] = out[...].astype(BF)
        for copy in copies:
            copy.wait()

    def load_kernel(coupling, value, _, value_rows, k1, sems):
        copies = k1_copies(coupling, k1, 3, 4, sems)
        value_rows[...] = value[...].T
        for copy in copies:
            copy.wait()

    def target_kernel(k1, coupling, bar, noise, arrow, own, *refs):
        got, refs = refs[: n_space - 1], refs[n_space - 1 :]
        got_own, refs = refs[: n_space - 1], refs[n_space - 1 :]
        tail, target, part_own, part_other, response, e0, n1, whole, sems = refs
        noise_copy = pltpu.make_async_copy(noise.at[1], n1, sems.at[1])
        arrow_copy = pltpu.make_async_copy(arrow.at[0], e0, sems.at[2])
        noise_copy.start()
        (tail_copy,) = k1_copies(coupling, tail, 7, 1, sems)
        arrow_copy.start()

        def pull(factor, part, before):
            pulled = dot(factor[:, block(0)], bar[...])
            for step in peers:
                pulled = pulled + dot(factor[:, block(step)], got[step - 1][...])
            before.wait()
            target[part] = (n1[part].astype(F32) - pulled).astype(BF)

        response[...] = total_of(own, got_own).astype(BF)
        pull(k1.at[:head], pl.ds(0, head), noise_copy)
        tail_copy.wait()
        pull(tail, pl.ds(head, eighth), arrow_copy)
        whole[...] = (dot(e0[...], bar[...]) + dot(response[...], target[...])).T
        part_own[...] = whole[part_rows(0)]
        for step in peers:
            part_other[step - 1] = whole[part_rows(step)].astype(BF)

    def last_own_kernel(d1, target, value):
        lower_own(d1, target, value)

    def core_sum_kernel(part, _, *refs):
        got, (out, _) = refs[:-2], refs[-2:]
        total = part[...]
        for piece in got:
            total = total + piece[...].astype(F32)
        out[...] = total.astype(BF)

    def fold_kernel(sent, got, out):
        out[...] = (sent[...].astype(F32) + got[...].astype(F32)).astype(BF)

    def last_solve_kernel(d1, first, *refs):
        got, (own, other, value) = refs[: n_space - 1], refs[n_space - 1 :]
        value[...] = first[...]
        lower_rest(d1, got, value)
        lower_rows(value[...].T.astype(BF), d1, own, other)

    def response_kernel(k1, tail, response, own, other):
        full_rows(response, k1, tail, own, other)

    def pass_kernel(k1, tail, mask, solved, *refs):
        got, (base, own, other) = refs[: n_space - 1], refs[n_space - 1 :]
        value = jnp.where(mask[:1, :1] > 0, total_of(solved, got), 0.0)
        base[...] = value
        full_rows(value.astype(BF), k1, tail, own, other)

    def first_response_kernel(d0, e0, pushed, *refs):
        got, (own, other) = refs[: n_space - 1], refs[n_space - 1 :]
        left = (e0[...].astype(F32) - total_of(pushed, got)).astype(BF)
        lower_rows(left, d0, own, other)

    def first_solve_kernel(d0, value_rows, passed, *refs):
        got, (own, other) = refs[: n_space - 1], refs[n_space - 1 :]
        left = (value_rows[...] - total_of(passed, got)).astype(BF)
        lower_rows(left, d0, own, other)

    def through_tip(tip, right):
        inner = dot(tip, right).astype(BF)
        return dot(tip.astype(F32).T.astype(BF), inner).T.astype(BF)

    def turn_last_kernel(base, response, noise_fixed, tip, last_base, last_resp, noise_rows):
        noise_rows[...] = noise_fixed[...].T
        last_base[...] = base[...].T
        last_resp[...] = through_tip(tip[...], response[...])

    def turn_response_kernel(first, tip, *refs):
        got, out = refs[:-1], refs[-1]
        out[...] = through_tip(tip[...], total_of(first, got).astype(BF))

    def turn_first_kernel(solved, *refs):
        got, out = refs[:-1], refs[-1]
        out[...] = total_of(solved, got).T

    def mixed_kernel(noise_rows, *refs):
        terms, out = refs[:-1], refs[-1]
        total = terms[0][...].astype(F32)
        for piece in terms[1:]:
            total = total + piece[...].astype(F32)
        out[...] = (noise_rows[...] - total).astype(BF)

    def final_kernel(bases, responses, mixed, *refs):
        got, (out, whole, result, sems) = refs[: n_space - 1], refs[n_space - 1 :]
        for step, piece in enumerate([mixed, *got]):
            whole[part_rows(step)] = piece[...]
        copies = []
        for slot in range(2):
            for i in range(tiles):
                at = i * tile
                part = (slot, pl.ds(at, tile))
                update = dot_last(responses[slot][at : at + tile], whole[...])
                result[part] = (bases[slot][at : at + tile] - update).astype(BF)
                copies.append(
                    pltpu.make_async_copy(result.at[part], out.at[part], sems.at[slot, i])
                )
                copies[-1].start()
        for copy in copies:
            copy.wait()

    def fixed_kernel(tip, mixed, out):
        forward = dot_last(mixed[...], tip[...])
        out[...] = dot(forward.astype(BF), tip[...]).T

    def swap(value, step):
        pairs = [(i, (i - step) % n_space) for i in range(n_space)]
        return lax.ppermute(value, "space", pairs)

    def send_up(value):
        return [swap(value, -step) for step in peers]

    def send_down(values):
        return [swap(values[step - 1], step) for step in peers]

    steps = n_tm.bit_length() - 1
    assert n_tm == 1 << steps

    def swap_step(value, step):
        pairs = []
        for i in range(n_tm):
            for core in range(n_space):
                bit = 1 << (step + core * steps // n_space) % steps
                pairs.append((i * n_space + core, (i ^ bit) * n_space + core))
        return lax.ppermute(value, ("tm", "space"), pairs)

    node_f32, node_bf = shape_of((rows, columns), F32), shape_of((rows, columns), BF)
    flat_f32 = shape_of((columns, rows), F32)
    flat_others = shape_of((n_space - 1, columns, rows), BF)
    fixed_f32 = shape_of((fixed_rows, rows), F32)
    fixed_bf = shape_of((fixed_rows, rows), BF)
    fixed_others = shape_of((n_space - 1, fixed_rows, rows), BF)
    part_bf = shape_of((width, fixed_rows), BF)
    by_node = shape_of((rows, fixed_rows), BF)
    in_vmem = pltpu.VMEM((rows, nodes), BF)
    dma = pltpu.SemaphoreType.DMA

    def fold(sent, got, after):
        size = width * fixed_rows
        return call(fold_kernel, [part_bf], [sent, got], size, 6 * size, after=after)[0]

    def on_device(diag_inverse, coupling, arrow, tip_inverse, noise, noise_fixed, section_lengths):
        got_noise = send_up(noise)
        d0, d1, own, other, n0, mask = call(
            start_kernel,
            [in_vmem, in_vmem, fixed_f32, fixed_others, node_bf, shape_of((8, 128), F32)],
            [diag_inverse, arrow, noise, section_lengths],
            8,
            {i: pltpu.HBM for i in range(4)},
            [
                pltpu.VMEM((fixed_rows, rows), BF),
                pltpu.SMEM(section_lengths.shape, jnp.int32),
                dma((n_space, tiles)),
                dma((n_space, tiles)),
                dma((3,)),
            ],
        )
        got_response = send_down(other)
        value, bar, k1 = call(
            first_value_kernel,
            [node_f32, node_bf, in_vmem],
            [d0, n0, coupling, *got_noise],
            8,
            {2: pltpu.HBM},
            [dma((3,))],
        )
        got_bar = send_up(bar)
        value_rows, k1 = call(
            load_kernel,
            [flat_f32, in_vmem],
            [coupling, value, k1],
            8,
            {0: pltpu.HBM, 2: pl.ANY, ("out", 1): pl.ANY},
            [dma((4,))],
            aliases={2: 1},
        )
        tail, target, part_own, part_other, response, e0 = call(
            target_kernel,
            [
                pltpu.VMEM((eighth, nodes), BF),
                node_bf,
                shape_of((width, fixed_rows), F32),
                shape_of((n_space - 1, width, fixed_rows), BF),
                fixed_bf,
                fixed_bf,
            ],
            [k1, coupling, bar, noise, arrow, own, *got_bar, *got_response],
            8,
            {1: pltpu.HBM, 3: pltpu.HBM, 4: pltpu.HBM},
            [
                pltpu.VMEM((rows, columns), BF),
                pltpu.VMEM((columns, fixed_rows), F32),
                dma((3,)),
            ],
        )
        got_parts = send_down(part_other)
        (value,) = call(last_own_kernel, [node_f32], [d1, target], 8)
        sent, target = call(
            core_sum_kernel,
            [part_bf, node_bf],
            [part_own, target, *got_parts],
            0.2,
            {1: pl.ANY, ("out", 1): pl.ANY},
            aliases={1: 1},
            after=value,
        )
        got_target = send_up(target)
        step = 0
        got = []

        def advance(after=None):
            nonlocal sent, got, step
            if step == steps:
                return
            if step:
                (sent,) = call(fold_kernel, [part_bf], [sent, *got], 0.2, after=after)
            got = [swap_step(sent, step)]
            step += 1

        advance()
        solved, other = call(
            last_solve_kernel,
            [flat_f32, flat_others],
            [d1, value, *got_target],
            8,
            scratch=[pltpu.VMEM((rows, columns), F32)],
            after=sent,
        )
        got_solved = send_down(other)
        advance(solved)
        pushed, other = call(
            response_kernel, [fixed_f32, fixed_others], [k1, tail, response], 8, after=sent
        )
        got_pushed = send_down(other)
        base, passed, other = call(
            pass_kernel,
            [flat_f32, flat_f32, flat_others],
            [k1, tail, mask, solved, *got_solved],
            8,
            after=pushed,
        )
        got_passed = send_down(other)
        advance(base)
        last_base, last_resp, noise_rows = call(
            turn_last_kernel,
            [node_f32, by_node, shape_of((width, fixed_rows), F32)],
            [base, response, noise_fixed, tip_inverse],
            8,
            after=sent,
        )
        solved, other = call(
            first_solve_kernel,
            [flat_f32, flat_others],
            [d0, value_rows, passed, *got_passed],
            8,
            after=noise_rows,
        )
        got_solved = send_down(other)
        advance(solved)
        first, other = call(
            first_response_kernel,
            [fixed_f32, fixed_others],
            [d0, e0, pushed, *got_pushed],
            8,
            after=sent,
        )
        got_first = send_down(other)
        (first_base,) = call(turn_first_kernel, [node_f32], [solved, *got_solved], 8, after=first)
        (first_resp,) = call(
            turn_response_kernel, [by_node], [first, tip_inverse, *got_first], 8, after=first_base
        )
        while step < steps:
            advance()
        (mixed,) = call(mixed_kernel, [part_bf], [noise_rows, sent, *got], 0.2, after=first_resp)
        got_mixed = send_up(mixed)
        (fixed_out,) = call(
            fixed_kernel, [shape_of((fixed_rows, width), F32)], [tip_inverse, mixed], 8
        )
        (sample,) = call(
            lambda a, b, c, d, *refs: final_kernel((a, b), (c, d), *refs),
            [shape_of((2, rows, columns), BF)],
            [first_base, last_base, first_resp, last_resp, mixed, *got_mixed],
            8,
            {("out", 0): pl.ANY},
            [
                pltpu.VMEM((columns, fixed_rows), BF),
                pltpu.VMEM((2, rows, columns), BF),
                dma((2, tiles)),
            ],
            after=fixed_out,
            after_place=pltpu.HBM,
        )
        return (sample, fixed_out)

    return on_device


def solution(mesh):
    sizes = dict(mesh.shape)

    def program(diag_inverse, coupling, arrow, tip_inverse, noise, noise_fixed, section_lengths):
        device = build(
            sizes["tm"],
            sizes["space"],
            diag_inverse.shape[1] // sizes["space"],
            noise.shape[2],
            arrow.shape[1],
        )
        return jax.shard_map(
            device,
            mesh=mesh,
            in_specs=(
                P("tm", "space", None),
                P("tm", "space", None),
                P("tm", None, "space"),
                P(),
                P("tm", "space", None),
                P(None, "space"),
                P(),
            ),
            out_specs=(P("tm", "space", None), P(None, "space")),
            check_vma=False,
        )(diag_inverse, coupling, arrow, tip_inverse, noise, noise_fixed, section_lengths)

    return program
```

```python
import jax
import jax.numpy as jnp
from jax import lax
from jax.experimental import pallas as pl
from jax.experimental.pallas import tpu as pltpu
from jax.sharding import PartitionSpec as P

BF = jnp.bfloat16
F32 = jnp.float32
MIB = 1 << 20


def dot(left, right):
    return jnp.dot(left, right, preferred_element_type=F32)


def dot_last(left, right):
    return lax.dot_general(left, right, (((1,), (1,)), ((), ())), preferred_element_type=F32)


def rounded(value):
    return value.astype(BF).astype(F32)


def total_of(own_ref, got_refs):
    total = rounded(own_ref[...])
    for got in got_refs:
        total = total + got[...].astype(F32)
    return total


def shape_of(shape, dtype):
    return jax.ShapeDtypeStruct(shape, dtype)


def build(n_tm, n_space, rows, columns, fixed_rows):
    nodes = n_space * rows
    tile = 256 if rows % 256 == 0 else rows
    tiles = rows // tile
    eighth = rows // 8
    head = rows - eighth
    width = columns // n_space
    peers = range(1, n_space)

    def at_core():
        return lax.axis_index("space")

    def block(step, offset=0, size=rows):
        owner = lax.rem(at_core() - step + n_space, n_space)
        return pl.ds(pl.multiple_of(owner * rows + offset, tile), size)

    def part_rows(step):
        owner = lax.rem(at_core() - step + n_space, n_space)
        return pl.ds(pl.multiple_of(owner * width, width), width)

    def call(body, outs, args, cover, places=None, scratch=(), after=None, aliases=None, after_place=pl.ANY):
        places = dict(places or {})
        args = list(args)
        count = len(args)
        if after is not None:
            args.append(after)
            places[count] = after_place

        def run(*refs):
            body(*refs[:count], *refs[len(args) :])

        specs = [pl.BlockSpec(memory_space=places.get(i, pltpu.VMEM)) for i in range(len(args))]
        args = [
            pltpu.with_memory_space_constraint(a, pltpu.HBM)
            if places.get(i) is pltpu.HBM
            else a
            for i, a in enumerate(args)
        ]
        return pl.pallas_call(
            run,
            in_specs=specs,
            out_specs=[
                pl.BlockSpec(memory_space=places.get(("out", i), pltpu.VMEM))
                for i in range(len(outs))
            ],
            out_shape=outs,
            scratch_shapes=list(scratch),
            input_output_aliases=aliases or {},
            cost_estimate=pl.CostEstimate(
                flops=int(cover * 1e9), bytes_accessed=0, transcendentals=0
            ),
            compiler_params=pltpu.CompilerParams(vmem_limit_bytes=16 * MIB),
        )(*args)

    def lower_rows(left, factor, own_ref, other_ref):
        for step in peers:

            @pl.when(at_core() >= step)
            def _():
                other_ref[step - 1] = dot(left[...], factor[:, block(step)]).astype(BF)

            @pl.when(at_core() < step)
            def _():
                other_ref[step - 1] = jnp.zeros_like(other_ref[step - 1])

        for j in range(tiles):
            at = j * tile
            own_ref[:, at : at + tile] = dot(left[:, at:], factor[at:, block(0, at, tile)])

    def full_rows(left, factor, own_ref, other_ref):
        for step in peers:
            other_ref[step - 1] = dot(left[...], factor[:, block(step)]).astype(BF)
        own_ref[...] = dot(left[...], factor[:, block(0)])

    def lower_own(factor, right, out_ref, wait=None):
        for i in range(tiles):
            at = i * tile
            if wait:
                wait(i)
            out_ref[at : at + tile] = dot(
                factor[at : at + tile, block(0, 0, at + tile)], right[: at + tile]
            )

    def lower_rest(factor, got, value):
        for step in peers:

            @pl.when(at_core() >= step)
            def _():
                value[...] = value[...] + dot(factor[:, block(step)], got[step - 1][...])

    def start_kernel(
        diag, arrow, noise, lengths,
        d0, d1, own, other, n0, mask,
        e1, live_scratch, sem1, sem0, sems,
    ):
        arrow_copy = pltpu.make_async_copy(arrow.at[1], e1, sems.at[0])
        noise_copy = pltpu.make_async_copy(noise.at[0], n0, sems.at[1])
        live_copy = pltpu.make_async_copy(lengths, live_scratch, sems.at[2])

        def lower_copies(slot, target, sem):
            copies = {}
            for step in range(n_space):
                for i in range(tiles):
                    at = i * tile
                    size = rows if step else at + tile
                    part = (pl.ds(at, tile), block(step, 0, size))
                    copies[step, i] = pltpu.make_async_copy(
                        diag.at[(slot, *part)], target.at[part], sem.at[step, i]
                    )
            return copies

        def each(copies, i, act):
            act(copies[0, i])
            for step in peers:

                @pl.when(at_core() >= step)
                def _():
                    act(copies[step, i])

        copies1 = lower_copies(1, d1, sem1)
        copies0 = lower_copies(0, d0, sem0)
        live_copy.start()
        arrow_copy.start()
        for i in range(tiles):
            each(copies1, i, lambda copy: copy.start(priority=i % 2))
        live_copy.wait()
        arrow_copy.wait()
        live = live_scratch[lax.axis_index("tm")] > 1
        mask[...] = jnp.where(live, jnp.ones_like(mask[...]), jnp.zeros_like(mask[...]))
        e1[...] = jnp.where(live, e1[...], jnp.zeros_like(e1[...]))
        for i in range(tiles):
            each(copies1, i, lambda copy: copy.wait())
            each(copies0, i, lambda copy: copy.start(priority=i % 2))
        noise_copy.start()
        lower_rows(e1, d1, own, other)
        for i in range(tiles):
            each(copies0, i, lambda copy: copy.wait())
        noise_copy.wait()

    def k1_copies(coupling, k1, first, count, sems):
        copies = []
        for i in range(count):
            part = pl.ds((first + i) * eighth, eighth)
            target = k1.at[part] if k1.shape[0] == rows else k1
            copies.append(pltpu.make_async_copy(coupling.at[1, part], target, sems.at[i]))
            copies[-1].start(priority=i % 2)
        return copies

    def first_value_kernel(d0, n0, coupling, noise, *refs):
        got, (out, bar, k1, n1, sems) = refs[: n_space - 1], refs[n_space - 1 :]
        copies = k1_copies(coupling, k1, 0, 3, sems)
        copies.append(pltpu.make_async_copy(noise.at[1], n1, sems.at[3]))
        copies[-1].start()
        lower_own(d0, n0, out)
        lower_rest(d0, [piece.at[0] for piece in got], out)
        bar[...] = out[...].astype(BF)
        for copy in copies:
            copy.wait()

    def load_kernel(coupling, value, _, value_rows, k1, sems):
        copies = k1_copies(coupling, k1, 3, 4, sems)
        value_rows[...] = value[...].T
        for copy in copies:
            copy.wait()

    def target_kernel(k1, coupling, bar, n1, arrow, own, *refs):
        got, refs = refs[: n_space - 1], refs[n_space - 1 :]
        got_own, refs = refs[: n_space - 1], refs[n_space - 1 :]
        target, part_own, part_other, response, e0, tail, whole, sems = refs
        arrow_copy = pltpu.make_async_copy(arrow.at[0], e0, sems.at[1])
        (tail_copy,) = k1_copies(coupling, tail, 7, 1, sems)
        arrow_copy.start()

        def pull(at, size):
            factor = tail if at == head else k1.at[at : at + size]
            pulled = jnp.zeros((size, columns), F32)
            for step, piece in enumerate([bar, *got]):
                pulled = pulled + dot(factor[:, block(step)], piece[...])
            target[at : at + size] = (n1[at : at + size].astype(F32) - pulled).astype(BF)

        response[...] = total_of(own, got_own).astype(BF)
        for at in range(0, head, tile):
            pull(at, min(tile, head - at))
        arrow_copy.wait()
        whole[...] = dot(e0[...], bar[...])
        tail_copy.wait()
        pull(head, eighth)
        whole[...] = (whole[...] + dot(response[...], target[...])).T
        part_own[...] = whole[part_rows(0)]
        for step in peers:
            part_other[step - 1] = whole[part_rows(step)].astype(BF)

    def last_own_kernel(d1, target, coupling, _, value, k1, sems):
        (tail_copy,) = k1_copies(coupling, k1, 7, 1, sems)
        lower_own(d1, target, value)
        tail_copy.wait()

    def core_sum_kernel(part, _, *refs):
        got, (out, _) = refs[:-2], refs[-2:]
        total = part[...]
        for piece in got:
            total = total + piece[...].astype(F32)
        out[...] = total.astype(BF)

    def fold_kernel(sent, got, out):
        out[...] = (sent[...].astype(F32) + got[...].astype(F32)).astype(BF)

    def last_solve_kernel(d1, first, *refs):
        got, (own, other, value) = refs[: n_space - 1], refs[n_space - 1 :]
        value[...] = first[...]
        lower_rest(d1, got, value)
        lower_rows(value[...].T.astype(BF), d1, own, other)

    def response_kernel(k1, response, own, other):
        full_rows(response, k1, own, other)

    def pass_kernel(k1, mask, solved, *refs):
        got, (base, own, other) = refs[: n_space - 1], refs[n_space - 1 :]
        value = jnp.where(mask[:1, :1] > 0, total_of(solved, got), 0.0)
        base[...] = value
        full_rows(value.astype(BF), k1, own, other)

    def first_response_kernel(d0, e0, tip, pushed, *refs):
        got, (own, other) = refs[: n_space - 1], refs[n_space - 1 :]
        left = (e0[...].astype(F32) - total_of(pushed, got)).astype(BF)
        lower_rows(through_tip(tip[...], left).astype(BF), d0, own, other)

    def first_solve_kernel(d0, value_rows, passed, *refs):
        got, (own, other) = refs[: n_space - 1], refs[n_space - 1 :]
        left = (value_rows[...] - total_of(passed, got)).astype(BF)
        lower_rows(left, d0, own, other)

    def through_tip(tip, right):
        inner = dot(tip, right).astype(BF)
        return dot(tip.astype(F32).T.astype(BF), inner)

    def turn_last_kernel(base, response, noise_fixed, tip, last_base, last_resp, noise_rows):
        noise_rows[...] = noise_fixed[...].T
        last_base[...] = base[...].T
        last_resp[...] = through_tip(tip[...], response[...]).T.astype(BF)

    def turn_response_kernel(first, *refs):
        got, out = refs[:-1], refs[-1]
        out[...] = total_of(first, got).T.astype(BF)

    def turn_first_kernel(solved, *refs):
        got, out = refs[:-1], refs[-1]
        out[...] = total_of(solved, got).T

    def mixed_kernel(noise_rows, *refs):
        terms, out = refs[:-1], refs[-1]
        total = terms[0][...].astype(F32)
        for piece in terms[1:]:
            total = total + piece[...].astype(F32)
        out[...] = (noise_rows[...] - total).astype(BF)

    def final_kernel(bases, responses, mixed, *refs):
        got, (out, whole, result, sems) = refs[: n_space - 1], refs[n_space - 1 :]
        for step, piece in enumerate([mixed, *got]):
            whole[part_rows(step)] = piece[...]
        copies = []
        for slot in range(2):
            for i in range(tiles):
                at = i * tile
                part = (slot, pl.ds(at, tile))
                update = dot_last(responses[slot][at : at + tile], whole[...])
                result[part] = (bases[slot][at : at + tile] - update).astype(BF)
                copies.append(
                    pltpu.make_async_copy(result.at[part], out.at[part], sems.at[slot, i])
                )
                copies[-1].start()
        for copy in copies:
            copy.wait()

    def fixed_kernel(tip, mixed, out):
        forward = dot_last(mixed[...], tip[...])
        out[...] = dot(forward.astype(BF), tip[...]).T

    def swap(value, step):
        pairs = [(i, (i - step) % n_space) for i in range(n_space)]
        return lax.ppermute(value, "space", pairs)

    def send_up(value):
        return [swap(value, -step) for step in peers]

    def send_down(values):
        return [swap(values[step - 1], step) for step in peers]

    steps = n_tm.bit_length() - 1
    assert n_tm == 1 << steps

    def swap_step(value, step):
        pairs = []
        for i in range(n_tm):
            for core in range(n_space):
                bit = 1 << (step + core * steps // n_space) % steps
                pairs.append((i * n_space + core, (i ^ bit) * n_space + core))
        return lax.ppermute(value, ("tm", "space"), pairs)

    node_f32, node_bf = shape_of((rows, columns), F32), shape_of((rows, columns), BF)
    flat_f32 = shape_of((columns, rows), F32)
    flat_others = shape_of((n_space - 1, columns, rows), BF)
    fixed_f32 = shape_of((fixed_rows, rows), F32)
    fixed_bf = shape_of((fixed_rows, rows), BF)
    fixed_others = shape_of((n_space - 1, fixed_rows, rows), BF)
    part_bf = shape_of((width, fixed_rows), BF)
    by_node = shape_of((rows, fixed_rows), BF)
    in_vmem = pltpu.VMEM((rows, nodes), BF)
    dma = pltpu.SemaphoreType.DMA

    def fold(sent, got, after):
        size = width * fixed_rows
        return call(fold_kernel, [part_bf], [sent, got], size, 6 * size, after=after)[0]

    def on_device(diag_inverse, coupling, arrow, tip_inverse, noise, noise_fixed, section_lengths):
        got_noise = send_up(noise)
        d0, d1, own, other, n0, mask = call(
            start_kernel,
            [in_vmem, in_vmem, fixed_f32, fixed_others, node_bf, shape_of((8, 128), F32)],
            [diag_inverse, arrow, noise, section_lengths],
            8,
            {i: pltpu.HBM for i in range(4)},
            [
                pltpu.VMEM((fixed_rows, rows), BF),
                pltpu.SMEM(section_lengths.shape, jnp.int32),
                dma((n_space, tiles)),
                dma((n_space, tiles)),
                dma((3,)),
            ],
        )
        got_response = send_down(other)
        value, bar, k1, n1 = call(
            first_value_kernel,
            [node_f32, node_bf, in_vmem, node_bf],
            [d0, n0, coupling, noise, *got_noise],
            8,
            {2: pltpu.HBM, 3: pltpu.HBM},
            [dma((4,))],
        )
        got_bar = send_up(bar)
        value_rows, k1 = call(
            load_kernel,
            [flat_f32, in_vmem],
            [coupling, value, k1],
            8,
            {0: pltpu.HBM, 2: pl.ANY, ("out", 1): pl.ANY},
            [dma((4,))],
            aliases={2: 1},
        )
        target, part_own, part_other, response, e0 = call(
            target_kernel,
            [
                node_bf,
                shape_of((width, fixed_rows), F32),
                shape_of((n_space - 1, width, fixed_rows), BF),
                fixed_bf,
                fixed_bf,
            ],
            [k1, coupling, bar, n1, arrow, own, *got_bar, *got_response],
            8,
            {1: pltpu.HBM, 4: pltpu.HBM},
            [
                pltpu.VMEM((eighth, nodes), BF),
                pltpu.VMEM((columns, fixed_rows), F32),
                dma((2,)),
            ],
        )
        got_parts = send_down(part_other)
        value, k1 = call(
            last_own_kernel,
            [node_f32, in_vmem],
            [d1, target, coupling, k1],
            8,
            {2: pltpu.HBM, 3: pl.ANY, ("out", 1): pl.ANY},
            [dma((1,))],
            aliases={3: 1},
        )
        sent, target = call(
            core_sum_kernel,
            [part_bf, node_bf],
            [part_own, target, *got_parts],
            0.2,
            {1: pl.ANY, ("out", 1): pl.ANY},
            aliases={1: 1},
            after=value,
        )
        got_target = send_up(target)
        step = 0
        got = []

        def advance(after=None):
            nonlocal sent, got, step
            if step == steps:
                return
            if step:
                (sent,) = call(fold_kernel, [part_bf], [sent, *got], 0.2, after=after)
            got = [swap_step(sent, step)]
            step += 1

        advance()
        solved, other = call(
            last_solve_kernel,
            [flat_f32, flat_others],
            [d1, value, *got_target],
            8,
            scratch=[pltpu.VMEM((rows, columns), F32)],
            after=sent,
        )
        got_solved = send_down(other)
        advance(solved)
        pushed, other = call(
            response_kernel, [fixed_f32, fixed_others], [k1, response], 5, after=sent
        )
        got_pushed = send_down(other)
        base, passed, other = call(
            pass_kernel,
            [flat_f32, flat_f32, flat_others],
            [k1, mask, solved, *got_solved],
            8,
            after=pushed,
        )
        got_passed = send_down(other)
        advance(base)
        last_base, last_resp, noise_rows = call(
            turn_last_kernel,
            [node_f32, by_node, shape_of((width, fixed_rows), F32)],
            [base, response, noise_fixed, tip_inverse],
            5,
            after=sent,
        )
        solved, other = call(
            first_solve_kernel,
            [flat_f32, flat_others],
            [d0, value_rows, passed, *got_passed],
            8,
            after=noise_rows,
        )
        got_solved = send_down(other)
        advance(solved)
        first, other = call(
            first_response_kernel,
            [fixed_f32, fixed_others],
            [d0, e0, tip_inverse, pushed, *got_pushed],
            5,
            after=sent,
        )
        got_first = send_down(other)
        (first_base,) = call(turn_first_kernel, [node_f32], [solved, *got_solved], 8, after=first)
        (first_resp,) = call(
            turn_response_kernel, [by_node], [first, *got_first], 8, after=first_base
        )
        while step < steps:
            advance()
        (mixed,) = call(mixed_kernel, [part_bf], [noise_rows, sent, *got], 0.2, after=first_resp)
        got_mixed = send_up(mixed)
        (fixed_out,) = call(
            fixed_kernel, [shape_of((fixed_rows, width), F32)], [tip_inverse, mixed], 8
        )
        (sample,) = call(
            lambda a, b, c, d, *refs: final_kernel((a, b), (c, d), *refs),
            [shape_of((2, rows, columns), BF)],
            [first_base, last_base, first_resp, last_resp, mixed, *got_mixed],
            8,
            {("out", 0): pl.ANY},
            [
                pltpu.VMEM((columns, fixed_rows), BF),
                pltpu.VMEM((2, rows, columns), BF),
                dma((2, tiles)),
            ],
            after=fixed_out,
            after_place=pltpu.HBM,
        )
        return (sample, fixed_out)

    return on_device


def solution(mesh):
    sizes = dict(mesh.shape)

    def program(diag_inverse, coupling, arrow, tip_inverse, noise, noise_fixed, section_lengths):
        device = build(
            sizes["tm"],
            sizes["space"],
            diag_inverse.shape[1] // sizes["space"],
            noise.shape[2],
            arrow.shape[1],
        )
        return jax.shard_map(
            device,
            mesh=mesh,
            in_specs=(
                P("tm", "space", None),
                P("tm", "space", None),
                P("tm", None, "space"),
                P(),
                P("tm", "space", None),
                P(None, "space"),
                P(),
            ),
            out_specs=(P("tm", "space", None), P(None, "space")),
            check_vma=False,
        )(diag_inverse, coupling, arrow, tip_inverse, noise, noise_fixed, section_lengths)

    return program
```

```python
import jax
import jax.numpy as jnp
from jax import lax
from jax.experimental import pallas as pl
from jax.experimental.pallas import tpu as pltpu
from jax.sharding import PartitionSpec as P

BF = jnp.bfloat16
F32 = jnp.float32
MIB = 1 << 20


def dot(left, right):
    return jnp.dot(left, right, preferred_element_type=F32)


def dot_last(left, right):
    return lax.dot_general(left, right, (((1,), (1,)), ((), ())), preferred_element_type=F32)


def rounded(value):
    return value.astype(BF).astype(F32)


def total_of(own_ref, got_refs):
    total = rounded(own_ref[...])
    for got in got_refs:
        total = total + got[...].astype(F32)
    return total


def shape_of(shape, dtype):
    return jax.ShapeDtypeStruct(shape, dtype)


def build(n_tm, n_space, rows, columns, fixed_rows):
    nodes = n_space * rows
    tile = 256 if rows % 256 == 0 else rows
    tiles = rows // tile
    wide = 2 * tile if rows % (2 * tile) == 0 else tile
    eighth = rows // 8
    head = rows - eighth
    width = columns // n_space
    peers = range(1, n_space)

    def at_core():
        return lax.axis_index("space")

    def block(step, offset=0, size=rows):
        owner = lax.rem(at_core() - step + n_space, n_space)
        return pl.ds(pl.multiple_of(owner * rows + offset, tile), size)

    def part_rows(step):
        owner = lax.rem(at_core() - step + n_space, n_space)
        return pl.ds(pl.multiple_of(owner * width, width), width)

    def call(body, outs, args, cover, places=None, scratch=(), after=None, aliases=None, after_place=pl.ANY):
        places = dict(places or {})
        args = list(args)
        count = len(args)
        if after is not None:
            args.append(after)
            places[count] = after_place

        def run(*refs):
            body(*refs[:count], *refs[len(args) :])

        specs = [pl.BlockSpec(memory_space=places.get(i, pltpu.VMEM)) for i in range(len(args))]
        args = [
            pltpu.with_memory_space_constraint(a, pltpu.HBM)
            if places.get(i) is pltpu.HBM
            else a
            for i, a in enumerate(args)
        ]
        return pl.pallas_call(
            run,
            in_specs=specs,
            out_specs=[
                pl.BlockSpec(memory_space=places.get(("out", i), pltpu.VMEM))
                for i in range(len(outs))
            ],
            out_shape=outs,
            scratch_shapes=list(scratch),
            input_output_aliases=aliases or {},
            cost_estimate=pl.CostEstimate(
                flops=int(cover * 1e9), bytes_accessed=0, transcendentals=0
            ),
            compiler_params=pltpu.CompilerParams(vmem_limit_bytes=16 * MIB),
        )(*args)

    def lower_rows(left, factor, own_ref, other_ref):
        for step in peers:

            @pl.when(at_core() >= step)
            def _():
                other_ref[step - 1] = dot(left[...], factor[:, block(step)]).astype(BF)

            @pl.when(at_core() < step)
            def _():
                other_ref[step - 1] = jnp.zeros_like(other_ref[step - 1])

        for at in range(0, rows, wide):
            own_ref[:, at : at + wide] = dot(left[:, at:], factor[at:, block(0, at, wide)])

    def full_rows(left, factor, own_ref, other_ref):
        for step in peers:
            other_ref[step - 1] = dot(left[...], factor[:, block(step)]).astype(BF)
        own_ref[...] = dot(left[...], factor[:, block(0)])

    def lower_own(factor, right, out_ref, wait=None):
        for i in range(tiles):
            at = i * tile
            if wait:
                wait(i)
            out_ref[at : at + tile] = dot(
                factor[at : at + tile, block(0, 0, at + tile)], right[: at + tile]
            )

    def lower_rest(factor, got, value):
        for step in peers:

            @pl.when(at_core() >= step)
            def _():
                value[...] = value[...] + dot(factor[:, block(step)], got[step - 1][...])

    def start_kernel(
        diag, arrow, noise, lengths,
        d0, d1, own, other, n0, mask,
        e1, live_scratch, sem1, sem0, sems,
    ):
        arrow_copy = pltpu.make_async_copy(arrow.at[1], e1, sems.at[0])
        noise_copy = pltpu.make_async_copy(noise.at[0], n0, sems.at[1])
        live_copy = pltpu.make_async_copy(lengths, live_scratch, sems.at[2])

        def lower_copies(slot, target, sem):
            copies = {}
            for step in range(n_space):
                for i in range(tiles):
                    at = i * tile
                    size = rows if step else at + tile
                    part = (pl.ds(at, tile), block(step, 0, size))
                    copies[step, i] = pltpu.make_async_copy(
                        diag.at[(slot, *part)], target.at[part], sem.at[step, i]
                    )
            return copies

        def each(copies, i, act):
            act(copies[0, i])
            for step in peers:

                @pl.when(at_core() >= step)
                def _():
                    act(copies[step, i])

        copies1 = lower_copies(1, d1, sem1)
        copies0 = lower_copies(0, d0, sem0)
        live_copy.start()
        arrow_copy.start()
        for i in range(tiles):
            each(copies1, i, lambda copy: copy.start(priority=i % 2))
        for factor in (d0, d1):
            for at in range(0, rows, wide):
                for inner in range(at + tile, at + wide, tile):
                    part = (pl.ds(at, inner - at), block(0, inner, tile))
                    factor[part] = jnp.zeros((inner - at, tile), BF)
        live_copy.wait()
        arrow_copy.wait()
        live = live_scratch[lax.axis_index("tm")] > 1
        mask[...] = jnp.where(live, jnp.ones_like(mask[...]), jnp.zeros_like(mask[...]))
        e1[...] = jnp.where(live, e1[...], jnp.zeros_like(e1[...]))
        for i in range(tiles):
            each(copies1, i, lambda copy: copy.wait())
            each(copies0, i, lambda copy: copy.start(priority=i % 2))
        noise_copy.start()
        lower_rows(e1, d1, own, other)
        for i in range(tiles):
            each(copies0, i, lambda copy: copy.wait())
        noise_copy.wait()

    def k1_copies(coupling, k1, first, count, sems, split=2):
        copies = []
        size = max(eighth // split, 16)
        for i in range(count * eighth // size):
            part = pl.ds(first * eighth + i * size, size)
            target = k1.at[part] if k1.shape[0] == rows else k1.at[pl.ds(i * size, size)]
            copies.append(pltpu.make_async_copy(coupling.at[1, part], target, sems.at[i]))
            copies[-1].start(priority=i % 2)
        return copies

    def first_value_kernel(d0, n0, coupling, noise, *refs):
        got, (out, bar, k1, n1, sems) = refs[: n_space - 1], refs[n_space - 1 :]
        copies = k1_copies(coupling, k1, 0, 3, sems)
        copies.append(pltpu.make_async_copy(noise.at[1], n1, sems.at[6]))
        copies[-1].start()
        lower_own(d0, n0, out)
        lower_rest(d0, [piece.at[0] for piece in got], out)
        bar[...] = out[...].astype(BF)
        for copy in copies:
            copy.wait()

    def load_kernel(coupling, value, _, value_rows, k1, sems):
        copies = k1_copies(coupling, k1, 3, 4, sems)
        value_rows[...] = value[...].T
        for copy in copies:
            copy.wait()

    def target_kernel(k1, coupling, bar, n1, arrow, own, *refs):
        got, refs = refs[: n_space - 1], refs[n_space - 1 :]
        got_own, refs = refs[: n_space - 1], refs[n_space - 1 :]
        target, part_own, part_other, response, e0, tail, whole, sems = refs
        arrow_copy = pltpu.make_async_copy(arrow.at[0], e0, sems.at[2])
        tail_copies = k1_copies(coupling, tail, 7, 1, sems)
        arrow_copy.start()

        def pull(at, size):
            factor = tail if at == head else k1.at[at : at + size]
            pulled = jnp.zeros((size, columns), F32)
            for step, piece in enumerate([bar, *got]):
                pulled = pulled + dot(factor[:, block(step)], piece[...])
            target[at : at + size] = (n1[at : at + size].astype(F32) - pulled).astype(BF)

        response[...] = total_of(own, got_own).astype(BF)
        for at in range(0, head, tile):
            pull(at, min(tile, head - at))
        arrow_copy.wait()
        whole[...] = dot(e0[...], bar[...])
        for copy in tail_copies:
            copy.wait()
        pull(head, eighth)
        whole[...] = (whole[...] + dot(response[...], target[...])).T
        part_own[...] = whole[part_rows(0)]
        for step in peers:
            part_other[step - 1] = whole[part_rows(step)].astype(BF)

    def last_own_kernel(d1, target, coupling, _, value, k1, sems):
        copies = k1_copies(coupling, k1, 7, 1, sems, 4)
        lower_own(d1, target, value)
        for copy in copies:
            copy.wait()

    def core_sum_kernel(part, _, *refs):
        got, (out, _) = refs[:-2], refs[-2:]
        total = part[...]
        for piece in got:
            total = total + piece[...].astype(F32)
        out[...] = total.astype(BF)

    def fold_kernel(sent, got, out):
        out[...] = (sent[...].astype(F32) + got[...].astype(F32)).astype(BF)

    def last_solve_kernel(d1, first, *refs):
        got, (own, other, value) = refs[: n_space - 1], refs[n_space - 1 :]
        value[...] = first[...]
        lower_rest(d1, got, value)
        lower_rows(value[...].astype(BF).T, d1, own, other)

    def response_kernel(k1, response, own, other):
        full_rows(response, k1, own, other)

    def pass_kernel(k1, mask, solved, *refs):
        got, (base, own, other) = refs[: n_space - 1], refs[n_space - 1 :]
        value = jnp.where(mask[:1, :1] > 0, total_of(solved, got), 0.0)
        base[...] = value
        full_rows(value.astype(BF), k1, own, other)

    def first_response_kernel(d0, e0, tip, pushed, *refs):
        got, (own, other) = refs[: n_space - 1], refs[n_space - 1 :]
        left = (e0[...].astype(F32) - total_of(pushed, got)).astype(BF)
        lower_rows(through_tip(tip[...], left).astype(BF), d0, own, other)

    def first_solve_kernel(d0, value_rows, passed, *refs):
        got, (own, other) = refs[: n_space - 1], refs[n_space - 1 :]
        left = (value_rows[...] - total_of(passed, got)).astype(BF)
        lower_rows(left, d0, own, other)

    def through_tip(tip, right):
        inner = dot(tip, right).astype(BF)
        return dot(tip.astype(F32).T.astype(BF), inner)

    def turn_last_kernel(base, response, noise_fixed, tip, last_base, last_resp, noise_rows):
        noise_rows[...] = noise_fixed[...].T
        last_base[...] = base[...].T
        last_resp[...] = through_tip(tip[...], response[...]).T.astype(BF)

    def turn_response_kernel(first, *refs):
        got, out = refs[:-1], refs[-1]
        out[...] = total_of(first, got).T.astype(BF)

    def turn_first_kernel(solved, *refs):
        got, out = refs[:-1], refs[-1]
        out[...] = total_of(solved, got).T

    def mixed_kernel(noise_rows, *refs):
        terms, out = refs[:-1], refs[-1]
        total = terms[0][...].astype(F32)
        for piece in terms[1:]:
            total = total + piece[...].astype(F32)
        out[...] = (noise_rows[...] - total).astype(BF)

    def final_kernel(bases, responses, mixed, *refs):
        got, (out, whole, result, sems) = refs[: n_space - 1], refs[n_space - 1 :]
        for step, piece in enumerate([mixed, *got]):
            whole[part_rows(step)] = piece[...]
        copies = []
        for slot in range(2):
            for i in range(tiles):
                at = i * tile
                part = (slot, pl.ds(at, tile))
                update = dot_last(responses[slot][at : at + tile], whole[...])
                result[part] = (bases[slot][at : at + tile] - update).astype(BF)
                copies.append(
                    pltpu.make_async_copy(result.at[part], out.at[part], sems.at[slot, i])
                )
                copies[-1].start()
        for copy in copies:
            copy.wait()

    def fixed_kernel(tip, mixed, out):
        forward = dot_last(mixed[...], tip[...])
        out[...] = dot(forward.astype(BF), tip[...]).T

    def swap(value, step):
        pairs = [(i, (i - step) % n_space) for i in range(n_space)]
        return lax.ppermute(value, "space", pairs)

    def send_up(value):
        return [swap(value, -step) for step in peers]

    def send_down(values):
        return [swap(values[step - 1], step) for step in peers]

    steps = n_tm.bit_length() - 1
    assert n_tm == 1 << steps

    def swap_step(value, step):
        pairs = []
        for i in range(n_tm):
            for core in range(n_space):
                bit = 1 << step
                if step < steps - 1:
                    bit = 1 << (step + core * (steps - 1) // n_space) % (steps - 1)
                pairs.append((i * n_space + core, (i ^ bit) * n_space + core))
        return lax.ppermute(value, ("tm", "space"), pairs)

    node_f32, node_bf = shape_of((rows, columns), F32), shape_of((rows, columns), BF)
    flat_f32 = shape_of((columns, rows), F32)
    flat_others = shape_of((n_space - 1, columns, rows), BF)
    fixed_f32 = shape_of((fixed_rows, rows), F32)
    fixed_bf = shape_of((fixed_rows, rows), BF)
    fixed_others = shape_of((n_space - 1, fixed_rows, rows), BF)
    part_bf = shape_of((width, fixed_rows), BF)
    by_node = shape_of((rows, fixed_rows), BF)
    in_vmem = pltpu.VMEM((rows, nodes), BF)
    dma = pltpu.SemaphoreType.DMA

    def fold(sent, got, after):
        size = width * fixed_rows
        return call(fold_kernel, [part_bf], [sent, got], size, 6 * size, after=after)[0]

    def on_device(diag_inverse, coupling, arrow, tip_inverse, noise, noise_fixed, section_lengths):
        got_noise = send_up(noise)
        d0, d1, own, other, n0, mask = call(
            start_kernel,
            [in_vmem, in_vmem, fixed_f32, fixed_others, node_bf, shape_of((8, 128), F32)],
            [diag_inverse, arrow, noise, section_lengths],
            8,
            {i: pltpu.HBM for i in range(4)},
            [
                pltpu.VMEM((fixed_rows, rows), BF),
                pltpu.SMEM(section_lengths.shape, jnp.int32),
                dma((n_space, tiles)),
                dma((n_space, tiles)),
                dma((3,)),
            ],
        )
        got_response = send_down(other)
        value, bar, k1, n1 = call(
            first_value_kernel,
            [node_f32, node_bf, in_vmem, node_bf],
            [d0, n0, coupling, noise, *got_noise],
            8,
            {2: pltpu.HBM, 3: pltpu.HBM},
            [dma((7,))],
        )
        got_bar = send_up(bar)
        value_rows, k1 = call(
            load_kernel,
            [flat_f32, in_vmem],
            [coupling, value, k1],
            8,
            {0: pltpu.HBM, 2: pl.ANY, ("out", 1): pl.ANY},
            [dma((8,))],
            aliases={2: 1},
        )
        target, part_own, part_other, response, e0 = call(
            target_kernel,
            [
                node_bf,
                shape_of((width, fixed_rows), F32),
                shape_of((n_space - 1, width, fixed_rows), BF),
                fixed_bf,
                fixed_bf,
            ],
            [k1, coupling, bar, n1, arrow, own, *got_bar, *got_response],
            8,
            {1: pltpu.HBM, 4: pltpu.HBM},
            [
                pltpu.VMEM((eighth, nodes), BF),
                pltpu.VMEM((columns, fixed_rows), F32),
                dma((3,)),
            ],
        )
        got_parts = send_down(part_other)
        value, k1 = call(
            last_own_kernel,
            [node_f32, in_vmem],
            [d1, target, coupling, k1],
            8,
            {2: pltpu.HBM, 3: pl.ANY, ("out", 1): pl.ANY},
            [dma((4,))],
            aliases={3: 1},
        )
        sent, target = call(
            core_sum_kernel,
            [part_bf, node_bf],
            [part_own, target, *got_parts],
            0.2,
            {1: pl.ANY, ("out", 1): pl.ANY},
            aliases={1: 1},
            after=value,
        )
        got_target = send_up(target)
        step = 0
        got = []

        def advance(after=None):
            nonlocal sent, got, step
            if step == steps:
                return
            if step:
                (sent,) = call(fold_kernel, [part_bf], [sent, *got], 0.2, after=after)
            got = [swap_step(sent, step)]
            step += 1

        advance()
        solved, other = call(
            last_solve_kernel,
            [flat_f32, flat_others],
            [d1, value, *got_target],
            8,
            scratch=[pltpu.VMEM((rows, columns), F32)],
            after=sent,
        )
        got_solved = send_down(other)
        advance(solved)
        pushed, other = call(
            response_kernel, [fixed_f32, fixed_others], [k1, response], 5, after=sent
        )
        got_pushed = send_down(other)
        base, passed, other = call(
            pass_kernel,
            [flat_f32, flat_f32, flat_others],
            [k1, mask, solved, *got_solved],
            8,
            after=pushed,
        )
        got_passed = send_down(other)
        advance(base)
        last_base, last_resp, noise_rows = call(
            turn_last_kernel,
            [node_f32, by_node, shape_of((width, fixed_rows), F32)],
            [base, response, noise_fixed, tip_inverse],
            5,
            after=sent,
        )
        solved, other = call(
            first_solve_kernel,
            [flat_f32, flat_others],
            [d0, value_rows, passed, *got_passed],
            8,
            after=noise_rows,
        )
        got_solved = send_down(other)
        advance(solved)
        first, other = call(
            first_response_kernel,
            [fixed_f32, fixed_others],
            [d0, e0, tip_inverse, pushed, *got_pushed],
            5,
            after=sent,
        )
        got_first = send_down(other)
        (first_base,) = call(turn_first_kernel, [node_f32], [solved, *got_solved], 8, after=first)
        (first_resp,) = call(
            turn_response_kernel, [by_node], [first, *got_first], 8, after=first_base
        )
        while step < steps:
            advance()
        (mixed,) = call(mixed_kernel, [part_bf], [noise_rows, sent, *got], 0.2, after=first_resp)
        got_mixed = send_up(mixed)
        (fixed_out,) = call(
            fixed_kernel, [shape_of((fixed_rows, width), F32)], [tip_inverse, mixed], 8
        )
        (sample,) = call(
            lambda a, b, c, d, *refs: final_kernel((a, b), (c, d), *refs),
            [shape_of((2, rows, columns), BF)],
            [first_base, last_base, first_resp, last_resp, mixed, *got_mixed],
            8,
            {("out", 0): pl.ANY},
            [
                pltpu.VMEM((columns, fixed_rows), BF),
                pltpu.VMEM((2, rows, columns), BF),
                dma((2, tiles)),
            ],
            after=fixed_out,
            after_place=pltpu.HBM,
        )
        return (sample, fixed_out)

    return on_device


def solution(mesh):
    sizes = dict(mesh.shape)

    def program(diag_inverse, coupling, arrow, tip_inverse, noise, noise_fixed, section_lengths):
        device = build(
            sizes["tm"],
            sizes["space"],
            diag_inverse.shape[1] // sizes["space"],
            noise.shape[2],
            arrow.shape[1],
        )
        return jax.shard_map(
            device,
            mesh=mesh,
            in_specs=(
                P("tm", "space", None),
                P("tm", "space", None),
                P("tm", None, "space"),
                P(),
                P("tm", "space", None),
                P(None, "space"),
                P(),
            ),
            out_specs=(P("tm", "space", None), P(None, "space")),
            check_vma=False,
        )(diag_inverse, coupling, arrow, tip_inverse, noise, noise_fixed, section_lengths)

    return program
```

```python
import jax
import jax.numpy as jnp
from jax import lax
from jax.experimental import pallas as pl
from jax.experimental.pallas import tpu as pltpu
from jax.sharding import PartitionSpec as P

BF = jnp.bfloat16
F32 = jnp.float32
MIB = 1 << 20


def dot(left, right):
    return jnp.dot(left, right, preferred_element_type=F32)


def dot_last(left, right):
    return lax.dot_general(left, right, (((1,), (1,)), ((), ())), preferred_element_type=F32)


def rounded(value):
    return value.astype(BF).astype(F32)


def total_of(own_ref, got_refs):
    total = rounded(own_ref[...])
    for got in got_refs:
        total = total + got[...].astype(F32)
    return total


def shape_of(shape, dtype):
    return jax.ShapeDtypeStruct(shape, dtype)


def build(n_tm, n_space, rows, columns, fixed_rows):
    nodes = n_space * rows
    tile = 256 if rows % 256 == 0 else rows
    tiles = rows // tile
    quarter = rows // 4
    head = rows - quarter
    width = columns // n_space
    peers = range(1, n_space)

    def at_core():
        return lax.axis_index("space")

    def block(step, offset=0, size=rows):
        owner = lax.rem(at_core() - step + n_space, n_space)
        return pl.ds(pl.multiple_of(owner * rows + offset, tile), size)

    def part_rows(step):
        owner = lax.rem(at_core() - step + n_space, n_space)
        return pl.ds(pl.multiple_of(owner * width, width), width)

    def call(body, outs, args, cover, places=None, scratch=(), after=None, aliases=None, after_place=pl.ANY):
        places = dict(places or {})
        args = list(args)
        count = len(args)
        if after is not None:
            args.append(after)
            places[count] = after_place

        def run(*refs):
            body(*refs[:count], *refs[len(args) :])

        specs = [pl.BlockSpec(memory_space=places.get(i, pltpu.VMEM)) for i in range(len(args))]
        args = [
            pltpu.with_memory_space_constraint(a, pltpu.HBM)
            if places.get(i) is pltpu.HBM
            else a
            for i, a in enumerate(args)
        ]
        return pl.pallas_call(
            run,
            in_specs=specs,
            out_specs=[
                pl.BlockSpec(memory_space=places.get(("out", i), pltpu.VMEM))
                for i in range(len(outs))
            ],
            out_shape=outs,
            scratch_shapes=list(scratch),
            input_output_aliases=aliases or {},
            cost_estimate=pl.CostEstimate(
                flops=int(cover * 1e9), bytes_accessed=0, transcendentals=0
            ),
            compiler_params=pltpu.CompilerParams(vmem_limit_bytes=16 * MIB),
        )(*args)

    def lower_rows(left, factor, own_ref, other_ref):
        for step in peers:

            @pl.when(at_core() >= step)
            def _():
                other_ref[step - 1] = dot(left[...], factor[:, block(step)]).astype(BF)

            @pl.when(at_core() < step)
            def _():
                other_ref[step - 1] = jnp.zeros_like(other_ref[step - 1])

        for j in range(tiles):
            at = j * tile
            own_ref[:, at : at + tile] = dot(left[:, at:], factor[at:, block(0, at, tile)])

    def full_rows(left, factor, own_ref, other_ref):
        for step in peers:
            other_ref[step - 1] = dot(left[...], factor[:, block(step)]).astype(BF)
        own_ref[...] = dot(left[...], factor[:, block(0)])

    def lower_own(factor, right, out_ref, wait=None):
        for i in range(tiles):
            at = i * tile
            if wait:
                wait(i)
            out_ref[at : at + tile] = dot(
                factor[at : at + tile, block(0, 0, at + tile)], right[: at + tile]
            )

    def lower_rest(factor, got, value):
        for step in peers:

            @pl.when(at_core() >= step)
            def _():
                value[...] = value[...] + dot(factor[:, block(step)], got[step - 1][...])

    def start_kernel(
        diag, arrow, noise, lengths,
        d0, d1, own, other, n0, mask,
        e1, live_scratch, sem1, sem0, sems,
    ):
        arrow_copy = pltpu.make_async_copy(arrow.at[1], e1, sems.at[0])
        noise_copy = pltpu.make_async_copy(noise.at[0], n0, sems.at[1])
        live_copy = pltpu.make_async_copy(lengths, live_scratch, sems.at[2])

        def lower_copies(slot, target, sem):
            copies = {}
            for step in range(n_space):
                for i in range(tiles):
                    at = i * tile
                    size = rows if step else at + tile
                    part = (pl.ds(at, tile), block(step, 0, size))
                    copies[step, i] = pltpu.make_async_copy(
                        diag.at[(slot, *part)], target.at[part], sem.at[step, i]
                    )
            return copies

        def each(copies, i, act):
            act(copies[0, i])
            for step in peers:

                @pl.when(at_core() >= step)
                def _():
                    act(copies[step, i])

        copies1 = lower_copies(1, d1, sem1)
        copies0 = lower_copies(0, d0, sem0)
        live_copy.start()
        arrow_copy.start()
        for i in range(tiles):
            each(copies1, i, lambda copy: copy.start(priority=i % 2))
        live_copy.wait()
        arrow_copy.wait()
        live = live_scratch[lax.axis_index("tm")] > 1
        mask[...] = jnp.where(live, jnp.ones_like(mask[...]), jnp.zeros_like(mask[...]))
        e1[...] = jnp.where(live, e1[...], jnp.zeros_like(e1[...]))
        for i in range(tiles):
            each(copies1, i, lambda copy: copy.wait())
            each(copies0, i, lambda copy: copy.start(priority=i % 2))
        noise_copy.start()
        lower_rows(e1, d1, own, other)
        for i in range(tiles):
            each(copies0, i, lambda copy: copy.wait())
        noise_copy.wait()

    def k1_copies(coupling, k1, first, count, sems):
        copies = []
        size = quarter // 2
        for i in range(2 * count):
            part = pl.ds(first * quarter + i * size, size)
            target = k1.at[part] if k1.shape[0] == rows else k1.at[pl.ds(i * size, size)]
            copies.append(pltpu.make_async_copy(coupling.at[1, part], target, sems.at[i]))
            copies[-1].start(priority=i % 2)
        return copies

    def first_value_kernel(d0, n0, coupling, noise, *refs):
        got, (out, bar, k1, n1, sems) = refs[: n_space - 1], refs[n_space - 1 :]
        copies = k1_copies(coupling, k1, 0, 1, sems)
        copies.append(pltpu.make_async_copy(noise.at[1], n1, sems.at[2]))
        copies[-1].start()
        lower_own(d0, n0, out)
        lower_rest(d0, [piece.at[0] for piece in got], out)
        bar[...] = out[...].astype(BF)
        for copy in copies:
            copy.wait()

    def load_kernel(coupling, value, _, value_rows, k1, sems):
        copies = k1_copies(coupling, k1, 1, 2, sems)
        value_rows[...] = value[...].T
        for copy in copies:
            copy.wait()

    def target_kernel(k1, coupling, bar, n1, arrow, own, *refs):
        got, refs = refs[: n_space - 1], refs[n_space - 1 :]
        got_own, refs = refs[: n_space - 1], refs[n_space - 1 :]
        target, part_own, part_other, response, e0, tail, whole, sems = refs
        arrow_copy = pltpu.make_async_copy(arrow.at[0], e0, sems.at[2])
        tail_copies = k1_copies(coupling, tail, 3, 1, sems)
        arrow_copy.start()

        def pull(at, size):
            factor = tail if at == head else k1.at[at : at + size]
            pulled = jnp.zeros((size, columns), F32)
            for step, piece in enumerate([bar, *got]):
                pulled = pulled + dot(factor[:, block(step)], piece[...])
            target[at : at + size] = (n1[at : at + size].astype(F32) - pulled).astype(BF)

        response[...] = total_of(own, got_own).astype(BF)
        for at in range(0, head, tile):
            pull(at, min(tile, head - at))
        arrow_copy.wait()
        whole[...] = dot(e0[...], bar[...])
        for copy in tail_copies:
            copy.wait()
        pull(head, quarter)
        whole[...] = (whole[...] + dot(response[...], target[...])).T
        part_own[...] = whole[part_rows(0)]
        for step in peers:
            part_other[step - 1] = whole[part_rows(step)].astype(BF)

    def last_own_kernel(d1, target, value):
        lower_own(d1, target, value)

    def core_sum_kernel(part, _, *refs):
        got, (out, _) = refs[:-2], refs[-2:]
        total = part[...]
        for piece in got:
            total = total + piece[...].astype(F32)
        out[...] = total.astype(BF)

    def fold_kernel(sent, got, out):
        out[...] = (sent[...].astype(F32) + got[...].astype(F32)).astype(BF)

    def last_solve_kernel(d1, first, coupling, _, *refs):
        got, (own, other, k1, value, sems) = refs[: n_space - 1], refs[n_space - 1 :]
        copies = k1_copies(coupling, k1, 3, 1, sems)
        value[...] = first[...]
        lower_rest(d1, got, value)
        lower_rows(value[...].astype(BF).T, d1, own, other)
        for copy in copies:
            copy.wait()

    def response_kernel(k1, response, own, other):
        full_rows(response, k1, own, other)

    def pass_kernel(k1, mask, solved, *refs):
        got, (base, own, other) = refs[: n_space - 1], refs[n_space - 1 :]
        value = jnp.where(mask[:1, :1] > 0, total_of(solved, got), 0.0)
        base[...] = value
        full_rows(value.astype(BF), k1, own, other)

    def first_response_kernel(d0, e0, tip, pushed, *refs):
        got, (own, other) = refs[: n_space - 1], refs[n_space - 1 :]
        left = (e0[...].astype(F32) - total_of(pushed, got)).astype(BF)
        lower_rows(through_tip(tip[...], left).astype(BF), d0, own, other)

    def first_solve_kernel(d0, value_rows, passed, *refs):
        got, (own, other) = refs[: n_space - 1], refs[n_space - 1 :]
        left = (value_rows[...] - total_of(passed, got)).astype(BF)
        lower_rows(left, d0, own, other)

    def through_tip(tip, right):
        inner = dot(tip, right).astype(BF)
        return dot(tip.astype(F32).T.astype(BF), inner)

    def turn_last_kernel(base, response, noise_fixed, tip, last_base, last_resp, noise_rows):
        noise_rows[...] = noise_fixed[...].T
        last_base[...] = base[...].T
        last_resp[...] = through_tip(tip[...], response[...]).T.astype(BF)

    def turn_response_kernel(first, *refs):
        got, out = refs[:-1], refs[-1]
        out[...] = total_of(first, got).T.astype(BF)

    def turn_first_kernel(solved, *refs):
        got, out = refs[:-1], refs[-1]
        out[...] = total_of(solved, got).T

    def mixed_kernel(noise_rows, *refs):
        terms, out = refs[:-1], refs[-1]
        total = terms[0][...].astype(F32)
        for piece in terms[1:]:
            total = total + piece[...].astype(F32)
        out[...] = (noise_rows[...] - total).astype(BF)

    def final_kernel(bases, responses, mixed, *refs):
        got, (out, whole, result, sems) = refs[: n_space - 1], refs[n_space - 1 :]
        for step, piece in enumerate([mixed, *got]):
            whole[part_rows(step)] = piece[...]
        copies = []
        for slot in range(2):
            for i in range(tiles):
                at = i * tile
                part = (slot, pl.ds(at, tile))
                update = dot_last(responses[slot][at : at + tile], whole[...])
                result[part] = (bases[slot][at : at + tile] - update).astype(BF)
                copies.append(
                    pltpu.make_async_copy(result.at[part], out.at[part], sems.at[slot, i])
                )
                copies[-1].start()
        for copy in copies:
            copy.wait()

    def fixed_kernel(tip, mixed, out):
        forward = dot_last(mixed[...], tip[...])
        out[...] = dot(forward.astype(BF), tip[...]).T

    def swap(value, step):
        pairs = [(i, (i - step) % n_space) for i in range(n_space)]
        return lax.ppermute(value, "space", pairs)

    def send_up(value):
        return [swap(value, -step) for step in peers]

    def send_down(values):
        return [swap(values[step - 1], step) for step in peers]

    steps = n_tm.bit_length() - 1
    assert n_tm == 1 << steps

    def swap_step(value, step):
        pairs = []
        for i in range(n_tm):
            for core in range(n_space):
                bit = 1 << (step + core * steps // n_space) % steps
                pairs.append((i * n_space + core, (i ^ bit) * n_space + core))
        return lax.ppermute(value, ("tm", "space"), pairs)

    node_f32, node_bf = shape_of((rows, columns), F32), shape_of((rows, columns), BF)
    flat_f32 = shape_of((columns, rows), F32)
    flat_others = shape_of((n_space - 1, columns, rows), BF)
    fixed_f32 = shape_of((fixed_rows, rows), F32)
    fixed_bf = shape_of((fixed_rows, rows), BF)
    fixed_others = shape_of((n_space - 1, fixed_rows, rows), BF)
    part_bf = shape_of((width, fixed_rows), BF)
    by_node = shape_of((rows, fixed_rows), BF)
    in_vmem = pltpu.VMEM((rows, nodes), BF)
    dma = pltpu.SemaphoreType.DMA

    def fold(sent, got, after):
        size = width * fixed_rows
        return call(fold_kernel, [part_bf], [sent, got], size, 6 * size, after=after)[0]

    def on_device(diag_inverse, coupling, arrow, tip_inverse, noise, noise_fixed, section_lengths):
        got_noise = send_up(noise)
        d0, d1, own, other, n0, mask = call(
            start_kernel,
            [in_vmem, in_vmem, fixed_f32, fixed_others, node_bf, shape_of((8, 128), F32)],
            [diag_inverse, arrow, noise, section_lengths],
            8,
            {i: pltpu.HBM for i in range(4)},
            [
                pltpu.VMEM((fixed_rows, rows), BF),
                pltpu.SMEM(section_lengths.shape, jnp.int32),
                dma((n_space, tiles)),
                dma((n_space, tiles)),
                dma((3,)),
            ],
        )
        got_response = send_down(other)
        value, bar, k1, n1 = call(
            first_value_kernel,
            [node_f32, node_bf, in_vmem, node_bf],
            [d0, n0, coupling, noise, *got_noise],
            8,
            {2: pltpu.HBM, 3: pltpu.HBM},
            [dma((3,))],
        )
        got_bar = send_up(bar)
        value_rows, k1 = call(
            load_kernel,
            [flat_f32, in_vmem],
            [coupling, value, k1],
            8,
            {0: pltpu.HBM, 2: pl.ANY, ("out", 1): pl.ANY},
            [dma((4,))],
            aliases={2: 1},
        )
        target, part_own, part_other, response, e0 = call(
            target_kernel,
            [
                node_bf,
                shape_of((width, fixed_rows), F32),
                shape_of((n_space - 1, width, fixed_rows), BF),
                fixed_bf,
                fixed_bf,
            ],
            [k1, coupling, bar, n1, arrow, own, *got_bar, *got_response],
            8,
            {1: pltpu.HBM, 4: pltpu.HBM},
            [
                pltpu.VMEM((quarter, nodes), BF),
                pltpu.VMEM((columns, fixed_rows), F32),
                dma((3,)),
            ],
        )
        got_parts = send_down(part_other)
        (value,) = call(last_own_kernel, [node_f32], [d1, target], 8)
        sent, target = call(
            core_sum_kernel,
            [part_bf, node_bf],
            [part_own, target, *got_parts],
            0.2,
            {1: pl.ANY, ("out", 1): pl.ANY},
            aliases={1: 1},
            after=value,
        )
        got_target = send_up(target)
        step = 0
        got = []

        def advance(after=None):
            nonlocal sent, got, step
            if step == steps:
                return
            if step:
                (sent,) = call(fold_kernel, [part_bf], [sent, *got], 0.2, after=after)
            got = [swap_step(sent, step)]
            step += 1

        advance()
        solved, other, k1 = call(
            last_solve_kernel,
            [flat_f32, flat_others, in_vmem],
            [d1, value, coupling, k1, *got_target],
            8,
            {2: pltpu.HBM, 3: pl.ANY, ("out", 2): pl.ANY},
            [pltpu.VMEM((rows, columns), F32), dma((2,))],
            aliases={3: 2},
            after=sent,
        )
        got_solved = send_down(other)
        advance(solved)
        pushed, other = call(
            response_kernel, [fixed_f32, fixed_others], [k1, response], 5, after=sent
        )
        got_pushed = send_down(other)
        base, passed, other = call(
            pass_kernel,
            [flat_f32, flat_f32, flat_others],
            [k1, mask, solved, *got_solved],
            8,
            after=pushed,
        )
        got_passed = send_down(other)
        advance(base)
        first, other = call(
            first_response_kernel,
            [fixed_f32, fixed_others],
            [d0, e0, tip_inverse, pushed, *got_pushed],
            5,
            after=sent,
        )
        got_first = send_down(other)
        solved, other = call(
            first_solve_kernel,
            [flat_f32, flat_others],
            [d0, value_rows, passed, *got_passed],
            8,
            after=first,
        )
        got_solved = send_down(other)
        advance(solved)
        last_base, last_resp, noise_rows = call(
            turn_last_kernel,
            [node_f32, by_node, shape_of((width, fixed_rows), F32)],
            [base, response, noise_fixed, tip_inverse],
            5,
            after=sent,
        )
        (first_resp,) = call(turn_response_kernel, [by_node], [first, *got_first], 8, after=noise_rows)
        (first_base,) = call(
            turn_first_kernel, [node_f32], [solved, *got_solved], 8, after=first_resp
        )
        while step < steps:
            advance()
        (mixed,) = call(mixed_kernel, [part_bf], [noise_rows, sent, *got], 0.2, after=first_base)
        got_mixed = send_up(mixed)
        (fixed_out,) = call(
            fixed_kernel, [shape_of((fixed_rows, width), F32)], [tip_inverse, mixed], 8
        )
        (sample,) = call(
            lambda a, b, c, d, *refs: final_kernel((a, b), (c, d), *refs),
            [shape_of((2, rows, columns), BF)],
            [first_base, last_base, first_resp, last_resp, mixed, *got_mixed],
            8,
            {("out", 0): pl.ANY},
            [
                pltpu.VMEM((columns, fixed_rows), BF),
                pltpu.VMEM((2, rows, columns), BF),
                dma((2, tiles)),
            ],
            after=fixed_out,
            after_place=pltpu.HBM,
        )
        return (sample, fixed_out)

    return on_device


def solution(mesh):
    sizes = dict(mesh.shape)

    def program(diag_inverse, coupling, arrow, tip_inverse, noise, noise_fixed, section_lengths):
        device = build(
            sizes["tm"],
            sizes["space"],
            diag_inverse.shape[1] // sizes["space"],
            noise.shape[2],
            arrow.shape[1],
        )
        return jax.shard_map(
            device,
            mesh=mesh,
            in_specs=(
                P("tm", "space", None),
                P("tm", "space", None),
                P("tm", None, "space"),
                P(),
                P("tm", "space", None),
                P(None, "space"),
                P(),
            ),
            out_specs=(P("tm", "space", None), P(None, "space")),
            check_vma=False,
        )(diag_inverse, coupling, arrow, tip_inverse, noise, noise_fixed, section_lengths)

    return program
```

```python
import jax
import jax.numpy as jnp
from jax import lax
from jax.experimental import pallas as pl
from jax.experimental.pallas import tpu as pltpu
from jax.sharding import PartitionSpec as P

BF = jnp.bfloat16
F32 = jnp.float32
MIB = 1 << 20


def dot(left, right):
    return jnp.dot(left, right, preferred_element_type=F32)


def dot_last(left, right):
    return lax.dot_general(left, right, (((1,), (1,)), ((), ())), preferred_element_type=F32)


def rounded(value):
    return value.astype(BF).astype(F32)


def total_of(own_ref, got_refs):
    total = rounded(own_ref[...])
    for got in got_refs:
        total = total + got[...].astype(F32)
    return total


def shape_of(shape, dtype):
    return jax.ShapeDtypeStruct(shape, dtype)


def build(n_tm, n_space, rows, columns, fixed_rows):
    nodes = n_space * rows
    tile = 256 if rows % 256 == 0 else rows
    tiles = rows // tile
    quarter = rows // 4
    width = columns // n_space
    peers = range(1, n_space)

    def at_core():
        return lax.axis_index("space")

    def block(step, offset=0, size=rows):
        owner = lax.rem(at_core() - step + n_space, n_space)
        return pl.ds(pl.multiple_of(owner * rows + offset, tile), size)

    def part_rows(step):
        owner = lax.rem(at_core() - step + n_space, n_space)
        return pl.ds(pl.multiple_of(owner * width, width), width)

    def call(body, outs, args, cover, places=None, scratch=(), after=None, aliases=None, after_place=pl.ANY):
        places = dict(places or {})
        args = list(args)
        count = len(args)
        if after is not None:
            args.append(after)
            places[count] = after_place

        def run(*refs):
            body(*refs[:count], *refs[len(args) :])

        specs = [pl.BlockSpec(memory_space=places.get(i, pltpu.VMEM)) for i in range(len(args))]
        args = [
            pltpu.with_memory_space_constraint(a, pltpu.HBM)
            if places.get(i) is pltpu.HBM
            else a
            for i, a in enumerate(args)
        ]
        return pl.pallas_call(
            run,
            in_specs=specs,
            out_specs=[
                pl.BlockSpec(memory_space=places.get(("out", i), pltpu.VMEM))
                for i in range(len(outs))
            ],
            out_shape=outs,
            scratch_shapes=list(scratch),
            input_output_aliases=aliases or {},
            cost_estimate=pl.CostEstimate(
                flops=int(cover * 1e9), bytes_accessed=0, transcendentals=0
            ),
            compiler_params=pltpu.CompilerParams(vmem_limit_bytes=16 * MIB),
        )(*args)

    def lower_rows(left, factor, own_ref, other_ref):
        for step in peers:

            @pl.when(at_core() >= step)
            def _():
                other_ref[step - 1] = dot(left[...], factor[:, block(step)]).astype(BF)

            @pl.when(at_core() < step)
            def _():
                other_ref[step - 1] = jnp.zeros_like(other_ref[step - 1])

        for j in range(tiles):
            at = j * tile
            own_ref[:, at : at + tile] = dot(left[:, at:], factor[at:, block(0, at, tile)])

    def full_rows(left, factor, own_ref, other_ref):
        for step in peers:
            other_ref[step - 1] = dot(left[...], factor[:, block(step)]).astype(BF)
        own_ref[...] = dot(left[...], factor[:, block(0)])

    def lower_own(factor, right, out_ref, wait=None):
        for i in range(tiles):
            at = i * tile
            if wait:
                wait(i)
            out_ref[at : at + tile] = dot(
                factor[at : at + tile, block(0, 0, at + tile)], right[: at + tile]
            )

    def lower_rest(factor, got, value):
        for step in peers:

            @pl.when(at_core() >= step)
            def _():
                value[...] = value[...] + dot(factor[:, block(step)], got[step - 1][...])

    def start_kernel(
        diag, arrow, noise, lengths,
        d0, d1, own, other, n0, mask,
        e1, live_scratch, sem1, sem0, sems,
    ):
        arrow_copy = pltpu.make_async_copy(arrow.at[1], e1, sems.at[0])
        noise_copy = pltpu.make_async_copy(noise.at[0], n0, sems.at[1])
        live_copy = pltpu.make_async_copy(lengths, live_scratch, sems.at[2])

        def lower_copies(slot, target, sem):
            copies = {}
            for step in range(n_space):
                for i in range(tiles):
                    at = i * tile
                    size = rows if step else at + tile
                    part = (pl.ds(at, tile), block(step, 0, size))
                    copies[step, i] = pltpu.make_async_copy(
                        diag.at[(slot, *part)], target.at[part], sem.at[step, i]
                    )
            return copies

        def each(copies, i, act):
            act(copies[0, i])
            for step in peers:

                @pl.when(at_core() >= step)
                def _():
                    act(copies[step, i])

        copies1 = lower_copies(1, d1, sem1)
        copies0 = lower_copies(0, d0, sem0)
        live_copy.start()
        arrow_copy.start()
        for i in range(tiles):
            each(copies1, i, lambda copy: copy.start(priority=i % 2))
        live_copy.wait()
        arrow_copy.wait()
        live = live_scratch[lax.axis_index("tm")] > 1
        mask[...] = jnp.where(live, jnp.ones_like(mask[...]), jnp.zeros_like(mask[...]))
        e1[...] = jnp.where(live, e1[...], jnp.zeros_like(e1[...]))
        for i in range(tiles):
            each(copies1, i, lambda copy: copy.wait())
            each(copies0, i, lambda copy: copy.start(priority=i % 2))
        noise_copy.start()
        lower_rows(e1, d1, own, other)
        for i in range(tiles):
            each(copies0, i, lambda copy: copy.wait())
        noise_copy.wait()

    def k1_copies(coupling, k1, first, count, sems):
        copies = []
        size = quarter // 2
        for i in range(2 * count):
            part = pl.ds(first * quarter + i * size, size)
            copies.append(pltpu.make_async_copy(coupling.at[1, part], k1.at[part], sems.at[i]))
            copies[-1].start(priority=i % 2)
        return copies

    def first_value_kernel(d0, n0, coupling, noise, *refs):
        got, (out, bar, k1, n1, sems) = refs[: n_space - 1], refs[n_space - 1 :]
        copies = k1_copies(coupling, k1, 0, 1, sems)
        copies.append(pltpu.make_async_copy(noise.at[1], n1, sems.at[2]))
        copies[-1].start()
        lower_own(d0, n0, out)
        lower_rest(d0, [piece.at[0] for piece in got], out)
        bar[...] = out[...].astype(BF)
        for copy in copies:
            copy.wait()

    def load_kernel(coupling, arrow, value, _, value_rows, e0, k1, sems):
        copies = k1_copies(coupling, k1, 1, 3, sems)
        copies.append(pltpu.make_async_copy(arrow.at[0], e0, sems.at[6]))
        copies[-1].start()
        value_rows[...] = value[...].T
        for copy in copies:
            copy.wait()

    def target_kernel(k1, bar, n1, e0, own, *refs):
        got, refs = refs[: n_space - 1], refs[n_space - 1 :]
        got_own, refs = refs[: n_space - 1], refs[n_space - 1 :]
        target, part_own, part_other, response, whole = refs
        response[...] = total_of(own, got_own).astype(BF)
        for at in range(0, rows, tile):
            pulled = jnp.zeros((tile, columns), F32)
            for step, piece in enumerate([bar, *got]):
                pulled = pulled + dot(k1[at : at + tile, block(step)], piece[...])
            target[at : at + tile] = (n1[at : at + tile].astype(F32) - pulled).astype(BF)
        whole[...] = (dot(e0[...], bar[...]) + dot(response[...], target[...])).T
        part_own[...] = whole[part_rows(0)]
        for step in peers:
            part_other[step - 1] = whole[part_rows(step)].astype(BF)

    def last_own_kernel(d1, target, value):
        lower_own(d1, target, value)

    def core_sum_kernel(part, _, *refs):
        got, (out, _) = refs[:-2], refs[-2:]
        total = part[...]
        for piece in got:
            total = total + piece[...].astype(F32)
        out[...] = total.astype(BF)

    def fold_kernel(sent, got, out):
        out[...] = (sent[...].astype(F32) + got[...].astype(F32)).astype(BF)

    def last_solve_kernel(d1, first, *refs):
        got, (own, other, value) = refs[: n_space - 1], refs[n_space - 1 :]
        value[...] = first[...]
        lower_rest(d1, got, value)
        lower_rows(value[...].astype(BF).T, d1, own, other)

    def response_kernel(k1, response, own, other):
        full_rows(response, k1, own, other)

    def pass_kernel(k1, mask, solved, *refs):
        got, (base, own, other) = refs[: n_space - 1], refs[n_space - 1 :]
        value = jnp.where(mask[:1, :1] > 0, total_of(solved, got), 0.0)
        base[...] = value
        full_rows(value.astype(BF), k1, own, other)

    def first_response_kernel(d0, e0, tip, pushed, *refs):
        got, (own, other) = refs[: n_space - 1], refs[n_space - 1 :]
        left = (e0[...].astype(F32) - total_of(pushed, got)).astype(BF)
        lower_rows(through_tip(tip[...], left).astype(BF), d0, own, other)

    def first_solve_kernel(d0, value_rows, passed, *refs):
        got, (own, other) = refs[: n_space - 1], refs[n_space - 1 :]
        left = (value_rows[...] - total_of(passed, got)).astype(BF)
        lower_rows(left, d0, own, other)

    def through_tip(tip, right):
        inner = dot(tip, right).astype(BF)
        return dot(tip.astype(F32).T.astype(BF), inner)

    def turn_tip_kernel(response, noise_fixed, tip, last_resp, noise_rows):
        noise_rows[...] = noise_fixed[...].T
        last_resp[...] = through_tip(tip[...], response[...]).T.astype(BF)

    def turn_last_kernel(base, out):
        out[...] = base[...].T

    def turn_response_kernel(first, *refs):
        got, out = refs[:-1], refs[-1]
        out[...] = total_of(first, got).T.astype(BF)

    def turn_first_kernel(solved, *refs):
        got, out = refs[:-1], refs[-1]
        out[...] = total_of(solved, got).T

    def mixed_kernel(noise_rows, *refs):
        terms, out = refs[:-1], refs[-1]
        total = terms[0][...].astype(F32)
        for piece in terms[1:]:
            total = total + piece[...].astype(F32)
        out[...] = (noise_rows[...] - total).astype(BF)

    def final_kernel(bases, responses, mixed, *refs):
        got, (out, whole, result, sems) = refs[: n_space - 1], refs[n_space - 1 :]
        for step, piece in enumerate([mixed, *got]):
            whole[part_rows(step)] = piece[...]
        copies = []
        for slot in range(2):
            for i in range(tiles):
                at = i * tile
                part = (slot, pl.ds(at, tile))
                update = dot_last(responses[slot][at : at + tile], whole[...])
                result[part] = (bases[slot][at : at + tile] - update).astype(BF)
                copies.append(
                    pltpu.make_async_copy(result.at[part], out.at[part], sems.at[slot, i])
                )
                copies[-1].start()
        for copy in copies:
            copy.wait()

    def fixed_kernel(tip, mixed, out):
        forward = dot_last(mixed[...], tip[...])
        out[...] = dot(forward.astype(BF), tip[...]).T

    def swap(value, step):
        pairs = [(i, (i - step) % n_space) for i in range(n_space)]
        return lax.ppermute(value, "space", pairs)

    def send_up(value):
        return [swap(value, -step) for step in peers]

    def send_down(values):
        return [swap(values[step - 1], step) for step in peers]

    steps = n_tm.bit_length() - 1
    assert n_tm == 1 << steps

    def swap_step(value, step):
        pairs = []
        for i in range(n_tm):
            for core in range(n_space):
                bit = 1 << step
                if step < steps - 1:
                    bit = 1 << (step + core * (steps - 1) // n_space) % (steps - 1)
                pairs.append((i * n_space + core, (i ^ bit) * n_space + core))
        return lax.ppermute(value, ("tm", "space"), pairs)

    node_f32, node_bf = shape_of((rows, columns), F32), shape_of((rows, columns), BF)
    flat_f32 = shape_of((columns, rows), F32)
    flat_others = shape_of((n_space - 1, columns, rows), BF)
    fixed_f32 = shape_of((fixed_rows, rows), F32)
    fixed_bf = shape_of((fixed_rows, rows), BF)
    fixed_others = shape_of((n_space - 1, fixed_rows, rows), BF)
    part_bf = shape_of((width, fixed_rows), BF)
    by_node = shape_of((rows, fixed_rows), BF)
    in_vmem = pltpu.VMEM((rows, nodes), BF)
    dma = pltpu.SemaphoreType.DMA

    def fold(sent, got, after):
        size = width * fixed_rows
        return call(fold_kernel, [part_bf], [sent, got], size, 6 * size, after=after)[0]

    def on_device(diag_inverse, coupling, arrow, tip_inverse, noise, noise_fixed, section_lengths):
        got_noise = send_up(noise)
        d0, d1, own, other, n0, mask = call(
            start_kernel,
            [in_vmem, in_vmem, fixed_f32, fixed_others, node_bf, shape_of((8, 128), F32)],
            [diag_inverse, arrow, noise, section_lengths],
            8,
            {i: pltpu.HBM for i in range(4)},
            [
                pltpu.VMEM((fixed_rows, rows), BF),
                pltpu.SMEM(section_lengths.shape, jnp.int32),
                dma((n_space, tiles)),
                dma((n_space, tiles)),
                dma((3,)),
            ],
        )
        got_response = send_down(other)
        value, bar, k1, n1 = call(
            first_value_kernel,
            [node_f32, node_bf, in_vmem, node_bf],
            [d0, n0, coupling, noise, *got_noise],
            8,
            {2: pltpu.HBM, 3: pltpu.HBM},
            [dma((3,))],
        )
        got_bar = send_up(bar)
        value_rows, e0, k1 = call(
            load_kernel,
            [flat_f32, fixed_bf, in_vmem],
            [coupling, arrow, value, k1],
            8,
            {0: pltpu.HBM, 1: pltpu.HBM, 3: pl.ANY, ("out", 2): pl.ANY},
            [dma((7,))],
            aliases={3: 2},
        )
        target, part_own, part_other, response = call(
            target_kernel,
            [
                node_bf,
                shape_of((width, fixed_rows), F32),
                shape_of((n_space - 1, width, fixed_rows), BF),
                fixed_bf,
            ],
            [k1, bar, n1, e0, own, *got_bar, *got_response],
            8,
            scratch=[pltpu.VMEM((columns, fixed_rows), F32)],
        )
        got_parts = send_down(part_other)
        (value,) = call(last_own_kernel, [node_f32], [d1, target], 8)
        sent, target = call(
            core_sum_kernel,
            [part_bf, node_bf],
            [part_own, target, *got_parts],
            0.2,
            {1: pl.ANY, ("out", 1): pl.ANY},
            aliases={1: 1},
            after=value,
        )
        got_target = send_up(target)
        step = 0
        got = []

        def advance(after=None):
            nonlocal sent, got, step
            if step == steps:
                return
            if step:
                (sent,) = call(fold_kernel, [part_bf], [sent, *got], 0.2, after=after)
            got = [swap_step(sent, step)]
            step += 1

        advance()
        solved, other = call(
            last_solve_kernel,
            [flat_f32, flat_others],
            [d1, value, *got_target],
            8,
            scratch=[pltpu.VMEM((rows, columns), F32)],
            after=sent,
        )
        got_solved = send_down(other)
        advance(solved)
        last_resp, noise_rows = call(
            turn_tip_kernel,
            [by_node, shape_of((width, fixed_rows), F32)],
            [response, noise_fixed, tip_inverse],
            5,
            after=sent,
        )
        base, passed, other = call(
            pass_kernel,
            [flat_f32, flat_f32, flat_others],
            [k1, mask, solved, *got_solved],
            8,
            after=noise_rows,
        )
        got_passed = send_down(other)
        advance(base)
        pushed, other = call(
            response_kernel, [fixed_f32, fixed_others], [k1, response], 5, after=sent
        )
        got_pushed = send_down(other)
        solved, other = call(
            first_solve_kernel,
            [flat_f32, flat_others],
            [d0, value_rows, passed, *got_passed],
            8,
            after=pushed,
        )
        got_solved = send_down(other)
        advance(solved)
        first, other = call(
            first_response_kernel,
            [fixed_f32, fixed_others],
            [d0, e0, tip_inverse, pushed, *got_pushed],
            5,
            after=sent,
        )
        got_first = send_down(other)
        (first_base,) = call(turn_first_kernel, [node_f32], [solved, *got_solved], 1, after=first)
        (last_base,) = call(turn_last_kernel, [node_f32], [base], 8, after=first_base)
        (first_resp,) = call(turn_response_kernel, [by_node], [first, *got_first], 1, after=last_base)
        while step < steps:
            advance()
        (mixed,) = call(mixed_kernel, [part_bf], [noise_rows, sent, *got], 0.2, after=first_resp)
        got_mixed = send_up(mixed)
        (fixed_out,) = call(
            fixed_kernel, [shape_of((fixed_rows, width), F32)], [tip_inverse, mixed], 8
        )
        (sample,) = call(
            lambda a, b, c, d, *refs: final_kernel((a, b), (c, d), *refs),
            [shape_of((2, rows, columns), BF)],
            [first_base, last_base, first_resp, last_resp, mixed, *got_mixed],
            8,
            {("out", 0): pl.ANY},
            [
                pltpu.VMEM((columns, fixed_rows), BF),
                pltpu.VMEM((2, rows, columns), BF),
                dma((2, tiles)),
            ],
            after=fixed_out,
            after_place=pltpu.HBM,
        )
        return (sample, fixed_out)

    return on_device


def solution(mesh):
    sizes = dict(mesh.shape)

    def program(diag_inverse, coupling, arrow, tip_inverse, noise, noise_fixed, section_lengths):
        device = build(
            sizes["tm"],
            sizes["space"],
            diag_inverse.shape[1] // sizes["space"],
            noise.shape[2],
            arrow.shape[1],
        )
        return jax.shard_map(
            device,
            mesh=mesh,
            in_specs=(
                P("tm", "space", None),
                P("tm", "space", None),
                P("tm", None, "space"),
                P(),
                P("tm", "space", None),
                P(None, "space"),
                P(),
            ),
            out_specs=(P("tm", "space", None), P(None, "space")),
            check_vma=False,
        )(diag_inverse, coupling, arrow, tip_inverse, noise, noise_fixed, section_lengths)

    return program
```

```python
import jax
import jax.numpy as jnp
from jax import lax
from jax.experimental import pallas as pl
from jax.experimental.pallas import tpu as pltpu
from jax.sharding import PartitionSpec as P

BF = jnp.bfloat16
F32 = jnp.float32
MIB = 1 << 20


def dot(left, right):
    return jnp.dot(left, right, preferred_element_type=F32)


def dot_last(left, right):
    return lax.dot_general(left, right, (((1,), (1,)), ((), ())), preferred_element_type=F32)


def rounded(value):
    return value.astype(BF).astype(F32)


def total_of(own_ref, got_refs):
    total = rounded(own_ref[...])
    for got in got_refs:
        total = total + got[...].astype(F32)
    return total


def shape_of(shape, dtype):
    return jax.ShapeDtypeStruct(shape, dtype)


def build(n_tm, n_space, rows, columns, fixed_rows):
    nodes = n_space * rows
    tile = 256 if rows % 256 == 0 else rows
    tiles = rows // tile
    quarter = rows // 4
    width = columns // n_space
    peers = range(1, n_space)

    def at_core():
        return lax.axis_index("space")

    def block(step, offset=0, size=rows):
        owner = lax.rem(at_core() - step + n_space, n_space)
        return pl.ds(pl.multiple_of(owner * rows + offset, tile), size)

    def part_rows(step):
        owner = lax.rem(at_core() - step + n_space, n_space)
        return pl.ds(pl.multiple_of(owner * width, width), width)

    def call(body, outs, args, cover, places=None, scratch=(), after=None, aliases=None, after_place=pl.ANY):
        places = dict(places or {})
        args = list(args)
        count = len(args)
        if after is not None:
            args.append(after)
            places[count] = after_place

        def run(*refs):
            body(*refs[:count], *refs[len(args) :])

        specs = [pl.BlockSpec(memory_space=places.get(i, pltpu.VMEM)) for i in range(len(args))]
        args = [
            pltpu.with_memory_space_constraint(a, pltpu.HBM)
            if places.get(i) is pltpu.HBM
            else a
            for i, a in enumerate(args)
        ]
        return pl.pallas_call(
            run,
            in_specs=specs,
            out_specs=[
                pl.BlockSpec(memory_space=places.get(("out", i), pltpu.VMEM))
                for i in range(len(outs))
            ],
            out_shape=outs,
            scratch_shapes=list(scratch),
            input_output_aliases=aliases or {},
            cost_estimate=pl.CostEstimate(
                flops=int(cover * 1e9), bytes_accessed=0, transcendentals=0
            ),
            compiler_params=pltpu.CompilerParams(vmem_limit_bytes=16 * MIB),
        )(*args)

    def lower_rows(left, factor, own_ref, other_ref):
        for step in peers:

            @pl.when(at_core() >= step)
            def _():
                other_ref[step - 1] = dot(left[...], factor[:, block(step)]).astype(BF)

            @pl.when(at_core() < step)
            def _():
                other_ref[step - 1] = jnp.zeros_like(other_ref[step - 1])

        for j in range(tiles):
            at = j * tile
            own_ref[:, at : at + tile] = dot(left[:, at:], factor[at:, block(0, at, tile)])

    def full_rows(left, factor, own_ref, other_ref):
        for step in peers:
            other_ref[step - 1] = dot(left[...], factor[:, block(step)]).astype(BF)
        own_ref[...] = dot(left[...], factor[:, block(0)])

    def lower_own(factor, right, out_ref, wait=None):
        for i in range(tiles):
            at = i * tile
            if wait:
                wait(i)
            out_ref[at : at + tile] = dot(
                factor[at : at + tile, block(0, 0, at + tile)], right[: at + tile]
            )

    def lower_rest(factor, got, value):
        for step in peers:

            @pl.when(at_core() >= step)
            def _():
                value[...] = value[...] + dot(factor[:, block(step)], got[step - 1][...])

    def start_kernel(
        diag, arrow, noise, lengths,
        d0, d1, own, other, n0, mask,
        e1, live_scratch, sem1, sem0, sems,
    ):
        arrow_copy = pltpu.make_async_copy(arrow.at[1], e1, sems.at[0])
        noise_copy = pltpu.make_async_copy(noise.at[0], n0, sems.at[1])
        live_copy = pltpu.make_async_copy(lengths, live_scratch, sems.at[2])

        def lower_copies(slot, target, sem):
            copies = {}
            for step in range(n_space):
                for i in range(tiles):
                    at = i * tile
                    size = rows if step else at + tile
                    part = (pl.ds(at, tile), block(step, 0, size))
                    copies[step, i] = pltpu.make_async_copy(
                        diag.at[(slot, *part)], target.at[part], sem.at[step, i]
                    )
            return copies

        def each(copies, i, act):
            act(copies[0, i])
            for step in peers:

                @pl.when(at_core() >= step)
                def _():
                    act(copies[step, i])

        copies1 = lower_copies(1, d1, sem1)
        copies0 = lower_copies(0, d0, sem0)
        live_copy.start()
        arrow_copy.start()
        for i in range(tiles):
            each(copies1, i, lambda copy: copy.start(priority=i % 2))
        live_copy.wait()
        arrow_copy.wait()
        live = live_scratch[lax.axis_index("tm")] > 1
        mask[...] = jnp.where(live, jnp.ones_like(mask[...]), jnp.zeros_like(mask[...]))
        e1[...] = jnp.where(live, e1[...], jnp.zeros_like(e1[...]))
        for i in range(tiles):
            each(copies1, i, lambda copy: copy.wait())
            each(copies0, i, lambda copy: copy.start(priority=i % 2))
        noise_copy.start()
        lower_rows(e1, d1, own, other)
        for i in range(tiles):
            each(copies0, i, lambda copy: copy.wait())
        noise_copy.wait()

    def k1_copies(coupling, k1, first, count, sems):
        copies = []
        size = quarter // 2
        for i in range(2 * count):
            part = pl.ds(first * quarter + i * size, size)
            copies.append(pltpu.make_async_copy(coupling.at[1, part], k1.at[part], sems.at[i]))
            copies[-1].start(priority=i % 2)
        return copies

    def first_value_kernel(d0, n0, coupling, noise, *refs):
        got, (out, bar, k1, n1, sems) = refs[: n_space - 1], refs[n_space - 1 :]
        copies = k1_copies(coupling, k1, 0, 1, sems)
        copies.append(pltpu.make_async_copy(noise.at[1], n1, sems.at[2]))
        copies[-1].start()
        lower_own(d0, n0, out)
        lower_rest(d0, [piece.at[0] for piece in got], out)
        bar[...] = out[...].astype(BF)
        for copy in copies:
            copy.wait()

    def load_kernel(coupling, arrow, value, _, value_rows, e0, k1, sems):
        copies = k1_copies(coupling, k1, 1, 3, sems)
        copies.append(pltpu.make_async_copy(arrow.at[0], e0, sems.at[6]))
        copies[-1].start()
        value_rows[...] = value[...].T
        for copy in copies:
            copy.wait()

    def target_kernel(k1, bar, n1, e0, own, *refs):
        got, refs = refs[: n_space - 1], refs[n_space - 1 :]
        got_own, refs = refs[: n_space - 1], refs[n_space - 1 :]
        target, part_own, part_other, response, whole = refs
        response[...] = total_of(own, got_own).astype(BF)
        for at in range(0, rows, tile):
            pulled = jnp.zeros((tile, columns), F32)
            for step, piece in enumerate([bar, *got]):
                pulled = pulled + dot(k1[at : at + tile, block(step)], piece[...])
            target[at : at + tile] = (n1[at : at + tile].astype(F32) - pulled).astype(BF)
        whole[...] = (dot(e0[...], bar[...]) + dot(response[...], target[...])).T
        part_own[...] = whole[part_rows(0)]
        for step in peers:
            part_other[step - 1] = whole[part_rows(step)].astype(BF)

    def last_own_kernel(d1, target, value):
        lower_own(d1, target, value)

    def core_sum_kernel(part, _, *refs):
        got, (out, _) = refs[:-2], refs[-2:]
        total = part[...]
        for piece in got:
            total = total + piece[...].astype(F32)
        out[...] = total.astype(BF)

    def fold_kernel(sent, got, out):
        out[...] = (sent[...].astype(F32) + got[...].astype(F32)).astype(BF)

    def last_solve_kernel(d1, first, *refs):
        got, (own, other, value) = refs[: n_space - 1], refs[n_space - 1 :]
        value[...] = first[...]
        lower_rest(d1, got, value)
        lower_rows(value[...].astype(BF).T, d1, own, other)

    def pass_kernel(k1, mask, response, solved, *refs):
        got, (base, own, other, left) = refs[: n_space - 1], refs[n_space - 1 :]
        value = jnp.where(mask[:1, :1] > 0, total_of(solved, got), 0.0)
        base[...] = value
        left[:columns] = value.astype(BF)
        left[columns:] = response[...]
        full_rows(left, k1, own, other)

    def first_solve_kernel(d0, value_rows, e0, tip, passed, *refs):
        got, (own, other, left) = refs[: n_space - 1], refs[n_space - 1 :]
        total = total_of(passed, got)
        left[:columns] = (value_rows[...] - total[:columns]).astype(BF)
        pushed = (e0[...].astype(F32) - total[columns:]).astype(BF)
        left[columns:] = through_tip(tip[...], pushed).astype(BF)
        lower_rows(left, d0, own, other)

    def through_tip(tip, right):
        inner = dot(tip, right).astype(BF)
        return dot(tip.astype(F32).T.astype(BF), inner)

    def turn_tip_kernel(response, tip, last_resp):
        last_resp[...] = through_tip(tip[...], response[...]).T.astype(BF)

    def turn_kernel(value, out):
        out[...] = value[...].T

    def turn_first_kernel(solved, *refs):
        got, (base, response) = refs[: n_space - 1], refs[n_space - 1 :]
        total = total_of(solved, got)
        base[...] = total[:columns].T
        response[...] = total[columns:].T.astype(BF)

    def mixed_kernel(noise_rows, *refs):
        terms, out = refs[:-1], refs[-1]
        total = terms[0][...].astype(F32)
        for piece in terms[1:]:
            total = total + piece[...].astype(F32)
        out[...] = (noise_rows[...] - total).astype(BF)

    def final_kernel(bases, responses, mixed, *refs):
        got, (out, whole, result, sems) = refs[: n_space - 1], refs[n_space - 1 :]
        for step, piece in enumerate([mixed, *got]):
            whole[part_rows(step)] = piece[...]
        copies = []
        for slot in range(2):
            for i in range(tiles):
                at = i * tile
                part = (slot, pl.ds(at, tile))
                update = dot_last(responses[slot][at : at + tile], whole[...])
                result[part] = (bases[slot][at : at + tile] - update).astype(BF)
                copies.append(
                    pltpu.make_async_copy(result.at[part], out.at[part], sems.at[slot, i])
                )
                copies[-1].start()
        for copy in copies:
            copy.wait()

    def fixed_kernel(tip, mixed, out):
        forward = dot_last(mixed[...], tip[...])
        out[...] = dot(forward.astype(BF), tip[...]).T

    def swap(value, step):
        pairs = [(i, (i - step) % n_space) for i in range(n_space)]
        return lax.ppermute(value, "space", pairs)

    def send_up(value):
        return [swap(value, -step) for step in peers]

    def send_down(values):
        return [swap(values[step - 1], step) for step in peers]

    steps = n_tm.bit_length() - 1
    assert n_tm == 1 << steps

    def swap_step(value, step):
        pairs = []
        for i in range(n_tm):
            for core in range(n_space):
                bit = 1 << (step + core * steps // n_space) % steps
                pairs.append((i * n_space + core, (i ^ bit) * n_space + core))
        return lax.ppermute(value, ("tm", "space"), pairs)

    node_f32, node_bf = shape_of((rows, columns), F32), shape_of((rows, columns), BF)
    flat_f32 = shape_of((columns, rows), F32)
    flat_others = shape_of((n_space - 1, columns, rows), BF)
    fixed_f32 = shape_of((fixed_rows, rows), F32)
    both_f32 = shape_of((columns + fixed_rows, rows), F32)
    both_others = shape_of((n_space - 1, columns + fixed_rows, rows), BF)
    both_left = pltpu.VMEM((columns + fixed_rows, rows), BF)
    fixed_bf = shape_of((fixed_rows, rows), BF)
    fixed_others = shape_of((n_space - 1, fixed_rows, rows), BF)
    part_bf = shape_of((width, fixed_rows), BF)
    by_node = shape_of((rows, fixed_rows), BF)
    in_vmem = pltpu.VMEM((rows, nodes), BF)
    dma = pltpu.SemaphoreType.DMA

    def fold(sent, got, after):
        size = width * fixed_rows
        return call(fold_kernel, [part_bf], [sent, got], size, 6 * size, after=after)[0]

    def on_device(diag_inverse, coupling, arrow, tip_inverse, noise, noise_fixed, section_lengths):
        got_noise = send_up(noise)
        d0, d1, own, other, n0, mask = call(
            start_kernel,
            [in_vmem, in_vmem, fixed_f32, fixed_others, node_bf, shape_of((8, 128), F32)],
            [diag_inverse, arrow, noise, section_lengths],
            8,
            {i: pltpu.HBM for i in range(4)},
            [
                pltpu.VMEM((fixed_rows, rows), BF),
                pltpu.SMEM(section_lengths.shape, jnp.int32),
                dma((n_space, tiles)),
                dma((n_space, tiles)),
                dma((3,)),
            ],
        )
        got_response = send_down(other)
        value, bar, k1, n1 = call(
            first_value_kernel,
            [node_f32, node_bf, in_vmem, node_bf],
            [d0, n0, coupling, noise, *got_noise],
            8,
            {2: pltpu.HBM, 3: pltpu.HBM},
            [dma((3,))],
        )
        got_bar = send_up(bar)
        value_rows, e0, k1 = call(
            load_kernel,
            [flat_f32, fixed_bf, in_vmem],
            [coupling, arrow, value, k1],
            8,
            {0: pltpu.HBM, 1: pltpu.HBM, 3: pl.ANY, ("out", 2): pl.ANY},
            [dma((7,))],
            aliases={3: 2},
        )
        target, part_own, part_other, response = call(
            target_kernel,
            [
                node_bf,
                shape_of((width, fixed_rows), F32),
                shape_of((n_space - 1, width, fixed_rows), BF),
                fixed_bf,
            ],
            [k1, bar, n1, e0, own, *got_bar, *got_response],
            8,
            scratch=[pltpu.VMEM((columns, fixed_rows), F32)],
        )
        got_parts = send_down(part_other)
        (value,) = call(last_own_kernel, [node_f32], [d1, target], 8)
        sent, target = call(
            core_sum_kernel,
            [part_bf, node_bf],
            [part_own, target, *got_parts],
            0.2,
            {1: pl.ANY, ("out", 1): pl.ANY},
            aliases={1: 1},
            after=value,
        )
        got_target = send_up(target)
        step = 0
        got = []

        def advance(after=None):
            nonlocal sent, got, step
            if step == steps:
                return
            if step:
                (sent,) = call(fold_kernel, [part_bf], [sent, *got], 0.2, after=after)
            got = [swap_step(sent, step)]
            step += 1

        advance()
        solved, other = call(
            last_solve_kernel,
            [flat_f32, flat_others],
            [d1, value, *got_target],
            8,
            scratch=[pltpu.VMEM((rows, columns), F32)],
            after=sent,
        )
        got_solved = send_down(other)
        advance(solved)
        (last_resp,) = call(
            turn_tip_kernel, [by_node], [response, tip_inverse], 5, after=sent
        )
        base, passed, other = call(
            pass_kernel,
            [flat_f32, both_f32, both_others],
            [k1, mask, response, solved, *got_solved],
            10,
            scratch=[both_left],
            after=last_resp,
        )
        got_passed = send_down(other)
        advance(base)
        (last_base,) = call(turn_kernel, [node_f32], [base], 11, after=sent)
        solved, other = call(
            first_solve_kernel,
            [both_f32, both_others],
            [d0, value_rows, e0, tip_inverse, passed, *got_passed],
            10,
            scratch=[both_left],
            after=last_base,
        )
        got_solved = send_down(other)
        advance(solved)
        (noise_rows,) = call(
            turn_kernel,
            [shape_of((width, fixed_rows), F32)],
            [noise_fixed],
            11,
            after=sent,
        )
        first_base, first_resp = call(
            turn_first_kernel, [node_f32, by_node], [solved, *got_solved], 1, after=noise_rows
        )
        while step < steps:
            advance()
        (mixed,) = call(mixed_kernel, [part_bf], [noise_rows, sent, *got], 0.2, after=first_resp)
        got_mixed = send_up(mixed)
        (fixed_out,) = call(
            fixed_kernel, [shape_of((fixed_rows, width), F32)], [tip_inverse, mixed], 8
        )
        (sample,) = call(
            lambda a, b, c, d, *refs: final_kernel((a, b), (c, d), *refs),
            [shape_of((2, rows, columns), BF)],
            [first_base, last_base, first_resp, last_resp, mixed, *got_mixed],
            8,
            {("out", 0): pl.ANY},
            [
                pltpu.VMEM((columns, fixed_rows), BF),
                pltpu.VMEM((2, rows, columns), BF),
                dma((2, tiles)),
            ],
            after=fixed_out,
            after_place=pltpu.HBM,
        )
        return (sample, fixed_out)

    return on_device


def solution(mesh):
    sizes = dict(mesh.shape)

    def program(diag_inverse, coupling, arrow, tip_inverse, noise, noise_fixed, section_lengths):
        device = build(
            sizes["tm"],
            sizes["space"],
            diag_inverse.shape[1] // sizes["space"],
            noise.shape[2],
            arrow.shape[1],
        )
        return jax.shard_map(
            device,
            mesh=mesh,
            in_specs=(
                P("tm", "space", None),
                P("tm", "space", None),
                P("tm", None, "space"),
                P(),
                P("tm", "space", None),
                P(None, "space"),
                P(),
            ),
            out_specs=(P("tm", "space", None), P(None, "space")),
            check_vma=False,
        )(diag_inverse, coupling, arrow, tip_inverse, noise, noise_fixed, section_lengths)

    return program
```

```python
import jax
import jax.numpy as jnp
from jax import lax
from jax.experimental import pallas as pl
from jax.experimental.pallas import tpu as pltpu
from jax.sharding import PartitionSpec as P

BF = jnp.bfloat16
F32 = jnp.float32
MIB = 1 << 20


def dot(left, right):
    return jnp.dot(left, right, preferred_element_type=F32)


def dot_last(left, right):
    return lax.dot_general(left, right, (((1,), (1,)), ((), ())), preferred_element_type=F32)


def rounded(value):
    return value.astype(BF).astype(F32)


def total_of(own_ref, got_refs):
    total = rounded(own_ref[...])
    for got in got_refs:
        total = total + got[...].astype(F32)
    return total


def shape_of(shape, dtype):
    return jax.ShapeDtypeStruct(shape, dtype)


def build(n_tm, n_space, rows, columns, fixed_rows):
    nodes = n_space * rows
    tile = 256 if rows % 256 == 0 else rows
    tiles = rows // tile
    quarter = rows // 4
    width = columns // n_space
    peers = range(1, n_space)

    def at_core():
        return lax.axis_index("space")

    def block(step, offset=0, size=rows):
        owner = lax.rem(at_core() - step + n_space, n_space)
        return pl.ds(pl.multiple_of(owner * rows + offset, tile), size)

    def part_rows(step):
        owner = lax.rem(at_core() - step + n_space, n_space)
        return pl.ds(pl.multiple_of(owner * width, width), width)

    def call(body, outs, args, cover, places=None, scratch=(), after=None, aliases=None, after_place=pl.ANY):
        places = dict(places or {})
        args = list(args)
        count = len(args)
        if after is not None:
            args.append(after)
            places[count] = after_place

        def run(*refs):
            body(*refs[:count], *refs[len(args) :])

        specs = [pl.BlockSpec(memory_space=places.get(i, pltpu.VMEM)) for i in range(len(args))]
        args = [
            pltpu.with_memory_space_constraint(a, pltpu.HBM)
            if places.get(i) is pltpu.HBM
            else a
            for i, a in enumerate(args)
        ]
        return pl.pallas_call(
            run,
            in_specs=specs,
            out_specs=[
                pl.BlockSpec(memory_space=places.get(("out", i), pltpu.VMEM))
                for i in range(len(outs))
            ],
            out_shape=outs,
            scratch_shapes=list(scratch),
            input_output_aliases=aliases or {},
            cost_estimate=pl.CostEstimate(
                flops=int(cover * 1e9), bytes_accessed=0, transcendentals=0
            ),
            compiler_params=pltpu.CompilerParams(vmem_limit_bytes=16 * MIB),
        )(*args)

    def lower_others(left, factor, other_ref):
        for step in peers:

            @pl.when(at_core() >= step)
            def _():
                other_ref[step - 1] = dot(left[...], factor[:, block(step)]).astype(BF)

            @pl.when(at_core() < step)
            def _():
                other_ref[step - 1] = jnp.zeros_like(other_ref[step - 1])

    def lower_block(left, factor, own_ref):
        for j in range(tiles):
            at = j * tile
            own_ref[:, at : at + tile] = dot(left[:, at:], factor[at:, block(0, at, tile)])

    def lower_rows(left, factor, own_ref, other_ref):
        lower_others(left, factor, other_ref)
        lower_block(left, factor, own_ref)

    def full_rows(left, factor, own_ref, other_ref):
        for step in peers:
            other_ref[step - 1] = dot(left[...], factor[:, block(step)]).astype(BF)
        own_ref[...] = dot(left[...], factor[:, block(0)])

    def lower_own(factor, right, out_ref, wait=None):
        for i in range(tiles):
            at = i * tile
            if wait:
                wait(i)
            out_ref[at : at + tile] = dot(
                factor[at : at + tile, block(0, 0, at + tile)], right[: at + tile]
            )

    def lower_rest(factor, got, value):
        for step in peers:

            @pl.when(at_core() >= step)
            def _():
                value[...] = value[...] + dot(factor[:, block(step)], got[step - 1][...])

    def start_kernel(
        diag, arrow, noise, lengths,
        d0, d1, own, other, n0, mask,
        e1, live_scratch, sem1, sem0, sems,
    ):
        arrow_copy = pltpu.make_async_copy(arrow.at[1], e1, sems.at[0])
        noise_copy = pltpu.make_async_copy(noise.at[0], n0, sems.at[1])
        live_copy = pltpu.make_async_copy(lengths, live_scratch, sems.at[2])

        def lower_copies(slot, target, sem):
            copies = {}
            for step in range(n_space):
                for i in range(tiles):
                    at = i * tile
                    size = rows if step else at + tile
                    part = (pl.ds(at, tile), block(step, 0, size))
                    copies[step, i] = pltpu.make_async_copy(
                        diag.at[(slot, *part)], target.at[part], sem.at[step, i]
                    )
            return copies

        def each(copies, i, act):
            act(copies[0, i])
            for step in peers:

                @pl.when(at_core() >= step)
                def _():
                    act(copies[step, i])

        copies1 = lower_copies(1, d1, sem1)
        copies0 = lower_copies(0, d0, sem0)
        live_copy.start()
        arrow_copy.start()
        for i in range(tiles):
            each(copies1, i, lambda copy: copy.start(priority=i % 2))
        live_copy.wait()
        arrow_copy.wait()
        live = live_scratch[lax.axis_index("tm")] > 1
        mask[...] = jnp.where(live, jnp.ones_like(mask[...]), jnp.zeros_like(mask[...]))
        e1[...] = jnp.where(live, e1[...], jnp.zeros_like(e1[...]))
        for i in range(tiles):
            each(copies1, i, lambda copy: copy.wait())
            each(copies0, i, lambda copy: copy.start(priority=i % 2))
        noise_copy.start()
        lower_rows(e1, d1, own, other)
        for i in range(tiles):
            each(copies0, i, lambda copy: copy.wait())
        noise_copy.wait()

    def k1_copies(coupling, k1, first, count, sems):
        copies = []
        size = quarter // 2
        for i in range(2 * count):
            part = pl.ds(first * quarter + i * size, size)
            copies.append(pltpu.make_async_copy(coupling.at[1, part], k1.at[part], sems.at[i]))
            copies[-1].start(priority=i % 2)
        return copies

    def first_value_kernel(d0, n0, coupling, noise, *refs):
        got, (out, bar, k1, n1, sems) = refs[: n_space - 1], refs[n_space - 1 :]
        copies = k1_copies(coupling, k1, 0, 1, sems)
        copies.append(pltpu.make_async_copy(noise.at[1], n1, sems.at[2]))
        copies[-1].start()
        lower_own(d0, n0, out)
        lower_rest(d0, [piece.at[0] for piece in got], out)
        bar[...] = out[...].astype(BF)
        for copy in copies:
            copy.wait()

    def load_kernel(coupling, arrow, value, _, value_rows, e0, k1, sems):
        copies = k1_copies(coupling, k1, 1, 3, sems)
        copies.append(pltpu.make_async_copy(arrow.at[0], e0, sems.at[6]))
        copies[-1].start()
        value_rows[...] = value[...].T
        for copy in copies:
            copy.wait()

    def target_kernel(k1, bar, n1, e0, own, *refs):
        got, refs = refs[: n_space - 1], refs[n_space - 1 :]
        got_own, refs = refs[: n_space - 1], refs[n_space - 1 :]
        target, part_own, part_other, response, whole = refs
        response[...] = total_of(own, got_own).astype(BF)
        for at in range(0, rows, tile):
            pulled = jnp.zeros((tile, columns), F32)
            for step, piece in enumerate([bar, *got]):
                pulled = pulled + dot(k1[at : at + tile, block(step)], piece[...])
            target[at : at + tile] = (n1[at : at + tile].astype(F32) - pulled).astype(BF)
        whole[...] = (dot(e0[...], bar[...]) + dot(response[...], target[...])).T
        part_own[...] = whole[part_rows(0)]
        for step in peers:
            part_other[step - 1] = whole[part_rows(step)].astype(BF)

    def last_own_kernel(d1, target, value):
        lower_own(d1, target, value)

    def core_sum_kernel(part, _, *refs):
        got, (out, _) = refs[:-2], refs[-2:]
        total = part[...]
        for piece in got:
            total = total + piece[...].astype(F32)
        out[...] = total.astype(BF)

    def fold_kernel(sent, got, out):
        out[...] = (sent[...].astype(F32) + got[...].astype(F32)).astype(BF)

    def last_solve_kernel(d1, first, *refs):
        got, (own, other, value) = refs[: n_space - 1], refs[n_space - 1 :]
        value[...] = first[...]
        lower_rest(d1, got, value)
        lower_rows(value[...].astype(BF).T, d1, own, other)

    def response_kernel(k1, response, own, other):
        full_rows(response, k1, own, other)

    def pass_kernel(k1, mask, solved, *refs):
        got, (base, own, other) = refs[: n_space - 1], refs[n_space - 1 :]
        value = jnp.where(mask[:1, :1] > 0, total_of(solved, got), 0.0)
        base[...] = value
        full_rows(value.astype(BF), k1, own, other)

    def first_response_kernel(d0, e0, tip, pushed, *refs):
        got, (left, other) = refs[: n_space - 1], refs[n_space - 1 :]
        inner = (e0[...].astype(F32) - total_of(pushed, got)).astype(BF)
        left[...] = through_tip(tip[...], inner).astype(BF)
        lower_others(left, d0, other)

    def own_response_kernel(d0, left, own):
        lower_block(left, d0, own)

    def first_solve_kernel(d0, value_rows, passed, *refs):
        got, (own, other) = refs[: n_space - 1], refs[n_space - 1 :]
        left = (value_rows[...] - total_of(passed, got)).astype(BF)
        lower_rows(left, d0, own, other)

    def through_tip(tip, right):
        inner = dot(tip, right).astype(BF)
        return dot(tip.astype(F32).T.astype(BF), inner)

    def turn_last_kernel(base, response, noise_fixed, tip, last_base, last_resp, noise_rows):
        noise_rows[...] = noise_fixed[...].T
        last_base[...] = base[...].T
        last_resp[...] = through_tip(tip[...], response[...]).T.astype(BF)

    def turn_response_kernel(first, *refs):
        got, out = refs[:-1], refs[-1]
        out[...] = total_of(first, got).T.astype(BF)

    def turn_first_kernel(solved, *refs):
        got, out = refs[:-1], refs[-1]
        out[...] = total_of(solved, got).T

    def mixed_kernel(noise_rows, *refs):
        terms, out = refs[:-1], refs[-1]
        total = terms[0][...].astype(F32)
        for piece in terms[1:]:
            total = total + piece[...].astype(F32)
        out[...] = (noise_rows[...] - total).astype(BF)

    def final_kernel(bases, responses, mixed, *refs):
        got, (out, whole, result, sems) = refs[: n_space - 1], refs[n_space - 1 :]
        for step, piece in enumerate([mixed, *got]):
            whole[part_rows(step)] = piece[...]
        copies = []
        for slot in range(2):
            for i in range(tiles):
                at = i * tile
                part = (slot, pl.ds(at, tile))
                update = dot_last(responses[slot][at : at + tile], whole[...])
                result[part] = (bases[slot][at : at + tile] - update).astype(BF)
                copies.append(
                    pltpu.make_async_copy(result.at[part], out.at[part], sems.at[slot, i])
                )
                copies[-1].start()
        for copy in copies:
            copy.wait()

    def fixed_kernel(tip, mixed, out):
        forward = dot_last(mixed[...], tip[...])
        out[...] = dot(forward.astype(BF), tip[...]).T

    def swap(value, step):
        pairs = [(i, (i - step) % n_space) for i in range(n_space)]
        return lax.ppermute(value, "space", pairs)

    def send_up(value):
        return [swap(value, -step) for step in peers]

    def send_down(values):
        return [swap(values[step - 1], step) for step in peers]

    steps = n_tm.bit_length() - 1
    assert n_tm == 1 << steps

    def swap_step(value, step):
        pairs = []
        for i in range(n_tm):
            for core in range(n_space):
                bit = 1 << (step + core * steps // n_space) % steps
                pairs.append((i * n_space + core, (i ^ bit) * n_space + core))
        return lax.ppermute(value, ("tm", "space"), pairs)

    node_f32, node_bf = shape_of((rows, columns), F32), shape_of((rows, columns), BF)
    flat_f32 = shape_of((columns, rows), F32)
    flat_others = shape_of((n_space - 1, columns, rows), BF)
    fixed_f32 = shape_of((fixed_rows, rows), F32)
    fixed_bf = shape_of((fixed_rows, rows), BF)
    fixed_others = shape_of((n_space - 1, fixed_rows, rows), BF)
    part_bf = shape_of((width, fixed_rows), BF)
    by_node = shape_of((rows, fixed_rows), BF)
    in_vmem = pltpu.VMEM((rows, nodes), BF)
    dma = pltpu.SemaphoreType.DMA

    def fold(sent, got, after):
        size = width * fixed_rows
        return call(fold_kernel, [part_bf], [sent, got], size, 6 * size, after=after)[0]

    def on_device(diag_inverse, coupling, arrow, tip_inverse, noise, noise_fixed, section_lengths):
        got_noise = send_up(noise)
        d0, d1, own, other, n0, mask = call(
            start_kernel,
            [in_vmem, in_vmem, fixed_f32, fixed_others, node_bf, shape_of((8, 128), F32)],
            [diag_inverse, arrow, noise, section_lengths],
            8,
            {i: pltpu.HBM for i in range(4)},
            [
                pltpu.VMEM((fixed_rows, rows), BF),
                pltpu.SMEM(section_lengths.shape, jnp.int32),
                dma((n_space, tiles)),
                dma((n_space, tiles)),
                dma((3,)),
            ],
        )
        got_response = send_down(other)
        value, bar, k1, n1 = call(
            first_value_kernel,
            [node_f32, node_bf, in_vmem, node_bf],
            [d0, n0, coupling, noise, *got_noise],
            8,
            {2: pltpu.HBM, 3: pltpu.HBM},
            [dma((3,))],
        )
        got_bar = send_up(bar)
        value_rows, e0, k1 = call(
            load_kernel,
            [flat_f32, fixed_bf, in_vmem],
            [coupling, arrow, value, k1],
            8,
            {0: pltpu.HBM, 1: pltpu.HBM, 3: pl.ANY, ("out", 2): pl.ANY},
            [dma((7,))],
            aliases={3: 2},
        )
        target, part_own, part_other, response = call(
            target_kernel,
            [
                node_bf,
                shape_of((width, fixed_rows), F32),
                shape_of((n_space - 1, width, fixed_rows), BF),
                fixed_bf,
            ],
            [k1, bar, n1, e0, own, *got_bar, *got_response],
            8,
            scratch=[pltpu.VMEM((columns, fixed_rows), F32)],
        )
        got_parts = send_down(part_other)
        (value,) = call(last_own_kernel, [node_f32], [d1, target], 8)
        sent, target = call(
            core_sum_kernel,
            [part_bf, node_bf],
            [part_own, target, *got_parts],
            0.2,
            {1: pl.ANY, ("out", 1): pl.ANY},
            aliases={1: 1},
            after=value,
        )
        got_target = send_up(target)
        step = 0
        got = []

        def advance(after=None):
            nonlocal sent, got, step
            if step == steps:
                return
            if step:
                (sent,) = call(fold_kernel, [part_bf], [sent, *got], 0.2, after=after)
            got = [swap_step(sent, step)]
            step += 1

        advance()
        solved, other = call(
            last_solve_kernel,
            [flat_f32, flat_others],
            [d1, value, *got_target],
            8,
            scratch=[pltpu.VMEM((rows, columns), F32)],
            after=sent,
        )
        got_solved = send_down(other)
        advance(solved)
        pushed, other = call(
            response_kernel, [fixed_f32, fixed_others], [k1, response], 5, after=sent
        )
        got_pushed = send_down(other)
        base, passed, other = call(
            pass_kernel,
            [flat_f32, flat_f32, flat_others],
            [k1, mask, solved, *got_solved],
            8,
            after=pushed,
        )
        got_passed = send_down(other)
        advance(base)
        last_base, last_resp, noise_rows = call(
            turn_last_kernel,
            [node_f32, by_node, shape_of((width, fixed_rows), F32)],
            [base, response, noise_fixed, tip_inverse],
            5,
            after=sent,
        )
        solved, other = call(
            first_solve_kernel,
            [flat_f32, flat_others],
            [d0, value_rows, passed, *got_passed],
            8,
            after=noise_rows,
        )
        got_solved = send_down(other)
        advance(solved)
        left, other = call(
            first_response_kernel,
            [fixed_bf, fixed_others],
            [d0, e0, tip_inverse, pushed, *got_pushed],
            5,
            after=sent,
        )
        got_first = send_down(other)
        (first_base,) = call(turn_first_kernel, [node_f32], [solved, *got_solved], 1, after=left)
        (first,) = call(own_response_kernel, [fixed_f32], [d0, left], 8, after=first_base)
        (first_resp,) = call(turn_response_kernel, [by_node], [first, *got_first], 1, after=first)
        while step < steps:
            advance()
        (mixed,) = call(mixed_kernel, [part_bf], [noise_rows, sent, *got], 0.2, after=first_resp)
        got_mixed = send_up(mixed)
        (fixed_out,) = call(
            fixed_kernel, [shape_of((fixed_rows, width), F32)], [tip_inverse, mixed], 8
        )
        (sample,) = call(
            lambda a, b, c, d, *refs: final_kernel((a, b), (c, d), *refs),
            [shape_of((2, rows, columns), BF)],
            [first_base, last_base, first_resp, last_resp, mixed, *got_mixed],
            8,
            {("out", 0): pl.ANY},
            [
                pltpu.VMEM((columns, fixed_rows), BF),
                pltpu.VMEM((2, rows, columns), BF),
                dma((2, tiles)),
            ],
            after=fixed_out,
            after_place=pltpu.HBM,
        )
        return (sample, fixed_out)

    return on_device


def solution(mesh):
    sizes = dict(mesh.shape)

    def program(diag_inverse, coupling, arrow, tip_inverse, noise, noise_fixed, section_lengths):
        device = build(
            sizes["tm"],
            sizes["space"],
            diag_inverse.shape[1] // sizes["space"],
            noise.shape[2],
            arrow.shape[1],
        )
        return jax.shard_map(
            device,
            mesh=mesh,
            in_specs=(
                P("tm", "space", None),
                P("tm", "space", None),
                P("tm", None, "space"),
                P(),
                P("tm", "space", None),
                P(None, "space"),
                P(),
            ),
            out_specs=(P("tm", "space", None), P(None, "space")),
            check_vma=False,
        )(diag_inverse, coupling, arrow, tip_inverse, noise, noise_fixed, section_lengths)

    return program
```

```python
import jax
import jax.numpy as jnp
from jax import lax
from jax.experimental import pallas as pl
from jax.experimental.pallas import tpu as pltpu
from jax.sharding import PartitionSpec as P

BF = jnp.bfloat16
F32 = jnp.float32
MIB = 1 << 20


def dot(left, right):
    return jnp.dot(left, right, preferred_element_type=F32)


def dot_last(left, right):
    return lax.dot_general(left, right, (((1,), (1,)), ((), ())), preferred_element_type=F32)


def rounded(value):
    return value.astype(BF).astype(F32)


def total_of(own_ref, got_refs):
    total = rounded(own_ref[...])
    for got in got_refs:
        total = total + got[...].astype(F32)
    return total


def shape_of(shape, dtype):
    return jax.ShapeDtypeStruct(shape, dtype)


def build(n_tm, n_space, rows, columns, fixed_rows):
    nodes = n_space * rows
    tile = 256 if rows % 256 == 0 else rows
    tiles = rows // tile
    quarter = rows // 4
    width = columns // n_space
    peers = range(1, n_space)

    def at_core():
        return lax.axis_index("space")

    def block(step, offset=0, size=rows):
        owner = lax.rem(at_core() - step + n_space, n_space)
        return pl.ds(pl.multiple_of(owner * rows + offset, tile), size)

    def part_rows(step):
        owner = lax.rem(at_core() - step + n_space, n_space)
        return pl.ds(pl.multiple_of(owner * width, width), width)

    def call(body, outs, args, cover, places=None, scratch=(), after=None, aliases=None, after_place=pl.ANY):
        places = dict(places or {})
        args = list(args)
        count = len(args)
        if after is not None:
            args.append(after)
            places[count] = after_place

        def run(*refs):
            body(*refs[:count], *refs[len(args) :])

        specs = [pl.BlockSpec(memory_space=places.get(i, pltpu.VMEM)) for i in range(len(args))]
        args = [
            pltpu.with_memory_space_constraint(a, pltpu.HBM)
            if places.get(i) is pltpu.HBM
            else a
            for i, a in enumerate(args)
        ]
        return pl.pallas_call(
            run,
            in_specs=specs,
            out_specs=[
                pl.BlockSpec(memory_space=places.get(("out", i), pltpu.VMEM))
                for i in range(len(outs))
            ],
            out_shape=outs,
            scratch_shapes=list(scratch),
            input_output_aliases=aliases or {},
            cost_estimate=pl.CostEstimate(
                flops=int(cover * 1e9), bytes_accessed=0, transcendentals=0
            ),
            compiler_params=pltpu.CompilerParams(vmem_limit_bytes=16 * MIB),
        )(*args)

    def lower_others(left, factor, other_ref):
        for step in peers:

            @pl.when(at_core() >= step)
            def _():
                other_ref[step - 1] = dot(left[...], factor[:, block(step)]).astype(BF)

            @pl.when(at_core() < step)
            def _():
                other_ref[step - 1] = jnp.zeros_like(other_ref[step - 1])

    def lower_block(left, factor, own_ref):
        for j in range(tiles):
            at = j * tile
            own_ref[:, at : at + tile] = dot(left[:, at:], factor[at:, block(0, at, tile)])

    def lower_rows(left, factor, own_ref, other_ref):
        lower_others(left, factor, other_ref)
        lower_block(left, factor, own_ref)

    def full_rows(left, factor, own_ref, other_ref):
        for step in peers:
            other_ref[step - 1] = dot(left[...], factor[:, block(step)]).astype(BF)
        own_ref[...] = dot(left[...], factor[:, block(0)])

    def lower_own(factor, right, out_ref, wait=None):
        for i in range(tiles):
            at = i * tile
            if wait:
                wait(i)
            out_ref[at : at + tile] = dot(
                factor[at : at + tile, block(0, 0, at + tile)], right[: at + tile]
            )

    def lower_rest(factor, got, value):
        for step in peers:

            @pl.when(at_core() >= step)
            def _():
                value[...] = value[...] + dot(factor[:, block(step)], got[step - 1][...])

    def start_kernel(
        diag, arrow, noise, lengths,
        d0, d1, own, other, n0, mask,
        e1, live_scratch, sem1, sem0, sems,
    ):
        arrow_copy = pltpu.make_async_copy(arrow.at[1], e1, sems.at[0])
        noise_copy = pltpu.make_async_copy(noise.at[0], n0, sems.at[1])
        live_copy = pltpu.make_async_copy(lengths, live_scratch, sems.at[2])

        def lower_copies(slot, target, sem):
            copies = {}
            for step in range(n_space):
                for i in range(tiles):
                    at = i * tile
                    size = rows if step else at + tile
                    part = (pl.ds(at, tile), block(step, 0, size))
                    copies[step, i] = pltpu.make_async_copy(
                        diag.at[(slot, *part)], target.at[part], sem.at[step, i]
                    )
            return copies

        def each(copies, i, act):
            act(copies[0, i])
            for step in peers:

                @pl.when(at_core() >= step)
                def _():
                    act(copies[step, i])

        copies1 = lower_copies(1, d1, sem1)
        copies0 = lower_copies(0, d0, sem0)
        live_copy.start()
        arrow_copy.start()
        for i in range(tiles):
            each(copies1, i, lambda copy: copy.start(priority=i % 2))
        live_copy.wait()
        arrow_copy.wait()
        live = live_scratch[lax.axis_index("tm")] > 1
        mask[...] = jnp.where(live, jnp.ones_like(mask[...]), jnp.zeros_like(mask[...]))
        e1[...] = jnp.where(live, e1[...], jnp.zeros_like(e1[...]))
        for i in range(tiles):
            each(copies1, i, lambda copy: copy.wait())
            each(copies0, i, lambda copy: copy.start(priority=i % 2))
        noise_copy.start()
        lower_rows(e1, d1, own, other)
        for i in range(tiles):
            each(copies0, i, lambda copy: copy.wait())
        noise_copy.wait()

    def k1_copies(coupling, k1, first, count, sems):
        copies = []
        size = quarter // 2
        for i in range(2 * count):
            part = pl.ds(first * quarter + i * size, size)
            copies.append(pltpu.make_async_copy(coupling.at[1, part], k1.at[part], sems.at[i]))
            copies[-1].start(priority=i % 2)
        return copies

    def first_value_kernel(d0, n0, coupling, noise, *refs):
        got, (out, bar, k1, n1, sems) = refs[: n_space - 1], refs[n_space - 1 :]
        copies = k1_copies(coupling, k1, 0, 1, sems)
        copies.append(pltpu.make_async_copy(noise.at[1], n1, sems.at[2]))
        copies[-1].start()
        lower_own(d0, n0, out)
        lower_rest(d0, [piece.at[0] for piece in got], out)
        bar[...] = out[...].astype(BF)
        for copy in copies:
            copy.wait()

    def load_kernel(coupling, arrow, value, _, value_rows, e0, k1, sems):
        copies = k1_copies(coupling, k1, 1, 3, sems)
        copies.append(pltpu.make_async_copy(arrow.at[0], e0, sems.at[6]))
        copies[-1].start()
        value_rows[...] = value[...].T
        for copy in copies:
            copy.wait()

    def target_kernel(k1, bar, n1, e0, own, *refs):
        got, refs = refs[: n_space - 1], refs[n_space - 1 :]
        got_own, refs = refs[: n_space - 1], refs[n_space - 1 :]
        target, part_own, part_other, response, whole = refs
        response[...] = total_of(own, got_own).astype(BF)
        for at in range(0, rows, tile):
            pulled = jnp.zeros((tile, columns), F32)
            for step, piece in enumerate([bar, *got]):
                pulled = pulled + dot(k1[at : at + tile, block(step)], piece[...])
            target[at : at + tile] = (n1[at : at + tile].astype(F32) - pulled).astype(BF)
        whole[...] = (dot(e0[...], bar[...]) + dot(response[...], target[...])).T
        part_own[...] = whole[part_rows(0)]
        for step in peers:
            part_other[step - 1] = whole[part_rows(step)].astype(BF)

    def last_own_kernel(d1, target, value):
        lower_own(d1, target, value)

    def core_sum_kernel(part, *refs):
        got, out = refs[:-1], refs[-1]
        total = part[...]
        for piece in got:
            total = total + piece[...].astype(F32)
        out[...] = total.astype(BF)

    def fold_kernel(sent, got, out):
        out[...] = (sent[...].astype(F32) + got[...].astype(F32)).astype(BF)

    def last_solve_kernel(d1, first, *refs):
        got, (own, other, value) = refs[: n_space - 1], refs[n_space - 1 :]
        value[...] = first[...]
        lower_rest(d1, got, value)
        lower_rows(value[...].astype(BF).T, d1, own, other)

    def response_kernel(k1, response, own, other):
        full_rows(response, k1, own, other)

    def pass_kernel(k1, mask, solved, *refs):
        got, (base, own, other) = refs[: n_space - 1], refs[n_space - 1 :]
        value = jnp.where(mask[:1, :1] > 0, total_of(solved, got), 0.0)
        base[...] = value
        full_rows(value.astype(BF), k1, own, other)

    def first_response_kernel(d0, e0, tip, pushed, *refs):
        got, (left, other) = refs[: n_space - 1], refs[n_space - 1 :]
        inner = (e0[...].astype(F32) - total_of(pushed, got)).astype(BF)
        left[...] = through_tip(tip[...], inner).astype(BF)
        lower_others(left, d0, other)

    def own_response_kernel(d0, left, own):
        lower_block(left, d0, own)

    def first_solve_kernel(d0, value_rows, passed, *refs):
        got, (own, other) = refs[: n_space - 1], refs[n_space - 1 :]
        left = (value_rows[...] - total_of(passed, got)).astype(BF)
        lower_rows(left, d0, own, other)

    def through_tip(tip, right):
        inner = dot(tip, right).astype(BF)
        return dot(tip.astype(F32).T.astype(BF), inner)

    def turn_last_kernel(base, response, noise_fixed, tip, last_base, last_resp, noise_rows):
        noise_rows[...] = noise_fixed[...].T
        last_base[...] = base[...].T
        last_resp[...] = through_tip(tip[...], response[...]).T.astype(BF)

    def turn_response_kernel(first, *refs):
        got, out = refs[:-1], refs[-1]
        out[...] = total_of(first, got).T.astype(BF)

    def turn_first_kernel(solved, *refs):
        got, out = refs[:-1], refs[-1]
        out[...] = total_of(solved, got).T

    def mixed_kernel(noise_rows, *refs):
        terms, out = refs[:-1], refs[-1]
        total = terms[0][...].astype(F32)
        for piece in terms[1:]:
            total = total + piece[...].astype(F32)
        out[...] = (noise_rows[...] - total).astype(BF)

    def final_kernel(bases, responses, mixed, *refs):
        got, (out, whole, result, sems) = refs[: n_space - 1], refs[n_space - 1 :]
        for step, piece in enumerate([mixed, *got]):
            whole[part_rows(step)] = piece[...]
        copies = []
        for slot in range(2):
            for i in range(tiles):
                at = i * tile
                part = (slot, pl.ds(at, tile))
                update = dot_last(responses[slot][at : at + tile], whole[...])
                result[part] = (bases[slot][at : at + tile] - update).astype(BF)
                copies.append(
                    pltpu.make_async_copy(result.at[part], out.at[part], sems.at[slot, i])
                )
                copies[-1].start()
        for copy in copies:
            copy.wait()

    def fixed_kernel(tip, mixed, out):
        forward = dot_last(mixed[...], tip[...])
        out[...] = dot(forward.astype(BF), tip[...]).T

    def swap(value, step):
        pairs = [(i, (i - step) % n_space) for i in range(n_space)]
        return lax.ppermute(value, "space", pairs)

    def send_up(value):
        return [swap(value, -step) for step in peers]

    def send_down(values):
        return [swap(values[step - 1], step) for step in peers]

    steps = n_tm.bit_length() - 1
    assert n_tm == 1 << steps

    def swap_step(value, step):
        pairs = []
        for i in range(n_tm):
            for core in range(n_space):
                bit = 1 << (step + core * steps // n_space) % steps
                pairs.append((i * n_space + core, (i ^ bit) * n_space + core))
        return lax.ppermute(value, ("tm", "space"), pairs)

    node_f32, node_bf = shape_of((rows, columns), F32), shape_of((rows, columns), BF)
    flat_f32 = shape_of((columns, rows), F32)
    flat_others = shape_of((n_space - 1, columns, rows), BF)
    fixed_f32 = shape_of((fixed_rows, rows), F32)
    fixed_bf = shape_of((fixed_rows, rows), BF)
    fixed_others = shape_of((n_space - 1, fixed_rows, rows), BF)
    part_bf = shape_of((width, fixed_rows), BF)
    by_node = shape_of((rows, fixed_rows), BF)
    in_vmem = pltpu.VMEM((rows, nodes), BF)
    dma = pltpu.SemaphoreType.DMA

    def fold(sent, got, after):
        size = width * fixed_rows
        return call(fold_kernel, [part_bf], [sent, got], size, 6 * size, after=after)[0]

    def on_device(diag_inverse, coupling, arrow, tip_inverse, noise, noise_fixed, section_lengths):
        got_noise = send_up(noise)
        d0, d1, own, other, n0, mask = call(
            start_kernel,
            [in_vmem, in_vmem, fixed_f32, fixed_others, node_bf, shape_of((8, 128), F32)],
            [diag_inverse, arrow, noise, section_lengths],
            8,
            {i: pltpu.HBM for i in range(4)},
            [
                pltpu.VMEM((fixed_rows, rows), BF),
                pltpu.SMEM(section_lengths.shape, jnp.int32),
                dma((n_space, tiles)),
                dma((n_space, tiles)),
                dma((3,)),
            ],
        )
        got_response = send_down(other)
        value, bar, k1, n1 = call(
            first_value_kernel,
            [node_f32, node_bf, in_vmem, node_bf],
            [d0, n0, coupling, noise, *got_noise],
            8,
            {2: pltpu.HBM, 3: pltpu.HBM},
            [dma((3,))],
        )
        got_bar = send_up(bar)
        value_rows, e0, k1 = call(
            load_kernel,
            [flat_f32, fixed_bf, in_vmem],
            [coupling, arrow, value, k1],
            8,
            {0: pltpu.HBM, 1: pltpu.HBM, 3: pl.ANY, ("out", 2): pl.ANY},
            [dma((7,))],
            aliases={3: 2},
        )
        target, part_own, part_other, response = call(
            target_kernel,
            [
                node_bf,
                shape_of((width, fixed_rows), F32),
                shape_of((n_space - 1, width, fixed_rows), BF),
                fixed_bf,
            ],
            [k1, bar, n1, e0, own, *got_bar, *got_response],
            8,
            scratch=[pltpu.VMEM((columns, fixed_rows), F32)],
        )
        got_target = send_up(target)
        got_parts = send_down(part_other)
        (value,) = call(last_own_kernel, [node_f32], [d1, target], 8)
        (sent,) = call(core_sum_kernel, [part_bf], [part_own, *got_parts], 0.2, after=value)
        step = 0
        got = []

        def advance(after=None):
            nonlocal sent, got, step
            if step == steps:
                return
            if step:
                (sent,) = call(fold_kernel, [part_bf], [sent, *got], 0.2, after=after)
            got = [swap_step(sent, step)]
            step += 1

        advance()
        solved, other = call(
            last_solve_kernel,
            [flat_f32, flat_others],
            [d1, value, *got_target],
            8,
            scratch=[pltpu.VMEM((rows, columns), F32)],
            after=sent,
        )
        got_solved = send_down(other)
        advance(solved)
        pushed, other = call(
            response_kernel, [fixed_f32, fixed_others], [k1, response], 5, after=sent
        )
        got_pushed = send_down(other)
        base, passed, other = call(
            pass_kernel,
            [flat_f32, flat_f32, flat_others],
            [k1, mask, solved, *got_solved],
            8,
            after=pushed,
        )
        got_passed = send_down(other)
        advance(base)
        last_base, last_resp, noise_rows = call(
            turn_last_kernel,
            [node_f32, by_node, shape_of((width, fixed_rows), F32)],
            [base, response, noise_fixed, tip_inverse],
            5,
            after=sent,
        )
        solved, other = call(
            first_solve_kernel,
            [flat_f32, flat_others],
            [d0, value_rows, passed, *got_passed],
            8,
            after=noise_rows,
        )
        got_solved = send_down(other)
        advance(solved)
        left, other = call(
            first_response_kernel,
            [fixed_bf, fixed_others],
            [d0, e0, tip_inverse, pushed, *got_pushed],
            5,
            after=sent,
        )
        got_first = send_down(other)
        (first_base,) = call(turn_first_kernel, [node_f32], [solved, *got_solved], 1, after=left)
        (first,) = call(own_response_kernel, [fixed_f32], [d0, left], 8, after=first_base)
        (first_resp,) = call(turn_response_kernel, [by_node], [first, *got_first], 1, after=first)
        while step < steps:
            advance()
        (mixed,) = call(mixed_kernel, [part_bf], [noise_rows, sent, *got], 0.2, after=first_resp)
        got_mixed = send_up(mixed)
        (fixed_out,) = call(
            fixed_kernel, [shape_of((fixed_rows, width), F32)], [tip_inverse, mixed], 8
        )
        (sample,) = call(
            lambda a, b, c, d, *refs: final_kernel((a, b), (c, d), *refs),
            [shape_of((2, rows, columns), BF)],
            [first_base, last_base, first_resp, last_resp, mixed, *got_mixed],
            8,
            {("out", 0): pl.ANY},
            [
                pltpu.VMEM((columns, fixed_rows), BF),
                pltpu.VMEM((2, rows, columns), BF),
                dma((2, tiles)),
            ],
            after=fixed_out,
            after_place=pltpu.HBM,
        )
        return (sample, fixed_out)

    return on_device


def solution(mesh):
    sizes = dict(mesh.shape)

    def program(diag_inverse, coupling, arrow, tip_inverse, noise, noise_fixed, section_lengths):
        device = build(
            sizes["tm"],
            sizes["space"],
            diag_inverse.shape[1] // sizes["space"],
            noise.shape[2],
            arrow.shape[1],
        )
        return jax.shard_map(
            device,
            mesh=mesh,
            in_specs=(
                P("tm", "space", None),
                P("tm", "space", None),
                P("tm", None, "space"),
                P(),
                P("tm", "space", None),
                P(None, "space"),
                P(),
            ),
            out_specs=(P("tm", "space", None), P(None, "space")),
            check_vma=False,
        )(diag_inverse, coupling, arrow, tip_inverse, noise, noise_fixed, section_lengths)

    return program
```

```python
import jax
import jax.numpy as jnp
from jax import lax
from jax.experimental import pallas as pl
from jax.experimental.pallas import tpu as pltpu
from jax.sharding import PartitionSpec as P

BF = jnp.bfloat16
F32 = jnp.float32
MIB = 1 << 20


def dot(left, right):
    return jnp.dot(left, right, preferred_element_type=F32)


def dot_last(left, right):
    return lax.dot_general(left, right, (((1,), (1,)), ((), ())), preferred_element_type=F32)


def rounded(value):
    return value.astype(BF).astype(F32)


def total_of(own_ref, got_refs):
    total = rounded(own_ref[...])
    for got in got_refs:
        total = total + got[...].astype(F32)
    return total


def shape_of(shape, dtype):
    return jax.ShapeDtypeStruct(shape, dtype)


def build(n_tm, n_space, rows, columns, fixed_rows):
    nodes = n_space * rows
    tile = 256 if rows % 256 == 0 else rows
    tiles = rows // tile
    quarter = rows // 4
    width = columns // n_space
    peers = range(1, n_space)

    def at_core():
        return lax.axis_index("space")

    def block(step, offset=0, size=rows):
        owner = lax.rem(at_core() - step + n_space, n_space)
        return pl.ds(pl.multiple_of(owner * rows + offset, tile), size)

    def part_rows(step):
        owner = lax.rem(at_core() - step + n_space, n_space)
        return pl.ds(pl.multiple_of(owner * width, width), width)

    def call(body, outs, args, cover, places=None, scratch=(), after=None, aliases=None, after_place=pl.ANY):
        places = dict(places or {})
        args = list(args)
        count = len(args)
        if after is not None:
            args.append(after)
            places[count] = after_place

        def run(*refs):
            body(*refs[:count], *refs[len(args) :])

        specs = [pl.BlockSpec(memory_space=places.get(i, pltpu.VMEM)) for i in range(len(args))]
        args = [
            pltpu.with_memory_space_constraint(a, pltpu.HBM)
            if places.get(i) is pltpu.HBM
            else a
            for i, a in enumerate(args)
        ]
        return pl.pallas_call(
            run,
            in_specs=specs,
            out_specs=[
                pl.BlockSpec(memory_space=places.get(("out", i), pltpu.VMEM))
                for i in range(len(outs))
            ],
            out_shape=outs,
            scratch_shapes=list(scratch),
            input_output_aliases=aliases or {},
            cost_estimate=pl.CostEstimate(
                flops=int(cover * 1e9), bytes_accessed=0, transcendentals=0
            ),
            compiler_params=pltpu.CompilerParams(vmem_limit_bytes=16 * MIB),
        )(*args)

    def lower_others(left, factor, other_ref):
        for step in peers:

            @pl.when(at_core() >= step)
            def _():
                other_ref[step - 1] = dot(left[...], factor[:, block(step)]).astype(BF)

            @pl.when(at_core() < step)
            def _():
                other_ref[step - 1] = jnp.zeros_like(other_ref[step - 1])

    def lower_block(left, factor, own_ref):
        for j in range(tiles):
            at = j * tile
            own_ref[:, at : at + tile] = dot(left[:, at:], factor[at:, block(0, at, tile)])

    def lower_rows(left, factor, own_ref, other_ref):
        lower_others(left, factor, other_ref)
        lower_block(left, factor, own_ref)

    def full_rows(left, factor, own_ref, other_ref):
        for step in peers:
            other_ref[step - 1] = dot(left[...], factor[:, block(step)]).astype(BF)
        own_ref[...] = dot(left[...], factor[:, block(0)])

    def lower_own(factor, right, out_ref, wait=None):
        for i in range(tiles):
            at = i * tile
            if wait:
                wait(i)
            out_ref[at : at + tile] = dot(
                factor[at : at + tile, block(0, 0, at + tile)], right[: at + tile]
            )

    def lower_rest(factor, got, value):
        for step in peers:

            @pl.when(at_core() >= step)
            def _():
                value[...] = value[...] + dot(factor[:, block(step)], got[step - 1][...])

    def start_kernel(
        diag, arrow, noise, lengths,
        d0, d1, own, other, n0, mask,
        e1, live_scratch, sem1, sem0, sems,
    ):
        arrow_copy = pltpu.make_async_copy(arrow.at[1], e1, sems.at[0])
        noise_copy = pltpu.make_async_copy(noise.at[0], n0, sems.at[1])
        live_copy = pltpu.make_async_copy(lengths, live_scratch, sems.at[2])

        def lower_copies(slot, target, sem):
            copies = {}
            for step in range(n_space):
                for i in range(tiles):
                    at = i * tile
                    size = rows if step else at + tile
                    part = (pl.ds(at, tile), block(step, 0, size))
                    copies[step, i] = pltpu.make_async_copy(
                        diag.at[(slot, *part)], target.at[part], sem.at[step, i]
                    )
            return copies

        def each(copies, i, act):
            act(copies[0, i])
            for step in peers:

                @pl.when(at_core() >= step)
                def _():
                    act(copies[step, i])

        copies1 = lower_copies(1, d1, sem1)
        copies0 = lower_copies(0, d0, sem0)
        live_copy.start()
        arrow_copy.start()
        for i in range(tiles):
            each(copies1, i, lambda copy: copy.start(priority=i % 2))
        live_copy.wait()
        arrow_copy.wait()
        live = live_scratch[lax.axis_index("tm")] > 1
        mask[...] = jnp.where(live, jnp.ones_like(mask[...]), jnp.zeros_like(mask[...]))
        e1[...] = jnp.where(live, e1[...], jnp.zeros_like(e1[...]))
        for i in range(tiles):
            each(copies1, i, lambda copy: copy.wait())
            each(copies0, i, lambda copy: copy.start(priority=i % 2))
        noise_copy.start()
        lower_rows(e1, d1, own, other)
        for i in range(tiles):
            each(copies0, i, lambda copy: copy.wait())
        noise_copy.wait()

    def k1_copies(coupling, k1, first, count, sems):
        copies = []
        size = quarter // 2
        for i in range(2 * count):
            part = pl.ds(first * quarter + i * size, size)
            copies.append(pltpu.make_async_copy(coupling.at[1, part], k1.at[part], sems.at[i]))
            copies[-1].start(priority=i % 2)
        return copies

    def first_value_kernel(d0, n0, coupling, noise, *refs):
        got, (out, bar, k1, n1, sems) = refs[: n_space - 1], refs[n_space - 1 :]
        copies = k1_copies(coupling, k1, 0, 1, sems)
        copies.append(pltpu.make_async_copy(noise.at[1], n1, sems.at[2]))
        copies[-1].start()
        lower_own(d0, n0, out)
        lower_rest(d0, [piece.at[0] for piece in got], out)
        bar[...] = out[...].astype(BF)
        for copy in copies:
            copy.wait()

    def load_kernel(coupling, arrow, value, _, value_rows, e0, k1, sems):
        copies = k1_copies(coupling, k1, 1, 3, sems)
        copies.append(pltpu.make_async_copy(arrow.at[0], e0, sems.at[6]))
        copies[-1].start()
        value_rows[...] = value[...].T
        for copy in copies:
            copy.wait()

    def target_kernel(k1, bar, n1, e0, own, *refs):
        got, refs = refs[: n_space - 1], refs[n_space - 1 :]
        got_own, refs = refs[: n_space - 1], refs[n_space - 1 :]
        target, part_own, part_other, response, whole = refs
        response[...] = total_of(own, got_own).astype(BF)
        for at in range(0, rows, tile):
            pulled = jnp.zeros((tile, columns), F32)
            for step, piece in enumerate([bar, *got]):
                pulled = pulled + dot(k1[at : at + tile, block(step)], piece[...])
            target[at : at + tile] = (n1[at : at + tile].astype(F32) - pulled).astype(BF)
        whole[...] = (dot(e0[...], bar[...]) + dot(response[...], target[...])).T
        part_own[...] = whole[part_rows(0)]
        for step in peers:
            part_other[step - 1] = whole[part_rows(step)].astype(BF)

    def last_own_kernel(d1, target, value):
        lower_own(d1, target, value)

    def core_sum_kernel(part, *refs):
        got, out = refs[:-1], refs[-1]
        total = part[...]
        for piece in got:
            total = total + piece[...].astype(F32)
        out[...] = total.astype(BF)

    def fold_kernel(sent, got, out):
        out[...] = (sent[...].astype(F32) + got[...].astype(F32)).astype(BF)

    def last_solve_kernel(d1, first, *refs):
        got, (own, other, value) = refs[: n_space - 1], refs[n_space - 1 :]
        value[...] = first[...]
        lower_rest(d1, got, value)
        lower_rows(value[...].astype(BF).T, d1, own, other)

    def response_kernel(k1, response, own, other):
        full_rows(response, k1, own, other)

    def pass_kernel(k1, mask, solved, *refs):
        got, (base, own, other) = refs[: n_space - 1], refs[n_space - 1 :]
        value = jnp.where(mask[:1, :1] > 0, total_of(solved, got), 0.0)
        base[...] = value
        full_rows(value.astype(BF), k1, own, other)

    def first_response_kernel(d0, e0, tip, pushed, *refs):
        got, (left, other) = refs[: n_space - 1], refs[n_space - 1 :]
        inner = (e0[...].astype(F32) - total_of(pushed, got)).astype(BF)
        left[...] = through_tip(tip[...], inner).astype(BF)
        lower_others(left, d0, other)

    def own_response_kernel(d0, left, own):
        lower_block(left, d0, own)

    def first_solve_kernel(d0, value_rows, passed, *refs):
        got, (own, other) = refs[: n_space - 1], refs[n_space - 1 :]
        left = (value_rows[...] - total_of(passed, got)).astype(BF)
        lower_rows(left, d0, own, other)

    def through_tip(tip, right):
        inner = dot(tip, right).astype(BF)
        return dot(tip.astype(F32).T.astype(BF), inner)

    def turn_last_kernel(base, response, noise_fixed, tip, last_base, last_resp, noise_rows):
        noise_rows[...] = noise_fixed[...].T
        last_base[...] = base[...].T
        last_resp[...] = through_tip(tip[...], response[...]).T.astype(BF)

    def turn_response_kernel(first, *refs):
        got, out = refs[:-1], refs[-1]
        out[...] = total_of(first, got).T.astype(BF)

    def turn_first_kernel(solved, *refs):
        got, out = refs[:-1], refs[-1]
        out[...] = total_of(solved, got).T

    def mixed_kernel(noise_rows, *refs):
        terms, out = refs[:-1], refs[-1]
        total = terms[0][...].astype(F32)
        for piece in terms[1:]:
            total = total + piece[...].astype(F32)
        out[...] = (noise_rows[...] - total).astype(BF)

    def final_kernel(bases, responses, mixed, *refs):
        got, (out, whole, result, sems) = refs[: n_space - 1], refs[n_space - 1 :]
        for step, piece in enumerate([mixed, *got]):
            whole[part_rows(step)] = piece[...]
        copies = []
        for slot in range(2):
            for i in range(tiles):
                at = i * tile
                part = (slot, pl.ds(at, tile))
                update = dot_last(responses[slot][at : at + tile], whole[...])
                result[part] = (bases[slot][at : at + tile] - update).astype(BF)
                copies.append(
                    pltpu.make_async_copy(result.at[part], out.at[part], sems.at[slot, i])
                )
                copies[-1].start()
        for copy in copies:
            copy.wait()

    def fixed_kernel(tip, mixed, out):
        forward = dot_last(mixed[...], tip[...])
        out[...] = dot(forward.astype(BF), tip[...]).T

    def swap(value, step):
        pairs = [(i, (i - step) % n_space) for i in range(n_space)]
        return lax.ppermute(value, "space", pairs)

    def send_up(value):
        return [swap(value, -step) for step in peers]

    def send_down(values):
        return [swap(values[step - 1], step) for step in peers]

    steps = n_tm.bit_length() - 1
    assert n_tm == 1 << steps

    def swap_step(value, step):
        pairs = []
        for i in range(n_tm):
            for core in range(n_space):
                bit = 1 << step
                if step < steps - 1:
                    bit = 1 << (step + core * (steps - 1) // n_space) % (steps - 1)
                pairs.append((i * n_space + core, (i ^ bit) * n_space + core))
        return lax.ppermute(value, ("tm", "space"), pairs)

    node_f32, node_bf = shape_of((rows, columns), F32), shape_of((rows, columns), BF)
    flat_f32 = shape_of((columns, rows), F32)
    flat_others = shape_of((n_space - 1, columns, rows), BF)
    fixed_f32 = shape_of((fixed_rows, rows), F32)
    fixed_bf = shape_of((fixed_rows, rows), BF)
    fixed_others = shape_of((n_space - 1, fixed_rows, rows), BF)
    part_bf = shape_of((width, fixed_rows), BF)
    by_node = shape_of((rows, fixed_rows), BF)
    in_vmem = pltpu.VMEM((rows, nodes), BF)
    dma = pltpu.SemaphoreType.DMA

    def fold(sent, got, after):
        size = width * fixed_rows
        return call(fold_kernel, [part_bf], [sent, got], size, 6 * size, after=after)[0]

    def on_device(diag_inverse, coupling, arrow, tip_inverse, noise, noise_fixed, section_lengths):
        got_noise = send_up(noise)
        d0, d1, own, other, n0, mask = call(
            start_kernel,
            [in_vmem, in_vmem, fixed_f32, fixed_others, node_bf, shape_of((8, 128), F32)],
            [diag_inverse, arrow, noise, section_lengths],
            8,
            {i: pltpu.HBM for i in range(4)},
            [
                pltpu.VMEM((fixed_rows, rows), BF),
                pltpu.SMEM(section_lengths.shape, jnp.int32),
                dma((n_space, tiles)),
                dma((n_space, tiles)),
                dma((3,)),
            ],
        )
        got_response = send_down(other)
        value, bar, k1, n1 = call(
            first_value_kernel,
            [node_f32, node_bf, in_vmem, node_bf],
            [d0, n0, coupling, noise, *got_noise],
            8,
            {2: pltpu.HBM, 3: pltpu.HBM},
            [dma((3,))],
        )
        got_bar = send_up(bar)
        value_rows, e0, k1 = call(
            load_kernel,
            [flat_f32, fixed_bf, in_vmem],
            [coupling, arrow, value, k1],
            8,
            {0: pltpu.HBM, 1: pltpu.HBM, 3: pl.ANY, ("out", 2): pl.ANY},
            [dma((7,))],
            aliases={3: 2},
        )
        target, part_own, part_other, response = call(
            target_kernel,
            [
                node_bf,
                shape_of((width, fixed_rows), F32),
                shape_of((n_space - 1, width, fixed_rows), BF),
                fixed_bf,
            ],
            [k1, bar, n1, e0, own, *got_bar, *got_response],
            8,
            scratch=[pltpu.VMEM((columns, fixed_rows), F32)],
        )
        got_target = send_up(target)
        got_parts = send_down(part_other)
        (value,) = call(last_own_kernel, [node_f32], [d1, target], 8)
        (sent,) = call(core_sum_kernel, [part_bf], [part_own, *got_parts], 0.2, after=value)
        step = 0
        got = []

        def advance(after=None):
            nonlocal sent, got, step
            if step == steps:
                return
            if step:
                (sent,) = call(fold_kernel, [part_bf], [sent, *got], 0.2, after=after)
            got = [swap_step(sent, step)]
            step += 1

        advance()
        solved, other = call(
            last_solve_kernel,
            [flat_f32, flat_others],
            [d1, value, *got_target],
            8,
            scratch=[pltpu.VMEM((rows, columns), F32)],
            after=sent,
        )
        got_solved = send_down(other)
        advance(solved)
        pushed, other = call(
            response_kernel, [fixed_f32, fixed_others], [k1, response], 5, after=sent
        )
        got_pushed = send_down(other)
        base, passed, other = call(
            pass_kernel,
            [flat_f32, flat_f32, flat_others],
            [k1, mask, solved, *got_solved],
            8,
            after=pushed,
        )
        got_passed = send_down(other)
        advance(base)
        last_base, last_resp, noise_rows = call(
            turn_last_kernel,
            [node_f32, by_node, shape_of((width, fixed_rows), F32)],
            [base, response, noise_fixed, tip_inverse],
            5,
            after=sent,
        )
        solved, other = call(
            first_solve_kernel,
            [flat_f32, flat_others],
            [d0, value_rows, passed, *got_passed],
            8,
            after=noise_rows,
        )
        got_solved = send_down(other)
        advance(solved)
        left, other = call(
            first_response_kernel,
            [fixed_bf, fixed_others],
            [d0, e0, tip_inverse, pushed, *got_pushed],
            5,
            after=sent,
        )
        got_first = send_down(other)
        (first_base,) = call(turn_first_kernel, [node_f32], [solved, *got_solved], 1, after=left)
        (first,) = call(own_response_kernel, [fixed_f32], [d0, left], 8, after=first_base)
        (first_resp,) = call(turn_response_kernel, [by_node], [first, *got_first], 1, after=first)
        while step < steps:
            advance()
        (mixed,) = call(mixed_kernel, [part_bf], [noise_rows, sent, *got], 0.2, after=first_resp)
        got_mixed = send_up(mixed)
        (fixed_out,) = call(
            fixed_kernel, [shape_of((fixed_rows, width), F32)], [tip_inverse, mixed], 8
        )
        (sample,) = call(
            lambda a, b, c, d, *refs: final_kernel((a, b), (c, d), *refs),
            [shape_of((2, rows, columns), BF)],
            [first_base, last_base, first_resp, last_resp, mixed, *got_mixed],
            8,
            {("out", 0): pl.ANY},
            [
                pltpu.VMEM((columns, fixed_rows), BF),
                pltpu.VMEM((2, rows, columns), BF),
                dma((2, tiles)),
            ],
            after=fixed_out,
            after_place=pltpu.HBM,
        )
        return (sample, fixed_out)

    return on_device


def solution(mesh):
    sizes = dict(mesh.shape)

    def program(diag_inverse, coupling, arrow, tip_inverse, noise, noise_fixed, section_lengths):
        device = build(
            sizes["tm"],
            sizes["space"],
            diag_inverse.shape[1] // sizes["space"],
            noise.shape[2],
            arrow.shape[1],
        )
        return jax.shard_map(
            device,
            mesh=mesh,
            in_specs=(
                P("tm", "space", None),
                P("tm", "space", None),
                P("tm", None, "space"),
                P(),
                P("tm", "space", None),
                P(None, "space"),
                P(),
            ),
            out_specs=(P("tm", "space", None), P(None, "space")),
            check_vma=False,
        )(diag_inverse, coupling, arrow, tip_inverse, noise, noise_fixed, section_lengths)

    return program
```

```python
import jax
import jax.numpy as jnp
from jax import lax
from jax.experimental import pallas as pl
from jax.experimental.pallas import tpu as pltpu
from jax.sharding import PartitionSpec as P

BF = jnp.bfloat16
F32 = jnp.float32
MIB = 1 << 20


def dot(left, right):
    return jnp.dot(left, right, preferred_element_type=F32)


def dot_last(left, right):
    return lax.dot_general(left, right, (((1,), (1,)), ((), ())), preferred_element_type=F32)


def rounded(value):
    return value.astype(BF).astype(F32)


def total_of(own_ref, got_refs):
    total = rounded(own_ref[...])
    for got in got_refs:
        total = total + got[...].astype(F32)
    return total


def shape_of(shape, dtype):
    return jax.ShapeDtypeStruct(shape, dtype)


def build(n_tm, n_space, rows, columns, fixed_rows):
    nodes = n_space * rows
    tile = 256 if rows % 256 == 0 else rows
    tiles = rows // tile
    quarter = rows // 4
    width = columns // n_space
    peers = range(1, n_space)

    def at_core():
        return lax.axis_index("space")

    def block(step, offset=0, size=rows):
        owner = lax.rem(at_core() - step + n_space, n_space)
        return pl.ds(pl.multiple_of(owner * rows + offset, tile), size)

    def part_rows(step):
        owner = lax.rem(at_core() - step + n_space, n_space)
        return pl.ds(pl.multiple_of(owner * width, width), width)

    def call(body, outs, args, cover, places=None, scratch=(), after=None, aliases=None, after_place=pl.ANY):
        places = dict(places or {})
        args = list(args)
        count = len(args)
        if after is not None:
            args.append(after)
            places[count] = after_place

        def run(*refs):
            body(*refs[:count], *refs[len(args) :])

        specs = [pl.BlockSpec(memory_space=places.get(i, pltpu.VMEM)) for i in range(len(args))]
        args = [
            pltpu.with_memory_space_constraint(a, pltpu.HBM)
            if places.get(i) is pltpu.HBM
            else a
            for i, a in enumerate(args)
        ]
        return pl.pallas_call(
            run,
            in_specs=specs,
            out_specs=[
                pl.BlockSpec(memory_space=places.get(("out", i), pltpu.VMEM))
                for i in range(len(outs))
            ],
            out_shape=outs,
            scratch_shapes=list(scratch),
            input_output_aliases=aliases or {},
            cost_estimate=pl.CostEstimate(
                flops=int(cover * 1e9), bytes_accessed=0, transcendentals=0
            ),
            compiler_params=pltpu.CompilerParams(vmem_limit_bytes=16 * MIB),
        )(*args)

    def lower_others(left, factor, other_ref):
        for step in peers:

            @pl.when(at_core() >= step)
            def _():
                other_ref[step - 1] = dot(left[...], factor[:, block(step)]).astype(BF)

            @pl.when(at_core() < step)
            def _():
                other_ref[step - 1] = jnp.zeros_like(other_ref[step - 1])

    def lower_block(left, factor, own_ref):
        for j in range(tiles):
            at = j * tile
            own_ref[:, at : at + tile] = dot(left[:, at:], factor[at:, block(0, at, tile)])

    def lower_rows(left, factor, own_ref, other_ref):
        lower_others(left, factor, other_ref)
        lower_block(left, factor, own_ref)

    def full_rows(left, factor, own_ref, other_ref):
        for step in peers:
            other_ref[step - 1] = dot(left[...], factor[:, block(step)]).astype(BF)
        own_ref[...] = dot(left[...], factor[:, block(0)])

    def lower_own(factor, right, out_ref, wait=None):
        for i in range(tiles):
            at = i * tile
            if wait:
                wait(i)
            out_ref[at : at + tile] = dot(
                factor[at : at + tile, block(0, 0, at + tile)], right[: at + tile]
            )

    def lower_rest(factor, got, value):
        for step in peers:

            @pl.when(at_core() >= step)
            def _():
                value[...] = value[...] + dot(factor[:, block(step)], got[step - 1][...])

    def start_kernel(
        diag, arrow, noise, lengths,
        d0, d1, own, other, n0, mask,
        e1, live_scratch, sem1, sem0, sems,
    ):
        arrow_copy = pltpu.make_async_copy(arrow.at[1], e1, sems.at[0])
        noise_copy = pltpu.make_async_copy(noise.at[0], n0, sems.at[1])
        live_copy = pltpu.make_async_copy(lengths, live_scratch, sems.at[2])

        def lower_copies(slot, target, sem):
            copies = {}
            for step in range(n_space):
                for i in range(tiles):
                    at = i * tile
                    size = rows if step else at + tile
                    part = (pl.ds(at, tile), block(step, 0, size))
                    copies[step, i] = pltpu.make_async_copy(
                        diag.at[(slot, *part)], target.at[part], sem.at[step, i]
                    )
            return copies

        def each(copies, i, act):
            act(copies[0, i])
            for step in peers:

                @pl.when(at_core() >= step)
                def _():
                    act(copies[step, i])

        copies1 = lower_copies(1, d1, sem1)
        copies0 = lower_copies(0, d0, sem0)
        live_copy.start()
        arrow_copy.start()
        for i in range(tiles):
            each(copies1, i, lambda copy: copy.start(priority=i % 2))
        live_copy.wait()
        arrow_copy.wait()
        live = live_scratch[lax.axis_index("tm")] > 1
        mask[...] = jnp.where(live, jnp.ones_like(mask[...]), jnp.zeros_like(mask[...]))
        e1[...] = jnp.where(live, e1[...], jnp.zeros_like(e1[...]))
        for i in range(tiles):
            each(copies1, i, lambda copy: copy.wait())
            each(copies0, i, lambda copy: copy.start(priority=i % 2))
        noise_copy.start()
        lower_rows(e1, d1, own, other)
        for i in range(tiles):
            each(copies0, i, lambda copy: copy.wait())
        noise_copy.wait()

    def k1_copies(coupling, k1, first, count, sems):
        copies = []
        size = quarter // 2
        for i in range(2 * count):
            part = pl.ds(first * quarter + i * size, size)
            copies.append(pltpu.make_async_copy(coupling.at[1, part], k1.at[part], sems.at[i]))
            copies[-1].start(priority=i % 2)
        return copies

    def first_value_kernel(d0, n0, coupling, noise, *refs):
        got, (out, bar, k1, n1, sems) = refs[: n_space - 1], refs[n_space - 1 :]
        copies = k1_copies(coupling, k1, 0, 1, sems)
        copies.append(pltpu.make_async_copy(noise.at[1], n1, sems.at[2]))
        copies[-1].start()
        lower_own(d0, n0, out)
        lower_rest(d0, [piece.at[0] for piece in got], out)
        bar[...] = out[...].astype(BF)
        for copy in copies:
            copy.wait()

    def load_kernel(coupling, arrow, value, _, value_rows, e0, k1, sems):
        copies = k1_copies(coupling, k1, 1, 3, sems)
        copies.append(pltpu.make_async_copy(arrow.at[0], e0, sems.at[6]))
        copies[-1].start()
        value_rows[...] = value[...].T
        for copy in copies:
            copy.wait()

    def target_kernel(k1, bar, n1, e0, own, *refs):
        got, refs = refs[: n_space - 1], refs[n_space - 1 :]
        got_own, refs = refs[: n_space - 1], refs[n_space - 1 :]
        target, part_own, part_other, response, whole = refs
        response[...] = total_of(own, got_own).astype(BF)
        for at in range(0, rows, tile):
            pulled = jnp.zeros((tile, columns), F32)
            for step, piece in enumerate([bar, *got]):
                pulled = pulled + dot(k1[at : at + tile, block(step)], piece[...])
            target[at : at + tile] = (n1[at : at + tile].astype(F32) - pulled).astype(BF)
        whole[...] = (dot(e0[...], bar[...]) + dot(response[...], target[...])).T
        part_own[...] = whole[part_rows(0)]
        for step in peers:
            part_other[step - 1] = whole[part_rows(step)].astype(BF)

    def last_own_kernel(d1, target, value):
        lower_own(d1, target, value)

    def core_sum_kernel(part, *refs):
        got, out = refs[:-1], refs[-1]
        total = part[...]
        for piece in got:
            total = total + piece[...].astype(F32)
        out[...] = total.astype(BF)

    def fold_kernel(sent, got, out):
        out[...] = (sent[...].astype(F32) + got[...].astype(F32)).astype(BF)

    def last_solve_kernel(d1, first, *refs):
        got, (own, other, value) = refs[: n_space - 1], refs[n_space - 1 :]
        value[...] = first[...]
        lower_rest(d1, got, value)
        lower_rows(value[...].astype(BF).T, d1, own, other)

    def response_kernel(k1, response, own, other):
        full_rows(response, k1, own, other)

    def pass_kernel(k1, mask, solved, *refs):
        got, (base, own, other) = refs[: n_space - 1], refs[n_space - 1 :]
        value = jnp.where(mask[:1, :1] > 0, total_of(solved, got), 0.0)
        base[...] = value
        full_rows(value.astype(BF), k1, own, other)

    def first_response_kernel(d0, e0, tip, pushed, *refs):
        got, (left, other) = refs[: n_space - 1], refs[n_space - 1 :]
        inner = (e0[...].astype(F32) - total_of(pushed, got)).astype(BF)
        left[...] = through_tip(tip[...], inner).astype(BF)
        lower_others(left, d0, other)

    def own_response_kernel(d0, left, own):
        lower_block(left, d0, own)

    def first_solve_kernel(d0, value_rows, passed, *refs):
        got, (own, other) = refs[: n_space - 1], refs[n_space - 1 :]
        left = (value_rows[...] - total_of(passed, got)).astype(BF)
        lower_rows(left, d0, own, other)

    def through_tip(tip, right):
        inner = dot(tip, right).astype(BF)
        return dot(tip.astype(F32).T.astype(BF), inner)

    def turn_tip_kernel(response, noise_fixed, tip, last_resp, noise_rows):
        noise_rows[...] = noise_fixed[...].T
        last_resp[...] = through_tip(tip[...], response[...]).T.astype(BF)

    def turn_last_kernel(base, out):
        out[...] = base[...].T

    def turn_response_kernel(first, *refs):
        got, out = refs[:-1], refs[-1]
        out[...] = total_of(first, got).T.astype(BF)

    def turn_first_kernel(solved, *refs):
        got, out = refs[:-1], refs[-1]
        out[...] = total_of(solved, got).T

    def mixed_kernel(noise_rows, *refs):
        terms, out = refs[:-1], refs[-1]
        total = terms[0][...].astype(F32)
        for piece in terms[1:]:
            total = total + piece[...].astype(F32)
        out[...] = (noise_rows[...] - total).astype(BF)

    def final_kernel(bases, responses, mixed, *refs):
        got, (out, whole, result, sems) = refs[: n_space - 1], refs[n_space - 1 :]
        for step, piece in enumerate([mixed, *got]):
            whole[part_rows(step)] = piece[...]
        copies = []
        for slot in range(2):
            for i in range(tiles):
                at = i * tile
                part = (slot, pl.ds(at, tile))
                update = dot_last(responses[slot][at : at + tile], whole[...])
                result[part] = (bases[slot][at : at + tile] - update).astype(BF)
                copies.append(
                    pltpu.make_async_copy(result.at[part], out.at[part], sems.at[slot, i])
                )
                copies[-1].start()
        for copy in copies:
            copy.wait()

    def fixed_kernel(tip, mixed, out):
        forward = dot_last(mixed[...], tip[...])
        out[...] = dot(forward.astype(BF), tip[...]).T

    def swap(value, step):
        pairs = [(i, (i - step) % n_space) for i in range(n_space)]
        return lax.ppermute(value, "space", pairs)

    def send_up(value):
        return [swap(value, -step) for step in peers]

    def send_down(values):
        return [swap(values[step - 1], step) for step in peers]

    steps = n_tm.bit_length() - 1
    assert n_tm == 1 << steps

    def swap_step(value, step):
        pairs = []
        for i in range(n_tm):
            for core in range(n_space):
                bit = 1 << step
                if step < steps - 1:
                    bit = 1 << (step + core * (steps - 1) // n_space) % (steps - 1)
                pairs.append((i * n_space + core, (i ^ bit) * n_space + core))
        return lax.ppermute(value, ("tm", "space"), pairs)

    node_f32, node_bf = shape_of((rows, columns), F32), shape_of((rows, columns), BF)
    flat_f32 = shape_of((columns, rows), F32)
    flat_others = shape_of((n_space - 1, columns, rows), BF)
    fixed_f32 = shape_of((fixed_rows, rows), F32)
    fixed_bf = shape_of((fixed_rows, rows), BF)
    fixed_others = shape_of((n_space - 1, fixed_rows, rows), BF)
    part_bf = shape_of((width, fixed_rows), BF)
    by_node = shape_of((rows, fixed_rows), BF)
    in_vmem = pltpu.VMEM((rows, nodes), BF)
    dma = pltpu.SemaphoreType.DMA

    def fold(sent, got, after):
        size = width * fixed_rows
        return call(fold_kernel, [part_bf], [sent, got], size, 6 * size, after=after)[0]

    def on_device(diag_inverse, coupling, arrow, tip_inverse, noise, noise_fixed, section_lengths):
        got_noise = send_up(noise)
        d0, d1, own, other, n0, mask = call(
            start_kernel,
            [in_vmem, in_vmem, fixed_f32, fixed_others, node_bf, shape_of((8, 128), F32)],
            [diag_inverse, arrow, noise, section_lengths],
            8,
            {i: pltpu.HBM for i in range(4)},
            [
                pltpu.VMEM((fixed_rows, rows), BF),
                pltpu.SMEM(section_lengths.shape, jnp.int32),
                dma((n_space, tiles)),
                dma((n_space, tiles)),
                dma((3,)),
            ],
        )
        got_response = send_down(other)
        value, bar, k1, n1 = call(
            first_value_kernel,
            [node_f32, node_bf, in_vmem, node_bf],
            [d0, n0, coupling, noise, *got_noise],
            8,
            {2: pltpu.HBM, 3: pltpu.HBM},
            [dma((3,))],
        )
        got_bar = send_up(bar)
        value_rows, e0, k1 = call(
            load_kernel,
            [flat_f32, fixed_bf, in_vmem],
            [coupling, arrow, value, k1],
            8,
            {0: pltpu.HBM, 1: pltpu.HBM, 3: pl.ANY, ("out", 2): pl.ANY},
            [dma((7,))],
            aliases={3: 2},
        )
        target, part_own, part_other, response = call(
            target_kernel,
            [
                node_bf,
                shape_of((width, fixed_rows), F32),
                shape_of((n_space - 1, width, fixed_rows), BF),
                fixed_bf,
            ],
            [k1, bar, n1, e0, own, *got_bar, *got_response],
            8,
            scratch=[pltpu.VMEM((columns, fixed_rows), F32)],
        )
        got_target = send_up(target)
        got_parts = send_down(part_other)
        (value,) = call(last_own_kernel, [node_f32], [d1, target], 8)
        (sent,) = call(core_sum_kernel, [part_bf], [part_own, *got_parts], 0.2, after=value)
        step = 0
        got = []

        def advance(after=None):
            nonlocal sent, got, step
            if step == steps:
                return
            if step:
                (sent,) = call(fold_kernel, [part_bf], [sent, *got], 0.2, after=after)
            got = [swap_step(sent, step)]
            step += 1

        advance()
        solved, other = call(
            last_solve_kernel,
            [flat_f32, flat_others],
            [d1, value, *got_target],
            8,
            scratch=[pltpu.VMEM((rows, columns), F32)],
            after=sent,
        )
        got_solved = send_down(other)
        advance(solved)
        last_resp, noise_rows = call(
            turn_tip_kernel,
            [by_node, shape_of((width, fixed_rows), F32)],
            [response, noise_fixed, tip_inverse],
            5,
            after=sent,
        )
        base, passed, other = call(
            pass_kernel,
            [flat_f32, flat_f32, flat_others],
            [k1, mask, solved, *got_solved],
            8,
            after=noise_rows,
        )
        got_passed = send_down(other)
        advance(base)
        pushed, other = call(
            response_kernel, [fixed_f32, fixed_others], [k1, response], 5, after=sent
        )
        got_pushed = send_down(other)
        solved, other = call(
            first_solve_kernel,
            [flat_f32, flat_others],
            [d0, value_rows, passed, *got_passed],
            8,
            after=pushed,
        )
        got_solved = send_down(other)
        advance(solved)
        left, other = call(
            first_response_kernel,
            [fixed_bf, fixed_others],
            [d0, e0, tip_inverse, pushed, *got_pushed],
            5,
            after=sent,
        )
        got_first = send_down(other)
        (first_base,) = call(turn_first_kernel, [node_f32], [solved, *got_solved], 1, after=left)
        (first,) = call(own_response_kernel, [fixed_f32], [d0, left], 8, after=first_base)
        (last_base,) = call(turn_last_kernel, [node_f32], [base], 1, after=first)
        (first_resp,) = call(turn_response_kernel, [by_node], [first, *got_first], 1, after=last_base)
        while step < steps:
            advance()
        (mixed,) = call(mixed_kernel, [part_bf], [noise_rows, sent, *got], 0.2, after=first_resp)
        got_mixed = send_up(mixed)
        (fixed_out,) = call(
            fixed_kernel, [shape_of((fixed_rows, width), F32)], [tip_inverse, mixed], 8
        )
        (sample,) = call(
            lambda a, b, c, d, *refs: final_kernel((a, b), (c, d), *refs),
            [shape_of((2, rows, columns), BF)],
            [first_base, last_base, first_resp, last_resp, mixed, *got_mixed],
            8,
            {("out", 0): pl.ANY},
            [
                pltpu.VMEM((columns, fixed_rows), BF),
                pltpu.VMEM((2, rows, columns), BF),
                dma((2, tiles)),
            ],
            after=fixed_out,
            after_place=pltpu.HBM,
        )
        return (sample, fixed_out)

    return on_device


def solution(mesh):
    sizes = dict(mesh.shape)

    def program(diag_inverse, coupling, arrow, tip_inverse, noise, noise_fixed, section_lengths):
        device = build(
            sizes["tm"],
            sizes["space"],
            diag_inverse.shape[1] // sizes["space"],
            noise.shape[2],
            arrow.shape[1],
        )
        return jax.shard_map(
            device,
            mesh=mesh,
            in_specs=(
                P("tm", "space", None),
                P("tm", "space", None),
                P("tm", None, "space"),
                P(),
                P("tm", "space", None),
                P(None, "space"),
                P(),
            ),
            out_specs=(P("tm", "space", None), P(None, "space")),
            check_vma=False,
        )(diag_inverse, coupling, arrow, tip_inverse, noise, noise_fixed, section_lengths)

    return program
```

```python
import jax
import jax.numpy as jnp
from jax import lax
from jax.experimental import pallas as pl
from jax.experimental.pallas import tpu as pltpu
from jax.sharding import PartitionSpec as P

BF = jnp.bfloat16
F32 = jnp.float32
MIB = 1 << 20


def dot(left, right):
    return jnp.dot(left, right, preferred_element_type=F32)


def dot_last(left, right):
    return lax.dot_general(left, right, (((1,), (1,)), ((), ())), preferred_element_type=F32)


def rounded(value):
    return value.astype(BF).astype(F32)


def total_of(own_ref, got_refs):
    total = rounded(own_ref[...])
    for got in got_refs:
        total = total + got[...].astype(F32)
    return total


def shape_of(shape, dtype):
    return jax.ShapeDtypeStruct(shape, dtype)


def build(n_tm, n_space, rows, columns, fixed_rows):
    nodes = n_space * rows
    tile = 256 if rows % 256 == 0 else rows
    tiles = rows // tile
    quarter = rows // 4
    width = columns // n_space
    peers = range(1, n_space)

    def at_core():
        return lax.axis_index("space")

    def block(step, offset=0, size=rows):
        owner = lax.rem(at_core() - step + n_space, n_space)
        return pl.ds(pl.multiple_of(owner * rows + offset, tile), size)

    def part_rows(step):
        owner = lax.rem(at_core() - step + n_space, n_space)
        return pl.ds(pl.multiple_of(owner * width, width), width)

    def call(body, outs, args, cover, places=None, scratch=(), after=None, aliases=None, after_place=pl.ANY):
        places = dict(places or {})
        args = list(args)
        count = len(args)
        if after is not None:
            args.append(after)
            places[count] = after_place

        def run(*refs):
            body(*refs[:count], *refs[len(args) :])

        specs = [pl.BlockSpec(memory_space=places.get(i, pltpu.VMEM)) for i in range(len(args))]
        args = [
            pltpu.with_memory_space_constraint(a, pltpu.HBM)
            if places.get(i) is pltpu.HBM
            else a
            for i, a in enumerate(args)
        ]
        return pl.pallas_call(
            run,
            in_specs=specs,
            out_specs=[
                pl.BlockSpec(memory_space=places.get(("out", i), pltpu.VMEM))
                for i in range(len(outs))
            ],
            out_shape=outs,
            scratch_shapes=list(scratch),
            input_output_aliases=aliases or {},
            cost_estimate=pl.CostEstimate(
                flops=int(cover * 1e9), bytes_accessed=0, transcendentals=0
            ),
            compiler_params=pltpu.CompilerParams(vmem_limit_bytes=16 * MIB),
        )(*args)

    def lower_others(left, factor, other_ref):
        for step in peers:

            @pl.when(at_core() >= step)
            def _():
                other_ref[step - 1] = dot(left[...], factor[:, block(step)]).astype(BF)

            @pl.when(at_core() < step)
            def _():
                other_ref[step - 1] = jnp.zeros_like(other_ref[step - 1])

    def lower_block(left, factor, own_ref):
        for j in range(tiles):
            at = j * tile
            own_ref[:, at : at + tile] = dot(left[:, at:], factor[at:, block(0, at, tile)])

    def lower_rows(left, factor, own_ref, other_ref):
        lower_others(left, factor, other_ref)
        lower_block(left, factor, own_ref)

    def full_rows(left, factor, own_ref, other_ref):
        for step in peers:
            other_ref[step - 1] = dot(left[...], factor[:, block(step)]).astype(BF)
        own_ref[...] = dot(left[...], factor[:, block(0)])

    def lower_own(factor, right, out_ref, wait=None):
        for i in range(tiles):
            at = i * tile
            if wait:
                wait(i)
            out_ref[at : at + tile] = dot(
                factor[at : at + tile, block(0, 0, at + tile)], right[: at + tile]
            )

    def lower_rest(factor, got, value):
        for step in peers:

            @pl.when(at_core() >= step)
            def _():
                value[...] = value[...] + dot(factor[:, block(step)], got[step - 1][...])

    def start_kernel(
        diag, arrow, noise, lengths,
        d0, d1, own, other, n0, mask,
        e1, live_scratch, sem1, sem0, sems,
    ):
        arrow_copy = pltpu.make_async_copy(arrow.at[1], e1, sems.at[0])
        noise_copy = pltpu.make_async_copy(noise.at[0], n0, sems.at[1])
        live_copy = pltpu.make_async_copy(lengths, live_scratch, sems.at[2])

        def lower_copies(slot, target, sem):
            copies = {}
            for step in range(n_space):
                for i in range(tiles):
                    at = i * tile
                    size = rows if step else at + tile
                    part = (pl.ds(at, tile), block(step, 0, size))
                    copies[step, i] = pltpu.make_async_copy(
                        diag.at[(slot, *part)], target.at[part], sem.at[step, i]
                    )
            return copies

        def each(copies, i, act):
            act(copies[0, i])
            for step in peers:

                @pl.when(at_core() >= step)
                def _():
                    act(copies[step, i])

        copies1 = lower_copies(1, d1, sem1)
        copies0 = lower_copies(0, d0, sem0)
        live_copy.start()
        arrow_copy.start()
        for i in range(tiles):
            each(copies1, i, lambda copy: copy.start(priority=i % 2))
        live_copy.wait()
        arrow_copy.wait()
        live = live_scratch[lax.axis_index("tm")] > 1
        mask[...] = jnp.where(live, jnp.ones_like(mask[...]), jnp.zeros_like(mask[...]))
        e1[...] = jnp.where(live, e1[...], jnp.zeros_like(e1[...]))
        for i in range(tiles):
            each(copies1, i, lambda copy: copy.wait())
            for early in range(2 * i, min(2 * i + 2, tiles)):
                each(copies0, early, lambda copy: copy.start(priority=1))
        noise_copy.start()
        lower_rows(e1, d1, own, other)
        for i in range(tiles):
            each(copies0, i, lambda copy: copy.wait())
        noise_copy.wait()

    def k1_copies(coupling, k1, first, count, sems):
        copies = []
        size = quarter // 2
        for i in range(2 * count):
            part = pl.ds(first * quarter + i * size, size)
            copies.append(pltpu.make_async_copy(coupling.at[1, part], k1.at[part], sems.at[i]))
            copies[-1].start(priority=i % 2)
        return copies

    def first_value_kernel(d0, n0, coupling, noise, *refs):
        got, (out, bar, k1, n1, sems) = refs[: n_space - 1], refs[n_space - 1 :]
        copies = k1_copies(coupling, k1, 0, 1, sems)
        copies.append(pltpu.make_async_copy(noise.at[1], n1, sems.at[2]))
        copies[-1].start()
        lower_own(d0, n0, out)
        lower_rest(d0, [piece.at[0] for piece in got], out)
        bar[...] = out[...].astype(BF)
        for copy in copies:
            copy.wait()

    def load_kernel(coupling, arrow, value, _, value_rows, e0, k1, sems):
        copies = k1_copies(coupling, k1, 1, 3, sems)
        copies.append(pltpu.make_async_copy(arrow.at[0], e0, sems.at[6]))
        copies[-1].start()
        value_rows[...] = value[...].T
        for copy in copies:
            copy.wait()

    def target_kernel(k1, bar, n1, e0, own, *refs):
        got, refs = refs[: n_space - 1], refs[n_space - 1 :]
        got_own, refs = refs[: n_space - 1], refs[n_space - 1 :]
        target, part_own, part_other, response, whole = refs
        response[...] = total_of(own, got_own).astype(BF)
        for at in range(0, rows, tile):
            pulled = jnp.zeros((tile, columns), F32)
            for step, piece in enumerate([bar, *got]):
                pulled = pulled + dot(k1[at : at + tile, block(step)], piece[...])
            target[at : at + tile] = (n1[at : at + tile].astype(F32) - pulled).astype(BF)
        whole[...] = (dot(e0[...], bar[...]) + dot(response[...], target[...])).T
        part_own[...] = whole[part_rows(0)]
        for step in peers:
            part_other[step - 1] = whole[part_rows(step)].astype(BF)

    def last_own_kernel(d1, target, value):
        lower_own(d1, target, value)

    def core_sum_kernel(part, *refs):
        got, out = refs[:-1], refs[-1]
        total = part[...]
        for piece in got:
            total = total + piece[...].astype(F32)
        out[...] = total.astype(BF)

    def fold_kernel(sent, got, out):
        out[...] = (sent[...].astype(F32) + got[...].astype(F32)).astype(BF)

    def last_solve_kernel(d1, first, *refs):
        got, (own, other, value) = refs[: n_space - 1], refs[n_space - 1 :]
        value[...] = first[...]
        lower_rest(d1, got, value)
        lower_rows(value[...].astype(BF).T, d1, own, other)

    def response_kernel(k1, response, own, other):
        full_rows(response, k1, own, other)

    def pass_kernel(k1, mask, solved, *refs):
        got, (base, own, other) = refs[: n_space - 1], refs[n_space - 1 :]
        value = jnp.where(mask[:1, :1] > 0, total_of(solved, got), 0.0)
        base[...] = value
        full_rows(value.astype(BF), k1, own, other)

    def first_response_kernel(d0, e0, tip, pushed, *refs):
        got, (left, other) = refs[: n_space - 1], refs[n_space - 1 :]
        inner = (e0[...].astype(F32) - total_of(pushed, got)).astype(BF)
        left[...] = through_tip(tip[...], inner).astype(BF)
        lower_others(left, d0, other)

    def own_response_kernel(d0, left, own):
        lower_block(left, d0, own)

    def first_solve_kernel(d0, value_rows, passed, *refs):
        got, (own, other) = refs[: n_space - 1], refs[n_space - 1 :]
        left = (value_rows[...] - total_of(passed, got)).astype(BF)
        lower_rows(left, d0, own, other)

    def through_tip(tip, right):
        inner = dot(tip, right).astype(BF)
        return dot(tip.astype(F32).T.astype(BF), inner)

    def turn_last_kernel(base, response, noise_fixed, tip, last_base, last_resp, noise_rows):
        noise_rows[...] = noise_fixed[...].T
        last_base[...] = base[...].T
        last_resp[...] = through_tip(tip[...], response[...]).T.astype(BF)

    def turn_response_kernel(first, *refs):
        got, out = refs[:-1], refs[-1]
        out[...] = total_of(first, got).T.astype(BF)

    def turn_first_kernel(solved, *refs):
        got, out = refs[:-1], refs[-1]
        out[...] = total_of(solved, got).T

    def mixed_kernel(noise_rows, *refs):
        terms, out = refs[:-1], refs[-1]
        total = terms[0][...].astype(F32)
        for piece in terms[1:]:
            total = total + piece[...].astype(F32)
        out[...] = (noise_rows[...] - total).astype(BF)

    def final_kernel(bases, responses, mixed, *refs):
        got, (out, whole, result, sems) = refs[: n_space - 1], refs[n_space - 1 :]
        for step, piece in enumerate([mixed, *got]):
            whole[part_rows(step)] = piece[...]
        copies = []
        for slot in range(2):
            for i in range(tiles):
                at = i * tile
                part = (slot, pl.ds(at, tile))
                update = dot_last(responses[slot][at : at + tile], whole[...])
                result[part] = (bases[slot][at : at + tile] - update).astype(BF)
                copies.append(
                    pltpu.make_async_copy(result.at[part], out.at[part], sems.at[slot, i])
                )
                copies[-1].start()
        for copy in copies:
            copy.wait()

    def fixed_kernel(tip, mixed, out):
        forward = dot_last(mixed[...], tip[...])
        out[...] = dot(forward.astype(BF), tip[...]).T

    def swap(value, step):
        pairs = [(i, (i - step) % n_space) for i in range(n_space)]
        return lax.ppermute(value, "space", pairs)

    def send_up(value):
        return [swap(value, -step) for step in peers]

    def send_down(values):
        return [swap(values[step - 1], step) for step in peers]

    steps = n_tm.bit_length() - 1
    assert n_tm == 1 << steps

    def swap_step(value, step):
        pairs = []
        for i in range(n_tm):
            for core in range(n_space):
                bit = 1 << (step + core * steps // n_space) % steps
                pairs.append((i * n_space + core, (i ^ bit) * n_space + core))
        return lax.ppermute(value, ("tm", "space"), pairs)

    node_f32, node_bf = shape_of((rows, columns), F32), shape_of((rows, columns), BF)
    flat_f32 = shape_of((columns, rows), F32)
    flat_others = shape_of((n_space - 1, columns, rows), BF)
    fixed_f32 = shape_of((fixed_rows, rows), F32)
    fixed_bf = shape_of((fixed_rows, rows), BF)
    fixed_others = shape_of((n_space - 1, fixed_rows, rows), BF)
    part_bf = shape_of((width, fixed_rows), BF)
    by_node = shape_of((rows, fixed_rows), BF)
    in_vmem = pltpu.VMEM((rows, nodes), BF)
    dma = pltpu.SemaphoreType.DMA

    def fold(sent, got, after):
        size = width * fixed_rows
        return call(fold_kernel, [part_bf], [sent, got], size, 6 * size, after=after)[0]

    def on_device(diag_inverse, coupling, arrow, tip_inverse, noise, noise_fixed, section_lengths):
        got_noise = send_up(noise)
        d0, d1, own, other, n0, mask = call(
            start_kernel,
            [in_vmem, in_vmem, fixed_f32, fixed_others, node_bf, shape_of((8, 128), F32)],
            [diag_inverse, arrow, noise, section_lengths],
            8,
            {i: pltpu.HBM for i in range(4)},
            [
                pltpu.VMEM((fixed_rows, rows), BF),
                pltpu.SMEM(section_lengths.shape, jnp.int32),
                dma((n_space, tiles)),
                dma((n_space, tiles)),
                dma((3,)),
            ],
        )
        got_response = send_down(other)
        value, bar, k1, n1 = call(
            first_value_kernel,
            [node_f32, node_bf, in_vmem, node_bf],
            [d0, n0, coupling, noise, *got_noise],
            8,
            {2: pltpu.HBM, 3: pltpu.HBM},
            [dma((3,))],
        )
        got_bar = send_up(bar)
        value_rows, e0, k1 = call(
            load_kernel,
            [flat_f32, fixed_bf, in_vmem],
            [coupling, arrow, value, k1],
            8,
            {0: pltpu.HBM, 1: pltpu.HBM, 3: pl.ANY, ("out", 2): pl.ANY},
            [dma((7,))],
            aliases={3: 2},
        )
        target, part_own, part_other, response = call(
            target_kernel,
            [
                node_bf,
                shape_of((width, fixed_rows), F32),
                shape_of((n_space - 1, width, fixed_rows), BF),
                fixed_bf,
            ],
            [k1, bar, n1, e0, own, *got_bar, *got_response],
            8,
            scratch=[pltpu.VMEM((columns, fixed_rows), F32)],
        )
        got_target = send_up(target)
        got_parts = send_down(part_other)
        (value,) = call(last_own_kernel, [node_f32], [d1, target], 8)
        (sent,) = call(core_sum_kernel, [part_bf], [part_own, *got_parts], 0.2, after=value)
        step = 0
        got = []

        def advance(after=None):
            nonlocal sent, got, step
            if step == steps:
                return
            if step:
                (sent,) = call(fold_kernel, [part_bf], [sent, *got], 0.2, after=after)
            got = [swap_step(sent, step)]
            step += 1

        advance()
        solved, other = call(
            last_solve_kernel,
            [flat_f32, flat_others],
            [d1, value, *got_target],
            8,
            scratch=[pltpu.VMEM((rows, columns), F32)],
            after=sent,
        )
        got_solved = send_down(other)
        advance(solved)
        pushed, other = call(
            response_kernel, [fixed_f32, fixed_others], [k1, response], 5, after=sent
        )
        got_pushed = send_down(other)
        base, passed, other = call(
            pass_kernel,
            [flat_f32, flat_f32, flat_others],
            [k1, mask, solved, *got_solved],
            8,
            after=pushed,
        )
        got_passed = send_down(other)
        advance(base)
        last_base, last_resp, noise_rows = call(
            turn_last_kernel,
            [node_f32, by_node, shape_of((width, fixed_rows), F32)],
            [base, response, noise_fixed, tip_inverse],
            5,
            after=sent,
        )
        solved, other = call(
            first_solve_kernel,
            [flat_f32, flat_others],
            [d0, value_rows, passed, *got_passed],
            8,
            after=noise_rows,
        )
        got_solved = send_down(other)
        advance(solved)
        left, other = call(
            first_response_kernel,
            [fixed_bf, fixed_others],
            [d0, e0, tip_inverse, pushed, *got_pushed],
            5,
            after=sent,
        )
        got_first = send_down(other)
        (first_base,) = call(turn_first_kernel, [node_f32], [solved, *got_solved], 1, after=left)
        (first,) = call(own_response_kernel, [fixed_f32], [d0, left], 8, after=first_base)
        (first_resp,) = call(turn_response_kernel, [by_node], [first, *got_first], 1, after=first)
        while step < steps:
            advance()
        (mixed,) = call(mixed_kernel, [part_bf], [noise_rows, sent, *got], 0.2, after=first_resp)
        got_mixed = send_up(mixed)
        (fixed_out,) = call(
            fixed_kernel, [shape_of((fixed_rows, width), F32)], [tip_inverse, mixed], 8
        )
        (sample,) = call(
            lambda a, b, c, d, *refs: final_kernel((a, b), (c, d), *refs),
            [shape_of((2, rows, columns), BF)],
            [first_base, last_base, first_resp, last_resp, mixed, *got_mixed],
            8,
            {("out", 0): pl.ANY},
            [
                pltpu.VMEM((columns, fixed_rows), BF),
                pltpu.VMEM((2, rows, columns), BF),
                dma((2, tiles)),
            ],
            after=fixed_out,
            after_place=pltpu.HBM,
        )
        return (sample, fixed_out)

    return on_device


def solution(mesh):
    sizes = dict(mesh.shape)

    def program(diag_inverse, coupling, arrow, tip_inverse, noise, noise_fixed, section_lengths):
        device = build(
            sizes["tm"],
            sizes["space"],
            diag_inverse.shape[1] // sizes["space"],
            noise.shape[2],
            arrow.shape[1],
        )
        return jax.shard_map(
            device,
            mesh=mesh,
            in_specs=(
                P("tm", "space", None),
                P("tm", "space", None),
                P("tm", None, "space"),
                P(),
                P("tm", "space", None),
                P(None, "space"),
                P(),
            ),
            out_specs=(P("tm", "space", None), P(None, "space")),
            check_vma=False,
        )(diag_inverse, coupling, arrow, tip_inverse, noise, noise_fixed, section_lengths)

    return program
```

```python
import jax
import jax.numpy as jnp
from jax import lax
from jax.experimental import pallas as pl
from jax.experimental.pallas import tpu as pltpu
from jax.sharding import PartitionSpec as P

BF = jnp.bfloat16
F32 = jnp.float32
MIB = 1 << 20


def dot(left, right):
    return jnp.dot(left, right, preferred_element_type=F32)


def dot_last(left, right):
    return lax.dot_general(left, right, (((1,), (1,)), ((), ())), preferred_element_type=F32)


def rounded(value):
    return value.astype(BF).astype(F32)


def total_of(own_ref, got_refs):
    total = rounded(own_ref[...])
    for got in got_refs:
        total = total + got[...].astype(F32)
    return total


def shape_of(shape, dtype):
    return jax.ShapeDtypeStruct(shape, dtype)


def build(n_tm, n_space, rows, columns, fixed_rows):
    nodes = n_space * rows
    tile = 256 if rows % 256 == 0 else rows
    tiles = rows // tile
    quarter = rows // 4
    width = columns // n_space
    peers = range(1, n_space)

    def at_core():
        return lax.axis_index("space")

    def block(step, offset=0, size=rows):
        owner = lax.rem(at_core() - step + n_space, n_space)
        return pl.ds(pl.multiple_of(owner * rows + offset, tile), size)

    def part_rows(step):
        owner = lax.rem(at_core() - step + n_space, n_space)
        return pl.ds(pl.multiple_of(owner * width, width), width)

    def call(body, outs, args, cover, places=None, scratch=(), after=None, aliases=None, after_place=pl.ANY):
        places = dict(places or {})
        args = list(args)
        count = len(args)
        if after is not None:
            args.append(after)
            places[count] = after_place

        def run(*refs):
            body(*refs[:count], *refs[len(args) :])

        specs = [pl.BlockSpec(memory_space=places.get(i, pltpu.VMEM)) for i in range(len(args))]
        args = [
            pltpu.with_memory_space_constraint(a, pltpu.HBM)
            if places.get(i) is pltpu.HBM
            else a
            for i, a in enumerate(args)
        ]
        return pl.pallas_call(
            run,
            in_specs=specs,
            out_specs=[
                pl.BlockSpec(memory_space=places.get(("out", i), pltpu.VMEM))
                for i in range(len(outs))
            ],
            out_shape=outs,
            scratch_shapes=list(scratch),
            input_output_aliases=aliases or {},
            cost_estimate=pl.CostEstimate(
                flops=int(cover * 1e9), bytes_accessed=0, transcendentals=0
            ),
            compiler_params=pltpu.CompilerParams(vmem_limit_bytes=16 * MIB),
        )(*args)

    def lower_others(left, factor, other_ref):
        for step in peers:

            @pl.when(at_core() >= step)
            def _():
                other_ref[step - 1] = dot(left[...], factor[:, block(step)]).astype(BF)

            @pl.when(at_core() < step)
            def _():
                other_ref[step - 1] = jnp.zeros_like(other_ref[step - 1])

    def lower_block(left, factor, own_ref):
        for j in range(tiles):
            at = j * tile
            own_ref[:, at : at + tile] = dot(left[:, at:], factor[at:, block(0, at, tile)])

    def lower_rows(left, factor, own_ref, other_ref):
        lower_others(left, factor, other_ref)
        lower_block(left, factor, own_ref)

    def full_rows(left, factor, own_ref, other_ref):
        for step in peers:
            other_ref[step - 1] = dot(left[...], factor[:, block(step)]).astype(BF)
        own_ref[...] = dot(left[...], factor[:, block(0)])

    def lower_own(factor, right, out_ref, wait=None):
        for i in range(tiles):
            at = i * tile
            if wait:
                wait(i)
            out_ref[at : at + tile] = dot(
                factor[at : at + tile, block(0, 0, at + tile)], right[: at + tile]
            )

    def lower_rest(factor, got, value):
        for step in peers:

            @pl.when(at_core() >= step)
            def _():
                value[...] = value[...] + dot(factor[:, block(step)], got[step - 1][...])

    def start_kernel(
        diag, arrow, noise, lengths,
        d0, d1, own, other, n0, mask,
        e1, live_scratch, sem1, sem0, sems,
    ):
        arrow_copy = pltpu.make_async_copy(arrow.at[1], e1, sems.at[0])
        noise_copy = pltpu.make_async_copy(noise.at[0], n0, sems.at[1])
        live_copy = pltpu.make_async_copy(lengths, live_scratch, sems.at[2])

        def lower_copies(slot, target, sem):
            copies = {}
            for step in range(n_space):
                for i in range(tiles):
                    at = i * tile
                    size = rows if step else at + tile
                    part = (pl.ds(at, tile), block(step, 0, size))
                    copies[step, i] = pltpu.make_async_copy(
                        diag.at[(slot, *part)], target.at[part], sem.at[step, i]
                    )
            return copies

        def each(copies, i, act):
            act(copies[0, i])
            for step in peers:

                @pl.when(at_core() >= step)
                def _():
                    act(copies[step, i])

        copies1 = lower_copies(1, d1, sem1)
        copies0 = lower_copies(0, d0, sem0)
        live_copy.start()
        arrow_copy.start()
        for i in range(tiles):
            each(copies1, i, lambda copy: copy.start(priority=i % 2))
        live_copy.wait()
        arrow_copy.wait()
        live = live_scratch[lax.axis_index("tm")] > 1
        mask[...] = jnp.where(live, jnp.ones_like(mask[...]), jnp.zeros_like(mask[...]))
        e1[...] = jnp.where(live, e1[...], jnp.zeros_like(e1[...]))
        for i in range(tiles):
            each(copies1, i, lambda copy: copy.wait())
            for early in range(tiles if i == 0 else 0):
                each(copies0, early, lambda copy: copy.start(priority=1))
        noise_copy.start()
        lower_rows(e1, d1, own, other)
        for i in range(tiles):
            each(copies0, i, lambda copy: copy.wait())
        noise_copy.wait()

    def k1_copies(coupling, k1, first, count, sems):
        copies = []
        size = quarter // 2
        for i in range(2 * count):
            part = pl.ds(first * quarter + i * size, size)
            copies.append(pltpu.make_async_copy(coupling.at[1, part], k1.at[part], sems.at[i]))
            copies[-1].start(priority=i % 2)
        return copies

    def first_value_kernel(d0, n0, coupling, noise, *refs):
        got, (out, bar, k1, n1, sems) = refs[: n_space - 1], refs[n_space - 1 :]
        copies = k1_copies(coupling, k1, 0, 1, sems)
        copies.append(pltpu.make_async_copy(noise.at[1], n1, sems.at[2]))
        copies[-1].start()
        lower_own(d0, n0, out)
        lower_rest(d0, [piece.at[0] for piece in got], out)
        bar[...] = out[...].astype(BF)
        for copy in copies:
            copy.wait()

    def load_kernel(coupling, arrow, value, _, value_rows, e0, k1, sems):
        copies = k1_copies(coupling, k1, 1, 3, sems)
        copies.append(pltpu.make_async_copy(arrow.at[0], e0, sems.at[6]))
        copies[-1].start()
        value_rows[...] = value[...].T
        for copy in copies:
            copy.wait()

    def target_kernel(k1, bar, n1, e0, own, *refs):
        got, refs = refs[: n_space - 1], refs[n_space - 1 :]
        got_own, refs = refs[: n_space - 1], refs[n_space - 1 :]
        target, part_own, part_other, response, whole = refs
        response[...] = total_of(own, got_own).astype(BF)
        for at in range(0, rows, tile):
            pulled = jnp.zeros((tile, columns), F32)
            for step, piece in enumerate([bar, *got]):
                pulled = pulled + dot(k1[at : at + tile, block(step)], piece[...])
            target[at : at + tile] = (n1[at : at + tile].astype(F32) - pulled).astype(BF)
        whole[...] = (dot(e0[...], bar[...]) + dot(response[...], target[...])).T
        part_own[...] = whole[part_rows(0)]
        for step in peers:
            part_other[step - 1] = whole[part_rows(step)].astype(BF)

    def last_own_kernel(d1, target, value):
        lower_own(d1, target, value)

    def core_sum_kernel(part, *refs):
        got, out = refs[:-1], refs[-1]
        total = part[...]
        for piece in got:
            total = total + piece[...].astype(F32)
        out[...] = total.astype(BF)

    def fold_kernel(sent, got, out):
        out[...] = (sent[...].astype(F32) + got[...].astype(F32)).astype(BF)

    def last_solve_kernel(d1, first, *refs):
        got, (own, other, value) = refs[: n_space - 1], refs[n_space - 1 :]
        value[...] = first[...]
        lower_rest(d1, got, value)
        lower_rows(value[...].astype(BF).T, d1, own, other)

    def response_kernel(k1, response, own, other):
        full_rows(response, k1, own, other)

    def pass_kernel(k1, mask, solved, *refs):
        got, (base, own, other) = refs[: n_space - 1], refs[n_space - 1 :]
        value = jnp.where(mask[:1, :1] > 0, total_of(solved, got), 0.0)
        base[...] = value
        full_rows(value.astype(BF), k1, own, other)

    def first_response_kernel(d0, e0, tip, pushed, *refs):
        got, (left, other) = refs[: n_space - 1], refs[n_space - 1 :]
        inner = (e0[...].astype(F32) - total_of(pushed, got)).astype(BF)
        left[...] = through_tip(tip[...], inner).astype(BF)
        lower_others(left, d0, other)

    def own_response_kernel(d0, left, own):
        lower_block(left, d0, own)

    def first_solve_kernel(d0, value_rows, passed, *refs):
        got, (own, other) = refs[: n_space - 1], refs[n_space - 1 :]
        left = (value_rows[...] - total_of(passed, got)).astype(BF)
        lower_rows(left, d0, own, other)

    def through_tip(tip, right):
        inner = dot(tip, right).astype(BF)
        return dot(tip.astype(F32).T.astype(BF), inner)

    def turn_last_kernel(base, response, noise_fixed, tip, last_base, last_resp, noise_rows):
        noise_rows[...] = noise_fixed[...].T
        last_base[...] = base[...].T
        last_resp[...] = through_tip(tip[...], response[...]).T.astype(BF)

    def turn_response_kernel(first, *refs):
        got, out = refs[:-1], refs[-1]
        out[...] = total_of(first, got).T.astype(BF)

    def turn_first_kernel(solved, *refs):
        got, out = refs[:-1], refs[-1]
        out[...] = total_of(solved, got).T

    def mixed_kernel(noise_rows, *refs):
        terms, out = refs[:-1], refs[-1]
        total = terms[0][...].astype(F32)
        for piece in terms[1:]:
            total = total + piece[...].astype(F32)
        out[...] = (noise_rows[...] - total).astype(BF)

    def final_kernel(bases, responses, mixed, *refs):
        got, (out, whole, result, sems) = refs[: n_space - 1], refs[n_space - 1 :]
        for step, piece in enumerate([mixed, *got]):
            whole[part_rows(step)] = piece[...]
        copies = []
        for slot in range(2):
            for i in range(tiles):
                at = i * tile
                part = (slot, pl.ds(at, tile))
                update = dot_last(responses[slot][at : at + tile], whole[...])
                result[part] = (bases[slot][at : at + tile] - update).astype(BF)
                copies.append(
                    pltpu.make_async_copy(result.at[part], out.at[part], sems.at[slot, i])
                )
                copies[-1].start()
        for copy in copies:
            copy.wait()

    def fixed_kernel(tip, mixed, out):
        forward = dot_last(mixed[...], tip[...])
        out[...] = dot(forward.astype(BF), tip[...]).T

    def swap(value, step):
        pairs = [(i, (i - step) % n_space) for i in range(n_space)]
        return lax.ppermute(value, "space", pairs)

    def send_up(value):
        return [swap(value, -step) for step in peers]

    def send_down(values):
        return [swap(values[step - 1], step) for step in peers]

    steps = n_tm.bit_length() - 1
    assert n_tm == 1 << steps

    def swap_step(value, step):
        pairs = []
        for i in range(n_tm):
            for core in range(n_space):
                bit = 1 << (step + core * steps // n_space) % steps
                pairs.append((i * n_space + core, (i ^ bit) * n_space + core))
        return lax.ppermute(value, ("tm", "space"), pairs)

    node_f32, node_bf = shape_of((rows, columns), F32), shape_of((rows, columns), BF)
    flat_f32 = shape_of((columns, rows), F32)
    flat_others = shape_of((n_space - 1, columns, rows), BF)
    fixed_f32 = shape_of((fixed_rows, rows), F32)
    fixed_bf = shape_of((fixed_rows, rows), BF)
    fixed_others = shape_of((n_space - 1, fixed_rows, rows), BF)
    part_bf = shape_of((width, fixed_rows), BF)
    by_node = shape_of((rows, fixed_rows), BF)
    in_vmem = pltpu.VMEM((rows, nodes), BF)
    dma = pltpu.SemaphoreType.DMA

    def fold(sent, got, after):
        size = width * fixed_rows
        return call(fold_kernel, [part_bf], [sent, got], size, 6 * size, after=after)[0]

    def on_device(diag_inverse, coupling, arrow, tip_inverse, noise, noise_fixed, section_lengths):
        got_noise = send_up(noise)
        d0, d1, own, other, n0, mask = call(
            start_kernel,
            [in_vmem, in_vmem, fixed_f32, fixed_others, node_bf, shape_of((8, 128), F32)],
            [diag_inverse, arrow, noise, section_lengths],
            8,
            {i: pltpu.HBM for i in range(4)},
            [
                pltpu.VMEM((fixed_rows, rows), BF),
                pltpu.SMEM(section_lengths.shape, jnp.int32),
                dma((n_space, tiles)),
                dma((n_space, tiles)),
                dma((3,)),
            ],
        )
        got_response = send_down(other)
        value, bar, k1, n1 = call(
            first_value_kernel,
            [node_f32, node_bf, in_vmem, node_bf],
            [d0, n0, coupling, noise, *got_noise],
            8,
            {2: pltpu.HBM, 3: pltpu.HBM},
            [dma((3,))],
        )
        got_bar = send_up(bar)
        value_rows, e0, k1 = call(
            load_kernel,
            [flat_f32, fixed_bf, in_vmem],
            [coupling, arrow, value, k1],
            8,
            {0: pltpu.HBM, 1: pltpu.HBM, 3: pl.ANY, ("out", 2): pl.ANY},
            [dma((7,))],
            aliases={3: 2},
        )
        target, part_own, part_other, response = call(
            target_kernel,
            [
                node_bf,
                shape_of((width, fixed_rows), F32),
                shape_of((n_space - 1, width, fixed_rows), BF),
                fixed_bf,
            ],
            [k1, bar, n1, e0, own, *got_bar, *got_response],
            8,
            scratch=[pltpu.VMEM((columns, fixed_rows), F32)],
        )
        got_target = send_up(target)
        got_parts = send_down(part_other)
        (value,) = call(last_own_kernel, [node_f32], [d1, target], 8)
        (sent,) = call(core_sum_kernel, [part_bf], [part_own, *got_parts], 0.2, after=value)
        step = 0
        got = []

        def advance(after=None):
            nonlocal sent, got, step
            if step == steps:
                return
            if step:
                (sent,) = call(fold_kernel, [part_bf], [sent, *got], 0.2, after=after)
            got = [swap_step(sent, step)]
            step += 1

        advance()
        solved, other = call(
            last_solve_kernel,
            [flat_f32, flat_others],
            [d1, value, *got_target],
            8,
            scratch=[pltpu.VMEM((rows, columns), F32)],
            after=sent,
        )
        got_solved = send_down(other)
        advance(solved)
        pushed, other = call(
            response_kernel, [fixed_f32, fixed_others], [k1, response], 5, after=sent
        )
        got_pushed = send_down(other)
        base, passed, other = call(
            pass_kernel,
            [flat_f32, flat_f32, flat_others],
            [k1, mask, solved, *got_solved],
            8,
            after=pushed,
        )
        got_passed = send_down(other)
        advance(base)
        last_base, last_resp, noise_rows = call(
            turn_last_kernel,
            [node_f32, by_node, shape_of((width, fixed_rows), F32)],
            [base, response, noise_fixed, tip_inverse],
            5,
            after=sent,
        )
        solved, other = call(
            first_solve_kernel,
            [flat_f32, flat_others],
            [d0, value_rows, passed, *got_passed],
            8,
            after=noise_rows,
        )
        got_solved = send_down(other)
        advance(solved)
        left, other = call(
            first_response_kernel,
            [fixed_bf, fixed_others],
            [d0, e0, tip_inverse, pushed, *got_pushed],
            5,
            after=sent,
        )
        got_first = send_down(other)
        (first_base,) = call(turn_first_kernel, [node_f32], [solved, *got_solved], 1, after=left)
        (first,) = call(own_response_kernel, [fixed_f32], [d0, left], 8, after=first_base)
        (first_resp,) = call(turn_response_kernel, [by_node], [first, *got_first], 1, after=first)
        while step < steps:
            advance()
        (mixed,) = call(mixed_kernel, [part_bf], [noise_rows, sent, *got], 0.2, after=first_resp)
        got_mixed = send_up(mixed)
        (fixed_out,) = call(
            fixed_kernel, [shape_of((fixed_rows, width), F32)], [tip_inverse, mixed], 8
        )
        (sample,) = call(
            lambda a, b, c, d, *refs: final_kernel((a, b), (c, d), *refs),
            [shape_of((2, rows, columns), BF)],
            [first_base, last_base, first_resp, last_resp, mixed, *got_mixed],
            8,
            {("out", 0): pl.ANY},
            [
                pltpu.VMEM((columns, fixed_rows), BF),
                pltpu.VMEM((2, rows, columns), BF),
                dma((2, tiles)),
            ],
            after=fixed_out,
            after_place=pltpu.HBM,
        )
        return (sample, fixed_out)

    return on_device


def solution(mesh):
    sizes = dict(mesh.shape)

    def program(diag_inverse, coupling, arrow, tip_inverse, noise, noise_fixed, section_lengths):
        device = build(
            sizes["tm"],
            sizes["space"],
            diag_inverse.shape[1] // sizes["space"],
            noise.shape[2],
            arrow.shape[1],
        )
        return jax.shard_map(
            device,
            mesh=mesh,
            in_specs=(
                P("tm", "space", None),
                P("tm", "space", None),
                P("tm", None, "space"),
                P(),
                P("tm", "space", None),
                P(None, "space"),
                P(),
            ),
            out_specs=(P("tm", "space", None), P(None, "space")),
            check_vma=False,
        )(diag_inverse, coupling, arrow, tip_inverse, noise, noise_fixed, section_lengths)

    return program
```
